32 devices in a mesh: dp: 2 (over core), fsdp: 16 (over z, y, x).
Axes of the slice: x: 2, y: 2, z: 4, core: 2. Of those that a mesh axis runs over, the one named last changes fastest.
Arguments:
- tokens: bfloat16 [16384, 768], P(('dp', 'fsdp')), may hold values from -6 to 6
- lengths: int32 [32], P(('dp', 'fsdp')), may hold values from 128 to 512, as said below
- rel_index: int32 [1024], replicated, may hold values from 0 to 511, as said below
- w_query: bfloat16 [768, 768], P(('dp', 'fsdp')), may hold values from -0.21875 to 0.21875
- b_query: bfloat16 [768], P(('dp', 'fsdp')), may hold values from -3 to 3
- w_key: bfloat16 [768, 768], P(('dp', 'fsdp')), may hold values from -0.21875 to 0.21875
- b_key: bfloat16 [768], P(('dp', 'fsdp')), may hold values from -3 to 3
- w_value: bfloat16 [768, 768], P(('dp', 'fsdp')), may hold values from -0.21875 to 0.21875
- b_value: bfloat16 [768], P(('dp', 'fsdp')), may hold values from -3 to 3
- w_out: bfloat16 [768, 768], P(('dp', 'fsdp')), may hold values from -1.75 to 1.75
- b_out: bfloat16 [768], P(('dp', 'fsdp')), may hold values from -3 to 3
- rel_table: bfloat16 [512, 768], P(None, ('dp', 'fsdp')), may hold values from -6 to 6
- gain_one: bfloat16 [768], P(('dp', 'fsdp')), may hold values from 0.5 to 1.5
- shift_one: bfloat16 [768], P(('dp', 'fsdp')), may hold values from -2 to 2
- w_up: bfloat16 [768, 3072], P(('dp', 'fsdp')), may hold values from -0.21875 to 0.21875
- b_up: bfloat16 [3072], P(('dp', 'fsdp')), may hold values from -3 to 3
- w_down: bfloat16 [3072, 768], P(('dp', 'fsdp')), may hold values from -0.109375 to 0.109375
- b_down: bfloat16 [768], P(('dp', 'fsdp')), may hold values from -3 to 3
- gain_two: bfloat16 [768], P(('dp', 'fsdp')), may hold values from 0.5 to 1.5
- shift_two: bfloat16 [768], P(('dp', 'fsdp')), may hold values from -2 to 2
- cotangent: bfloat16 [16384, 768], P(('dp', 'fsdp')), may hold values from -6 to 6
Outputs:
- output: bfloat16 [16384, 768], P(('dp', 'fsdp'))
- grad_tokens: float32 [16384, 768], P(('dp', 'fsdp'))
- grad_w_query: float32 [768, 768], P(('dp', 'fsdp'))
- grad_b_query: float32 [768], P(('dp', 'fsdp'))
- grad_w_key: float32 [768, 768], P(('dp', 'fsdp'))
- grad_b_key: float32 [768], P(('dp', 'fsdp'))
- grad_w_value: float32 [768, 768], P(('dp', 'fsdp'))
- grad_b_value: float32 [768], P(('dp', 'fsdp'))
- grad_w_out: float32 [768, 768], P(('dp', 'fsdp'))
- grad_b_out: float32 [768], P(('dp', 'fsdp'))
- grad_rel_table: float32 [512, 768], P(None, ('dp', 'fsdp'))
- grad_gain_one: float32 [768], P(('dp', 'fsdp'))
- grad_shift_one: float32 [768], P(('dp', 'fsdp'))
- grad_w_up: float32 [768, 3072], P(('dp', 'fsdp'))
- grad_b_up: float32 [3072], P(('dp', 'fsdp'))
- grad_w_down: float32 [3072, 768], P(('dp', 'fsdp'))
- grad_b_down: float32 [768], P(('dp', 'fsdp'))
- grad_gain_two: float32 [768], P(('dp', 'fsdp'))
- grad_shift_two: float32 [768], P(('dp', 'fsdp'))
The draws below stay inside these ranges and needn't reach their ends.
Inputs may be any that keep to these rules, and one draw needn't show every extreme that they name: `lengths`: some sequence is full in every draw. `rel_index`: entry t is the bucket of the offset t - 512; entry 0 is never read.
All inputs are finite; a program needn't handle non-finite values.
Results may differ from the reference program's by a relative error of at most 0.034.
Values may be sent and summed in bfloat16 or wider, within the bound.
A program may use at most 128 MiB of HBM per device.

```python
import jax
import jax.numpy as jnp
import numpy as np
from jax import lax

D = 768
HEADS = 12
HEAD = 64
FF = 3072
SPAN = 256
SEQ = 512
SEQS = 32
TOKENS = 16384


def draw_lengths(key, part):
    first, second = jax.random.split(key)
    values = jax.random.randint(first, (SEQS,), SEQ // 4, SEQ + 1, dtype=jnp.int32)
    full = jax.random.randint(second, (), 0, SEQS, dtype=jnp.int32)
    return jnp.where(jnp.arange(SEQS, dtype=jnp.int32) == full, SEQ, values)


def draw_rel_index(key, part):
    offsets = np.arange(2 * SEQ) - SEQ
    middle = SPAN // 2
    distance = np.abs(offsets)
    safe = np.maximum(distance, 1)
    far = np.ceil(np.log(safe / middle) / np.log((2 * SPAN - 1) / middle) * (middle - 1)) + middle
    bucket = np.where(distance <= middle, offsets, np.sign(offsets) * far)
    base = np.clip(bucket + SPAN, 0, 2 * SPAN - 1).astype(np.int32)
    jitter = jax.random.randint(key, (2 * SEQ,), -2, 3, dtype=jnp.int32)
    jitter = jnp.where(jnp.asarray(distance > middle), jitter, 0)
    index = jnp.clip(jnp.asarray(base) + jitter, 0, 2 * SPAN - 1)
    places = jnp.arange(2 * SEQ, dtype=jnp.int32)
    index = jnp.where(places == 1, 0, index)
    index = jnp.where(places == 2 * SEQ - 1, 2 * SPAN - 1, index)
    return index.astype(jnp.int32)


def strengthened(values, key, source, target, blocks, factor):
    owner, partner = [(jnp.arange(values.shape[position]) // (values.shape[position] // blocks)).reshape([-1 if axis == position else 1 for axis in range(values.ndim)]) for position in (source, target)]
    chosen = jax.random.permutation(key, blocks)[partner]
    strong = (owner == chosen) | (owner == (partner + blocks // 2) % blocks)
    return jnp.where(strong, factor * values, values)


def block_levels(stream_key, shape, shards, smallest, largest):
    level, own = 1.0, jax.random.fold_in(stream_key, 6)
    for position, shards_of in shards:
        draws = jnp.exp(jax.random.uniform(jax.random.fold_in(own, position), (shards_of,), jnp.float32, smallest / len(shards), largest / len(shards)))
        level = level * jnp.repeat(draws, shape[position] // shards_of).reshape([-1 if axis == position else 1 for axis in range(len(shape))])
    return level


def noise(own_key, dims, scale, limit, shards=(), kind=jnp.bfloat16):
    level = block_levels(own_key, dims, shards, -0.22, 0.18) if shards else 1.0
    drawn = jax.random.normal(own_key, dims, jnp.float32) * scale * level
    return jnp.minimum(jnp.maximum(drawn, -limit), limit).astype(kind)


def bell_draw_with(rng, extent, deviation, limit, shards, heavy, held_as=jnp.bfloat16):
    drawn = deviation * jax.random.normal(rng, extent, jnp.float32)
    if shards:
        drawn = drawn * block_levels(rng, extent, shards, -0.22, 0.18)
    return jnp.clip(strengthened(drawn, jax.random.fold_in(rng, 3), *heavy), -limit, limit).astype(held_as)


def setup_inputs(seed: int = 0) -> dict:
    key_of = jax.random.split(jax.random.key(seed), 22)
    tokens = bell_draw_with(key_of[0], (TOKENS, D), 1.0, 6.0, ((0, 32),), (0, 1, 32, 2.75))
    lengths = draw_lengths(jax.random.fold_in(key_of[21], 71), 0)
    rel_index = draw_rel_index(jax.random.fold_in(key_of[21], 71), 0)
    w_query = noise(key_of[3], (D, D), D ** -0.5, 0.21875, ((0, 32),))
    b_query = noise(key_of[4], (D,), 0.5, 3.0, ((0, 32),))
    w_key = noise(key_of[5], (D, D), D ** -0.5, 0.21875, ((0, 32),))
    b_key = noise(key_of[6], (D,), 0.5, 3.0, ((0, 32),))
    w_value = noise(key_of[7], (D, D), D ** -0.5, 0.21875, ((0, 32),))
    b_value = noise(key_of[8], (D,), 0.5, 3.0, ((0, 32),))
    w_out = noise(key_of[9], (D, D), (D // 64) ** -0.5, 1.75, ((0, 32),))
    b_out = noise(key_of[10], (D,), 0.5, 3.0, ((0, 32),))
    rel_table = noise(key_of[11], (2 * SPAN, D), 1.0, 6.0, ((1, 32),))
    gain_one = jnp.clip(1.0 + 0.1 * jax.random.normal(key_of[12], (D,), jnp.float32), 0.5, 1.5).astype(jnp.bfloat16)
    shift_one = noise(key_of[13], (D,), 0.3, 2.0, ((0, 32),))
    w_up = noise(key_of[14], (D, FF), D ** -0.5, 0.21875, ((0, 32),))
    b_up = noise(key_of[15], (FF,), 0.5, 3.0, ((0, 32),))
    w_down = noise(key_of[16], (FF, D), FF ** -0.5, 0.109375, ((0, 32),))
    b_down = noise(key_of[17], (D,), 0.5, 3.0, ((0, 32),))
    gain_two = jnp.clip(1.0 + 0.1 * jax.random.normal(key_of[18], (D,), jnp.float32), 0.5, 1.5).astype(jnp.bfloat16)
    shift_two = noise(key_of[19], (D,), 0.3, 2.0, ((0, 32),))
    cotangent = noise(key_of[20], (TOKENS, D), 1.0, 6.0, ((0, 32),))
    return dict(tokens=tokens, lengths=lengths, rel_index=rel_index, w_query=w_query, b_query=b_query, w_key=w_key, b_key=b_key, w_value=w_value, b_value=b_value, w_out=w_out, b_out=b_out, rel_table=rel_table, gain_one=gain_one, shift_one=shift_one, w_up=w_up, b_up=b_up, w_down=w_down, b_down=b_down, gain_two=gain_two, shift_two=shift_two, cotangent=cotangent)


@jax.custom_vjp
def low(v):
    return lax.optimization_barrier(v.astype(jnp.bfloat16)).astype(jnp.float32)

@jax.custom_vjp
def low_back(v):
    return v

def low_keep(v):
    return (low(v), None)

def low_pass(kept, grad):
    return (grad,)

def back_keep(v):
    return (v, None)

def back_low(kept, grad):
    return (low(grad),)
low.defvjp(low_keep, low_pass)
low_back.defvjp(back_keep, back_low)
EPS = 1e-06

def matmul(left, right):
    return jnp.dot(left, right, precision=lax.Precision.HIGHEST, preferred_element_type=jnp.float32)

def layer_norm(values, gain, shift):
    mean = lax.optimization_barrier(jnp.mean(values, axis=-1, keepdims=True))
    centred = values - mean
    spread = lax.optimization_barrier(jnp.mean(centred * centred, axis=-1, keepdims=True))
    return centred * lax.rsqrt(spread + EPS) * gain + shift

def skew(table, offset):
    count = table.shape[0]
    width = table.shape[1]
    flat = table.reshape(-1)
    piece = lax.slice_in_dim(flat, offset, offset + count * (width - 1))
    return piece.reshape(count, width - 1)[:, :count]

def split_heads(values):
    return values.reshape(values.shape[0], HEADS, HEAD).transpose(1, 0, 2)

def merge_heads(values):
    return values.transpose(1, 0, 2).reshape(values.shape[1], HEADS * HEAD)

def sequence_forward(inputs, length, pick, pick_reverse, w_query, b_query, w_key, b_key, w_value, b_value, w_out, b_out, rel_table, gain_one, shift_one, w_up, b_up, w_down, b_down, gain_two, shift_two):
    count = inputs.shape[0]
    live = jnp.arange(count, dtype=jnp.int32) < length
    query = low(low_back(matmul(inputs, w_query) + b_query))
    key = low(low_back(matmul(inputs, w_key) + b_key))
    value = low(low_back(matmul(inputs, w_value) + b_value))
    rel_key = low(low_back(matmul(rel_table, w_key) + b_key))
    rel_query = low(low_back(matmul(rel_table, w_query) + b_query))
    key_pos = low_back(matmul(pick_reverse, rel_key))
    query_pos = low_back(matmul(pick, rel_query))
    scale = (3.0 * HEAD) ** (-0.5)

    def head_fn(parts):
        head_query, head_key, head_value, head_key_pos, head_query_pos = parts
        content = matmul(head_query, head_key.T)
        to_place = skew(matmul(head_query, head_key_pos.T), count - 1)
        from_place = skew(matmul(head_key, head_query_pos.T), count).T
        scores = low_back(scale * (content + to_place + from_place))
        scores = jnp.where(live[None, :], scores, -1e+30)
        summit = lax.optimization_barrier(jnp.max(scores, axis=1, keepdims=True))
        weights = jnp.exp(scores - summit)
        probs = weights / lax.optimization_barrier(jnp.sum(weights, axis=1, keepdims=True))
        return matmul(low(probs), head_value)
    heads = lax.map(jax.checkpoint(head_fn), (split_heads(query), split_heads(key), split_heads(value), split_heads(key_pos), split_heads(query_pos)))
    context = low(low_back(merge_heads(heads)))
    mixed = inputs + low_back(matmul(context, w_out) + b_out)
    normed = layer_norm(mixed, gain_one, shift_one)
    up = low_back(matmul(low(normed), w_up) + b_up)
    act = low(jax.nn.gelu(up, approximate=False))
    second = normed + low_back(matmul(act, w_down) + b_down)
    return layer_norm(second, gain_two, shift_two) * live[:, None]

def reference(tokens, lengths, rel_index, w_query, b_query, w_key, b_key, w_value, b_value, w_out, b_out, rel_table, gain_one, shift_one, w_up, b_up, w_down, b_down, gain_two, shift_two, cotangent):
    weights = tuple((v.astype(jnp.float32) for v in (w_query, b_query, w_key, b_key, w_value, b_value, w_out, b_out, rel_table, gain_one, shift_one, w_up, b_up, w_down, b_down, gain_two, shift_two)))
    buckets = jnp.arange(2 * SPAN, dtype=jnp.int32)
    pick = (rel_index[:, None] == buckets[None, :]).astype(jnp.float32)
    pick_reverse = pick[::-1]
    batches = tokens.astype(jnp.float32).reshape(SEQS, SEQ, D)
    cotan_rows = cotangent.astype(jnp.float32).reshape(SEQS, SEQ, D)

    def advance(total, item):
        inputs, length, cotan_row = item

        def forward(values, *params):
            return sequence_forward(values, length, pick, pick_reverse, *params)
        result, pull = jax.vjp(forward, inputs, *weights)
        grads = pull(cotan_row)
        total = tuple((a + b for a, b in zip(total, grads[1:])))
        return (total, (result.astype(jnp.bfloat16), grads[0]))
    zeros = tuple((jnp.zeros(w.shape, jnp.float32) for w in weights))
    totals, (results, grad_inputs) = lax.scan(advance, zeros, (batches, lengths, cotan_rows))
    return (results.reshape(TOKENS, D), grad_inputs.reshape(TOKENS, D), totals[0], totals[1], totals[2], totals[3], totals[4], totals[5], totals[6], totals[7], totals[8], totals[9], totals[10], totals[11], totals[12], totals[13], totals[14], totals[15], totals[16])
```

```python
import jax, jax.numpy as jnp
from jax import lax
from jax.sharding import PartitionSpec as P
from jax.experimental import pallas as pl
from jax.experimental.pallas import tpu as pltpu

BF = jnp.bfloat16
F32 = jnp.float32
EPS = 1e-6


def dot(left, right, dims):
    return lax.dot_general(left, right, ((dims[:1], dims[1:]), ((), ())), preferred_element_type=F32)


def nn(left, right):
    return dot(left, right, (1, 0))


def nt(left, right):
    return dot(left, right, (1, 1))


def tn(left, right):
    return dot(left, right, (0, 0))


def iota(shape, axis):
    return lax.broadcasted_iota(jnp.int32, shape, axis)


def flip_matrix(size):
    return jnp.where(iota((size, size), 0) + iota((size, size), 1) == size - 1, 1.0, 0.0).astype(BF)


def attend_head(q_ref, k_ref, v_ref, kT_ref, kprT_ref, qpsT_ref, mask_ref, flip_ref, c0, hh, scale):
    T = q_ref.shape[0]
    B = T // 2
    lanes = pl.ds(c0, 128)
    rows = pl.ds(c0, 128)
    keep = (iota((1, 128), 1) // 64 == hh)
    qh = jnp.where(keep, q_ref[:, lanes], 0)
    kh = jnp.where(keep, k_ref[:, lanes], 0)
    content = nn(qh, kT_ref[rows, :])
    to, frm = [], []
    for b in range(2):
        u0 = B * (1 - b)
        t = nn(qh[b * B:(b + 1) * B], kprT_ref[rows, u0:u0 + 3 * B])
        to.append(pltpu.roll(t, 2 * B + 1, 1, stride=1, stride_axis=0)[:, :T])
        f = nn(kh[b * B:(b + 1) * B], qpsT_ref[rows, u0:u0 + 3 * B])
        frm.append(pltpu.roll(f, 2 * B + 1, 1, stride=1, stride_axis=0)[:, :T].T)
    s = content + jnp.concatenate(to, axis=0) + jnp.concatenate(frm, axis=1) + mask_ref[0:1, :]
    m = jnp.max(s, axis=1, keepdims=True)
    e = jnp.exp2((s - m) * (scale * 1.4426950408889634))
    total = jnp.sum(e, axis=1, keepdims=True)
    return (e * (1.0 / total)).astype(BF)


def attend_forward(pair, q_ref, k_ref, v_ref, kT_ref, kprT_ref, qpsT_ref, mask_ref, flip_ref, ctx_ref, pT_ref, scale):
    T = q_ref.shape[0]
    B = T // 2
    c0 = pl.multiple_of(pair * 128, 128)
    outs = []
    for hh in range(2):
        p = attend_head(q_ref, k_ref, v_ref, kT_ref, kprT_ref, qpsT_ref, mask_ref, flip_ref, c0, hh, scale)
        outs.append(nn(p, v_ref[:, pl.ds(c0, 128)]))
        pT_ref[2 * pair + hh, 0:B, :] = nt(flip_ref[...], p[:, B:T]).astype(BF)
        pT_ref[2 * pair + hh, B:T, :] = nt(flip_ref[...], p[:, 0:B]).astype(BF)
    ctx_ref[:, pl.ds(c0, 128)] = jnp.where(iota((1, 128), 1) < 64, outs[0], outs[1]).astype(BF)


def attend_backward(pair, q_ref, kf_ref, vf_ref, qT_ref, kfT_ref, kps_ref, qps_ref, dcT_ref, pT_ref,
                    dq_ref, dkf_ref, dvf_ref, dkpsT_ref, dqpsT_ref, scale):
    T = q_ref.shape[0]
    B = T // 2
    c0 = pl.multiple_of(pair * 128, 128)
    lanes = pl.ds(c0, 128)
    low = iota((1, 128), 1) < 64
    dqs, dks, dvs = [], [], []
    for hh in range(2):
        h = 2 * pair + hh
        r0 = pl.multiple_of(c0 + 64 * hh, 64)
        keep = (iota((1, 128), 1) // 64 == hh)
        vh = jnp.where(keep, vf_ref[:, lanes], 0)
        pT = pT_ref[h]
        dpT = nn(vh, dcT_ref[lanes, :])
        pw = pT.astype(F32)
        prod = pw * dpT
        inner = jnp.sum(prod, axis=0, keepdims=True) / jnp.sum(pw, axis=0, keepdims=True)
        dsT = (prod - pw * inner).astype(BF)
        dvs.append(nt(pT, dcT_ref[lanes, :]))
        dk = nn(dsT, q_ref[:, lanes])
        ds = dsT.T
        dq = nn(ds, kf_ref[:, lanes])
        zero = jnp.zeros((B, B), BF)
        dkp, dqp, gq, gk = [], [], [], []
        for b in range(2):
            gf = pltpu.roll(jnp.concatenate([dsT[b * B:(b + 1) * B], zero], axis=1), 0, 1, stride=1, stride_axis=0)
            dkp.append(nn(gf, qps_ref[b * B:b * B + 3 * B, lanes]))
            gq.append(nn(kfT_ref[pl.ds(r0, 64), b * B:(b + 1) * B], gf))
            gt = pltpu.roll(jnp.concatenate([ds[b * B:(b + 1) * B], zero], axis=1), 0, 1, stride=1, stride_axis=0)
            dqp.append(nn(gt, kps_ref[b * B:b * B + 3 * B, lanes]))
            gk.append(nn(qT_ref[pl.ds(r0, 64), b * B:(b + 1) * B], gt))
        dks.append(dk + jnp.concatenate(dkp, axis=0))
        dqs.append(dq + jnp.concatenate(dqp, axis=0))
        for ref, g in ((dqpsT_ref, gq), (dkpsT_ref, gk)):
            ref[pl.ds(r0, 64), 0:B] = (scale * g[0][:, 0:B]).astype(BF)
            ref[pl.ds(r0, 64), B:3 * B] = (scale * (g[0][:, B:] + g[1][:, 0:2 * B])).astype(BF)
            ref[pl.ds(r0, 64), 3 * B:] = (scale * g[1][:, 2 * B:]).astype(BF)
    dq_ref[:, lanes] = (scale * jnp.where(low, dqs[0], dqs[1])).astype(BF)
    dkf_ref[:, lanes] = (scale * jnp.where(low, dks[0], dks[1])).astype(BF)
    dvf_ref[:, lanes] = jnp.where(low, dvs[0], dvs[1]).astype(BF)


def normal_cdf_pair(x):
    a = jnp.abs(x)
    e = jnp.exp2(x * x * (-0.5 * 1.4426950408889634))
    t = 1.0 / (1.0 + (0.3275911 * 0.7071067811865476) * a)
    poly = ((((1.061405429 * t - 1.453152027) * t + 1.421413741) * t - 0.284496736) * t + 0.254829592) * t
    tail = 0.5 * poly * e
    return jnp.where(x < 0, tail, 1.0 - tail), e


def row_mean(x):
    return jnp.sum(x, axis=1, keepdims=True) * (1.0 / x.shape[1])


def norm_rows(x):
    centred = x - row_mean(x)
    inv = lax.rsqrt(row_mean(centred * centred) + EPS)
    return centred * inv, inv


def norm_back(g, n, inv):
    return (g - row_mean(g) - n * row_mean(g * n)) * inv


def column_sum(x):
    return jnp.sum(x, axis=0, keepdims=True)


def dense_block(length, x_ref, ctx_ref, cot_ref, wo_ref, wup_ref, wdown_ref, rows_ref, bup_ref,
                out_ref, gmixed_ref, dcT_ref, gwo_ref, gwup_ref, gwdown_ref, small_ref, gbup_ref,
                normed_ref, nb_ref, n1_ref, inv1_ref, act_ref, gp_ref, second_ref, gd_ref, gu_ref):
    T, D = x_ref.shape
    FF = wup_ref.shape[1]
    C = 256
    row = lambda k: rows_ref[k:k + 1, :]

    def cols(n, size=C):
        return pl.ds(pl.multiple_of(n * size, size), size)

    @pl.loop(0, D // C)
    def _(n):
        second_ref[:, cols(n)] = x_ref[:, cols(n)].astype(F32) + (nn(ctx_ref[...], wo_ref[:, cols(n)]) + rows_ref[3:4, cols(n)])

    R = 128

    @pl.loop(0, T // R)
    def _(r):
        rs = pl.ds(pl.multiple_of(r * R, R), R)
        n1, inv1 = norm_rows(second_ref[rs, :])
        normed = n1 * row(4) + row(5)
        n1_ref[rs, :] = n1
        inv1_ref[rs, :] = jnp.broadcast_to(inv1, (R, 128))
        normed_ref[rs, :] = normed
        nb_ref[rs, :] = normed.astype(BF)

    @pl.loop(0, FF // C)
    def _(n):
        up = nn(nb_ref[...], wup_ref[:, cols(n)]) + bup_ref[0:1, cols(n)]
        phi, e = normal_cdf_pair(up)
        act_ref[:, cols(n)] = (up * phi).astype(BF)
        gp_ref[:, cols(n)] = (phi + up * e * 0.3989422804014327).astype(gp_ref.dtype)

    @pl.loop(0, D // C)
    def _(n):
        second_ref[:, cols(n)] = normed_ref[:, cols(n)] + (nn(act_ref[...], wdown_ref[:, cols(n)]) + rows_ref[6:7, cols(n)])

    small_ref[...] = jnp.zeros_like(small_ref)

    @pl.loop(0, T // R)
    def _(r):
        rs = pl.ds(pl.multiple_of(r * R, R), R)
        live = jnp.where(iota((R, 1), 0) + r * R < length, 1.0, 0.0)
        n2, inv2 = norm_rows(second_ref[rs, :])
        out_ref[rs, :] = ((n2 * row(7) + row(8)) * live).astype(BF)
        start = cot_ref[rs, :].astype(F32) * live
        gsec = norm_back(start * row(7), n2, inv2)
        second_ref[rs, :] = gsec
        gd = gsec.astype(BF)
        gd_ref[rs, :] = gd
        small_ref[6:7, :] += column_sum(gd.astype(F32))
        small_ref[7:8, :] += column_sum(start * n2)
        small_ref[8:9, :] += column_sum(start)

    @pl.loop(0, FF // C)
    def _(n):
        gu = nt(gd_ref[...], wdown_ref[cols(n), :]) * gp_ref[:, cols(n)].astype(F32)
        gub = gu.astype(BF)
        gu_ref[:, cols(n)] = gub
        gbup_ref[0:1, cols(n)] = column_sum(gub.astype(F32))
        gwdown_ref[cols(n), :] = tn(act_ref[:, cols(n)], gd_ref[...]).astype(gwdown_ref.dtype)
        gwup_ref[:, cols(n)] = tn(nb_ref[...], gub).astype(gwup_ref.dtype)

    @pl.loop(0, D // C)
    def _(n):
        second_ref[:, cols(n)] += nt(gu_ref[...], wup_ref[cols(n), :])

    @pl.loop(0, T // R)
    def _(r):
        rs = pl.ds(pl.multiple_of(r * R, R), R)
        gn = second_ref[rs, :]
        n1 = n1_ref[rs, :]
        gm = norm_back(gn * row(4), n1, inv1_ref[rs, 0:1])
        gmixed_ref[rs, :] = gm
        ga = gm.astype(BF)
        gd_ref[rs, :] = ga
        small_ref[3:4, :] += column_sum(ga.astype(F32))
        small_ref[4:5, :] += column_sum(gn * n1)
        small_ref[5:6, :] += column_sum(gn)

    @pl.loop(0, D // C)
    def _(n):
        gwo_ref[cols(n), :] = tn(ctx_ref[:, cols(n)], gd_ref[...]).astype(gwo_ref.dtype)
        dcT_ref[cols(n), :] = nt(wo_ref[cols(n), :], gd_ref[...]).astype(BF)


def project(x_ref, relT_ref, wq_ref, wk_ref, wv_ref, rows_ref, bcols_ref, idx_ref, flip_ref,
            q_ref, k_ref, v_ref, qT_ref, kT_ref, kf_ref, vf_ref, kfT_ref, kprT_ref, qpsT_ref, kpsT_ref,
            pickB_ref, pickA_ref):
    T, D = x_ref.shape
    NB = relT_ref.shape[1]
    C = 256
    B = T // 2

    def cols(n, size=C):
        return pl.ds(pl.multiple_of(n * size, size), size)

    pickA_ref[...] = jnp.where(iota((NB, 2 * T), 0) == idx_ref[0:1, :], 1.0, 0.0).astype(BF)
    pickB_ref[...] = jnp.where(iota((NB, 2 * T), 0) == idx_ref[1:2, :], 1.0, 0.0).astype(BF)

    @pl.loop(0, D // C)
    def _(n):
        q = (nn(x_ref[...], wq_ref[:, cols(n)]) + rows_ref[0:1, cols(n)]).astype(BF)
        q_ref[:, cols(n)] = q
        qT_ref[cols(n), :] = q.T
        k = (nn(x_ref[...], wk_ref[:, cols(n)]) + rows_ref[1:2, cols(n)]).astype(BF)
        k_ref[:, cols(n)] = k
        kT_ref[cols(n), :] = k.T
        v = (nn(x_ref[...], wv_ref[:, cols(n)]) + rows_ref[2:3, cols(n)]).astype(BF)
        v_ref[:, cols(n)] = v
        for src, dst in ((k, kf_ref), (v, vf_ref)):
            dst[0:B, cols(n)] = nn(flip_ref[...], src[B:T]).astype(BF)
            dst[B:T, cols(n)] = nn(flip_ref[...], src[0:B]).astype(BF)
        kfT_ref[cols(n), :] = kf_ref[:, cols(n)].T
        rk = (tn(wk_ref[:, cols(n)], relT_ref[...]) + bcols_ref[cols(n), 1:2].astype(F32)).astype(BF)
        rq = (tn(wq_ref[:, cols(n)], relT_ref[...]) + bcols_ref[cols(n), 0:1].astype(F32)).astype(BF)
        kprT_ref[cols(n), :] = nn(rk, pickA_ref[...]).astype(BF)
        kpsT_ref[cols(n), :] = nn(rk, pickB_ref[...]).astype(BF)
        qpsT_ref[cols(n), :] = nn(rq, pickB_ref[...]).astype(BF)


def project_back(x_ref, relT_ref, wq_ref, wk_ref, wv_ref, pickB_ref, flip_ref, gmixed_ref,
                 dq_ref, dkf_ref, dvf_ref, dkpsT_ref, dqpsT_ref,
                 gtok_ref, gwq_ref, gwk_ref, gwv_ref, grelT_ref, small_ref,
                 dk_ref, dv_ref, grk_ref, grq_ref):
    T, D = x_ref.shape
    NB = relT_ref.shape[1]
    C = 256
    B = T // 2

    def cols(n, size=C):
        return pl.ds(pl.multiple_of(n * size, size), size)

    @pl.loop(0, D // C)
    def _(n):
        for src, dst in ((dkf_ref, dk_ref), (dvf_ref, dv_ref)):
            dst[0:B, cols(n)] = nn(flip_ref[...], src[B:T, cols(n)]).astype(BF)
            dst[B:T, cols(n)] = nn(flip_ref[...], src[0:B, cols(n)]).astype(BF)
        grk_ref[cols(n), :] = nt(dkpsT_ref[cols(n), :], pickB_ref[...]).astype(BF)
        grq_ref[cols(n), :] = nt(dqpsT_ref[cols(n), :], pickB_ref[...]).astype(BF)

    ones_t = jnp.ones((8, T), BF)
    ones_b = jnp.ones((8, NB), BF)

    @pl.loop(0, D // C)
    def _(n):
        gwq_ref[cols(n), :] = (tn(x_ref[:, cols(n)], dq_ref[...]) + nt(relT_ref[cols(n), :], grq_ref[...])).astype(gwq_ref.dtype)
        gwk_ref[cols(n), :] = (tn(x_ref[:, cols(n)], dk_ref[...]) + nt(relT_ref[cols(n), :], grk_ref[...])).astype(gwk_ref.dtype)
        gwv_ref[cols(n), :] = tn(x_ref[:, cols(n)], dv_ref[...]).astype(gwv_ref.dtype)
        grelT_ref[cols(n), :] = (nn(wk_ref[cols(n), :], grk_ref[...]) + nn(wq_ref[cols(n), :], grq_ref[...])).astype(grelT_ref.dtype)
        gtok_ref[:, cols(n)] = gmixed_ref[:, cols(n)] + (
            nt(dq_ref[...], wq_ref[cols(n), :]) + nt(dk_ref[...], wk_ref[cols(n), :]) + nt(dv_ref[...], wv_ref[cols(n), :]))
        small_ref[0:1, cols(n)] = (nn(ones_t, dq_ref[:, cols(n)]) + nt(ones_b, grq_ref[cols(n), :]))[0:1]
        small_ref[1:2, cols(n)] = (nn(ones_t, dk_ref[:, cols(n)]) + nt(ones_b, grk_ref[cols(n), :]))[0:1]
        small_ref[2:3, cols(n)] = nn(ones_t, dv_ref[:, cols(n)])[0:1]


def vmem_call(kernel, outs, scratch, operands, smem=0):
    specs = [pl.BlockSpec(memory_space=pltpu.SMEM)] * smem + [pl.BlockSpec(memory_space=pltpu.VMEM)] * (len(operands) - smem)
    return pl.pallas_call(
        kernel,
        out_shape=outs,
        in_specs=specs,
        out_specs=tuple(pl.BlockSpec(memory_space=pltpu.VMEM) for _ in outs),
        scratch_shapes=scratch,
        compiler_params=pltpu.CompilerParams(vmem_limit_bytes=60 * 2**20),
    )(*operands)


def layer(x, length, rel_index, cot, wq, wk, wv, wo, relT, wup, wdown, bcols, bup, grad_type):
    T, D = x.shape
    FF = wup.shape[1]
    NB = relT.shape[1]
    heads = D // 64
    scale = 192.0 ** -0.5
    S = jax.ShapeDtypeStruct
    V = pltpu.VMEM
    rows = bcols.astype(F32).T
    bup8 = jnp.broadcast_to(bup.astype(F32)[None, :], (8, FF))
    bcols = jnp.pad(bcols, ((0, 0), (0, 128 - bcols.shape[1])))
    shifted = jnp.concatenate([rel_index[1:], jnp.full((1,), -1, jnp.int32)])
    idx = jnp.concatenate([rel_index[None, ::-1], shifted[None, :], jnp.zeros((6, 2 * T), jnp.int32)])
    flip = flip_matrix(T // 2)
    mask = jnp.broadcast_to(jnp.where(jnp.arange(T)[None, :] < length[0], 0.0, -1e30).astype(F32), (8, T))

    td, dt, d2t = S((T, D), BF), S((D, T), BF), S((D, 2 * T), BF)
    q, k, v, qT, kT, kf, vf, kfT, kprT, qpsT, kpsT, pick = vmem_call(
        project, (td, td, td, dt, dt, td, td, dt, d2t, d2t, d2t, S((NB, 2 * T), BF)),
        (V((NB, 2 * T), BF),),
        (x, relT, wq, wk, wv, rows, bcols, idx, flip))

    def forward(*refs):
        @pl.loop(0, heads // 2)
        def _(p):
            attend_forward(p, *refs, scale)

    ctx, pT = vmem_call(forward, (td, S((heads, T, T), BF)), (), (q, k, v, kT, kprT, qpsT, mask, flip))

    def dense(length_ref, *refs):
        dense_block(length_ref[0], *refs)

    out, gmixed, dcT, gwo, gwup, gwdown, small, gbup = vmem_call(
        dense,
        (td, S((T, D), F32), dt, S((D, D), grad_type), S((D, FF), grad_type), S((FF, D), grad_type), S((16, D), F32), S((8, FF), F32)),
        (V((T, D), F32), V((T, D), BF), V((T, D), F32), V((T, 128), F32), V((T, FF), BF), V((T, FF), BF), V((T, D), F32), V((T, D), BF), V((T, FF), BF)),
        (length, x, ctx, cot, wo, wup, wdown, rows, bup8), smem=1)

    def backward(*refs):
        @pl.loop(0, heads // 2)
        def _(p):
            attend_backward(p, *refs, scale)

    dq, dkf, dvf, dkpsT, dqpsT = vmem_call(
        backward, (td, td, td, d2t, d2t), (), (q, kf, vf, qT, kfT, kpsT.T, qpsT.T, dcT, pT))
    gtok, gwq, gwk, gwv, grelT, small2 = vmem_call(
        project_back,
        (S((T, D), F32), S((D, D), grad_type), S((D, D), grad_type), S((D, D), grad_type), S((D, NB), grad_type), S((16, D), F32)),
        (V((T, D), BF), V((T, D), BF), V((D, NB), BF), V((D, NB), BF)),
        (x, relT, wq, wk, wv, pick, flip, gmixed, dq, dkf, dvf, dkpsT, dqpsT))
    small = jnp.concatenate([small2[:3], small[3:9]])
    return out, gtok, gwq, gwk, gwv, gwo, grelT, gwup, gwdown, small, gbup[0]


AXES = ("dp", "fsdp")


def body(tokens, lengths, rel_index, w_query, b_query, w_key, b_key, w_value, b_value, w_out, b_out, rel_table,
         gain_one, shift_one, w_up, b_up, w_down, b_down, gain_two, shift_two, cotangent):
    rows, D = w_query.shape
    NB = rel_table.shape[0]
    FF = w_up.shape[1]
    vectors = (b_query, b_key, b_value, b_out, gain_one, shift_one, b_down, gain_two, shift_two)
    per = FF // D
    cols = jnp.concatenate([jnp.stack(vectors, axis=1), b_up.reshape(rows, per), jnp.zeros((rows, 128 - 9 - per), BF)], axis=1)
    pack = jnp.concatenate([w_query, w_key, w_value, w_out, rel_table.T, cols], axis=1)
    gathered = lax.all_gather(pack, AXES, axis=0, tiled=True)
    wup = lax.all_gather(w_up, AXES, axis=0, tiled=True)
    wdown = lax.all_gather(w_down, AXES, axis=0, tiled=True)
    wq, wk, wv, wo = (gathered[:, i * D:(i + 1) * D] for i in range(4))
    relT = gathered[:, 4 * D:4 * D + NB]
    bcols = gathered[:, 4 * D + NB:]
    bup = bcols[:, 9:9 + per].reshape(FF)
    bcols = jnp.concatenate([bcols[:, :9], jnp.zeros((D, 7), BF)], axis=1)
    out, gtok, gwq, gwk, gwv, gwo, grelT, gwup, gwdown, small, gbup = layer(
        tokens, lengths, rel_index, cotangent, wq, wk, wv, wo, relT, wup, wdown, bcols, bup, F32)
    gwup = lax.psum_scatter(gwup, AXES, scatter_dimension=0, tiled=True)
    gwdown = lax.psum_scatter(gwdown, AXES, scatter_dimension=0, tiled=True)
    gcols = jnp.concatenate([small.T, gbup.reshape(D, per), jnp.zeros((D, 128 - 9 - per), F32)], axis=1)
    gpack = jnp.concatenate([gwq, gwk, gwv, gwo, grelT, gcols], axis=1)
    gpack = lax.psum_scatter(gpack, AXES, scatter_dimension=0, tiled=True)
    gq, gk, gv, go = (gpack[:, i * D:(i + 1) * D] for i in range(4))
    grel = gpack[:, 4 * D:4 * D + NB].T
    g = gpack[:, 4 * D + NB:]
    return (out, gtok, gq, g[:, 0], gk, g[:, 1], gv, g[:, 2], go, g[:, 3], grel, g[:, 4], g[:, 5],
            gwup, g[:, 9:9 + per].reshape(rows * per), gwdown, g[:, 6], g[:, 7], g[:, 8])


def solution(mesh):
    rows, vec = P(AXES, None), P(AXES)
    return jax.shard_map(
        body,
        mesh=mesh,
        in_specs=(rows, vec, P(), rows, vec, rows, vec, rows, vec, rows, vec, P(None, AXES), vec, vec, rows, vec, rows, vec, vec, vec, rows),
        out_specs=(rows, rows, rows, vec, rows, vec, rows, vec, rows, vec, P(None, AXES), vec, vec, rows, vec, rows, vec, vec, vec),
        check_vma=False,
    )
```

```python
import jax
import jax.numpy as jnp
from jax import lax
from jax.experimental import pallas as pl
from jax.experimental.pallas import tpu as pltpu
from jax.sharding import PartitionSpec as P

BF = jnp.bfloat16
F32 = jnp.float32
EPS = 1e-6
HEAD = 64
AXES = ("dp", "fsdp")
MESH = pl.DeviceIdType.MESH
LOG2E = 1.4426950408889634
GRID = (2, 4, 2, 2)
BLOCKS = 32
CUT = 384
SLOTS = 3


def dot(left, right, dims):
    return lax.dot_general(left, right, ((dims[:1], dims[1:]), ((), ())), preferred_element_type=F32)


def nn(left, right):
    return dot(left, right, (1, 0))


def nt(left, right):
    return dot(left, right, (1, 1))


def tn(left, right):
    return dot(left, right, (0, 0))


def iota(shape, axis):
    return lax.broadcasted_iota(jnp.int32, shape, axis)


def column_sum(x):
    return jnp.sum(x, axis=0, keepdims=True)


def row_mean(x):
    return jnp.sum(x, axis=1, keepdims=True) * (1.0 / x.shape[1])


def norm_rows(x):
    centred = x - row_mean(x)
    inv = lax.rsqrt(row_mean(centred * centred) + EPS)
    return centred * inv, inv


def norm_back(g, n, inv):
    return (g - row_mean(g) - n * row_mean(g * n)) * inv


def normal_cdf_pair(x):
    a = jnp.abs(x)
    e = jnp.exp2(x * x * (-0.5 * LOG2E))
    t = 1.0 / (1.0 + (0.3275911 * 0.7071067811865476) * a)
    poly = ((((1.061405429 * t - 1.453152027) * t + 1.421413741) * t - 0.284496736) * t + 0.254829592) * t
    tail = 0.5 * poly * e
    return jnp.where(x < 0, tail, 1.0 - tail), e


def tile(n, size):
    return pl.ds(pl.multiple_of(n * size, size), size)


def matrix(value):
    rows = 1
    for size in value.shape[:-1]:
        rows *= size
    return value.reshape(rows, value.shape[-1])


def pair_forward(pair, q_ref, k_ref, v_ref, kprT_ref, qpsT_ref, mask_ref, flip_ref, ctx_ref, pT_ref, scale):
    T = q_ref.shape[0]
    B = T // 2
    lanes = tile(pair, 128)
    outs = []
    for hh in range(2):
        keep = iota((1, 128), 1) // HEAD == hh
        qh = jnp.where(keep, q_ref[:, lanes], 0)
        kh = jnp.where(keep, k_ref[:, lanes], 0)
        content = nt(qh, k_ref[:, lanes])
        to, frm = [], []
        for b in range(2):
            u0 = B * (1 - b)
            t = nn(qh[b * B:(b + 1) * B], kprT_ref[lanes, u0:u0 + 3 * B])
            to.append(pltpu.roll(t, 2 * B + 1, 1, stride=1, stride_axis=0)[:, :T])
            f = nn(kh[b * B:(b + 1) * B], qpsT_ref[lanes, u0:u0 + 3 * B])
            frm.append(pltpu.roll(f, 2 * B + 1, 1, stride=1, stride_axis=0)[:, :T].T)
        s = content + jnp.concatenate(to, axis=0) + jnp.concatenate(frm, axis=1) + mask_ref[0:1, :]
        top = jnp.max(s, axis=1, keepdims=True)
        e = jnp.exp2((s - top) * (scale * LOG2E))
        p = (e * (1.0 / jnp.sum(e, axis=1, keepdims=True))).astype(BF)
        outs.append(nn(p, v_ref[:, lanes]))
        pT_ref[2 * pair + hh, 0:B, :] = nt(flip_ref[...], p[:, B:T]).astype(BF)
        pT_ref[2 * pair + hh, B:T, :] = nt(flip_ref[...], p[:, 0:B]).astype(BF)
    ctx_ref[:, lanes] = jnp.where(iota((1, 128), 1) < HEAD, outs[0], outs[1]).astype(BF)


def pair_backward(pair, q_ref, kf_ref, vf_ref, kpsT_ref, qpsT_ref, dcT_ref, pT_ref, scale):
    T = q_ref.shape[0]
    B = T // 2
    lanes = tile(pair, 128)
    low = iota((1, 128), 1) < HEAD
    q, kf, dcT = q_ref[:, lanes], kf_ref[:, lanes], dcT_ref[lanes, :]
    dqs, dks, dvs, gks, gqs = [], [], [], [], []
    for hh in range(2):
        vh = jnp.where(iota((1, 128), 1) // HEAD == hh, vf_ref[:, lanes], 0)
        pT = pT_ref[2 * pair + hh]
        dpT = nn(vh, dcT)
        wide = pT.astype(F32)
        prod = wide * dpT
        inner = column_sum(prod) / column_sum(wide)
        dsT = (prod - wide * inner).astype(BF)
        ds = dsT.T
        zero = jnp.zeros((B, B), BF)
        dk, dq, gq, gk = [], [], [], []
        for b in range(2):
            rows, span = slice(b * B, (b + 1) * B), slice(b * B, b * B + 3 * B)
            gf = pltpu.roll(jnp.concatenate([dsT[rows], zero], axis=1), 0, 1, stride=1, stride_axis=0)
            dk.append(nn(dsT[rows], q) + nt(gf, qpsT_ref[lanes, span]))
            gq.append(tn(kf[rows], gf)[hh * HEAD:(hh + 1) * HEAD])
            gt = pltpu.roll(jnp.concatenate([ds[rows], zero], axis=1), 0, 1, stride=1, stride_axis=0)
            dq.append(nn(ds[rows], kf) + nt(gt, kpsT_ref[lanes, span]))
            gk.append(tn(q[rows], gt)[hh * HEAD:(hh + 1) * HEAD])
        dks.append(jnp.concatenate(dk, axis=0))
        dqs.append(jnp.concatenate(dq, axis=0))
        dvs.append(nt(pT, dcT))
        gqs.append(gq)
        gks.append(gk)
    for ref, pieces in ((qpsT_ref, gqs), (kpsT_ref, gks)):
        for hh in range(2):
            g = pieces[hh]
            rows = pl.ds(pl.multiple_of(pair * 128 + HEAD * hh, HEAD), HEAD)
            ref[rows, 0:B] = (scale * g[0][:, 0:B]).astype(BF)
            ref[rows, B:3 * B] = (scale * (g[0][:, B:] + g[1][:, 0:2 * B])).astype(BF)
            ref[rows, 3 * B:] = (scale * g[1][:, 2 * B:]).astype(BF)
    q_ref[:, lanes] = (scale * jnp.where(low, dqs[0], dqs[1])).astype(BF)
    kf_ref[:, lanes] = (scale * jnp.where(low, dks[0], dks[1])).astype(BF)
    vf_ref[:, lanes] = jnp.where(low, dvs[0], dvs[1]).astype(BF)


class Place:
    def __init__(self):
        self.nz = GRID[1]
        self.c = lax.axis_index("dp")
        f = lax.axis_index("fsdp")
        self.x = lax.rem(f, 2)
        self.y = lax.rem(lax.div(f, 2), 2)
        self.z = lax.div(f, 4)
        self.nx = 1 - self.x
        self.ny = 1 - self.y

    def at(self, c=None, z=None, y=None, x=None):
        c = self.c if c is None else c
        z = self.z if z is None else z
        y = self.y if y is None else y
        x = self.x if x is None else x
        return (c, (z * 2 + y) * 2 + x)

    def zs(self):
        return [lax.rem(self.z + d, self.nz) for d in range(1, self.nz)]

    def barrier(self):
        sem = pltpu.get_barrier_semaphore()
        peers = [self.at(z=z) for z in self.zs()] + [self.at(x=self.nx), self.at(y=self.ny), self.at(c=1 - self.c)]
        for peer in peers:
            pl.semaphore_signal(sem, inc=1, device_id=peer, device_id_type=MESH)
        pl.semaphore_wait(sem, len(peers))


def remote(src, dst, send, recv, to):
    return pltpu.make_async_remote_copy(src_ref=src, dst_ref=dst, send_sem=send, recv_sem=recv, device_id=to, device_id_type=MESH)


class Gather:
    def __init__(self, place, piece, cols, send, recv):
        self.p, self.piece, self.send, self.recv = place, piece, send, recv
        self.all, self.h1, self.h2 = pl.ds(0, cols), pl.ds(0, CUT), pl.ds(CUT, cols - CUT)

    def copies(self, k, arriving=False):
        p, g, every = self.p, self.piece, slice(None)
        x, y, c = (p.nx, p.ny, 1 - p.c) if arriving else (p.x, p.y, p.c)
        if k == 0:
            for d in range(1, p.nz):
                z = lax.rem(p.z + (p.nz - d if arriving else d), p.nz)
                yield d - 1, g(p.c, z if arriving else p.z, p.y, p.x, self.all), p.at(z=z)
        elif k == 1:
            yield 3, g(p.c, every, p.y, x, self.h1), p.at(x=p.nx)
            yield 4, g(p.c, every, y, p.x, self.h2), p.at(y=p.ny)
        elif k == 2:
            yield 5, g(p.c, every, y, every, self.h1), p.at(y=p.ny)
            yield 6, g(p.c, every, every, x, self.h2), p.at(x=p.nx)
        else:
            yield 7, g(c, every, every, every, self.all), p.at(c=1 - p.c)

    def make(self, k, arriving=False):
        return [remote(ref, ref, self.send.at[i], self.recv.at[i], to) for i, ref, to in self.copies(k, arriving)]

    def step(self, k):
        if k > 0:
            for copy in self.make(k - 1, arriving=True):
                copy.wait_recv()
        if k < 4:
            for copy in self.make(k):
                copy.start()
        else:
            for j in range(4):
                for copy in self.make(j):
                    copy.wait_send()


def add_into(ref, other):
    ref[...] = (ref[...].astype(F32) + other[...].astype(F32)).astype(BF)


class Scatter:
    def __init__(self, place, piece, cols, order, buffers, send, recv, credit, finish):
        self.p, self.piece, self.order, self.send, self.recv = place, piece, order, send, recv
        self.credit, self.finish = credit, finish
        rest = pl.ds(0, cols - CUT)
        self.all, self.h1, self.h2 = pl.ds(0, cols), pl.ds(0, CUT), pl.ds(CUT, cols - CUT)
        rd, ry, rx, rx2, ry2, rz = buffers
        self.rd = rd.at[order % SLOTS, :, :, :, :, self.all]
        self.ry, self.rx = ry.at[order], rx.at[order, :, :, :, rest]
        self.rx2, self.ry2 = rx2.at[order], ry2.at[order, :, :, rest]
        self.rz = rz.at[order, :, :, self.all]

    def make(self, k):
        p, g, every = self.p, self.piece, slice(None)
        if k == 0:
            found = [(g(1 - p.c, every, every, every, self.all), self.rd, p.at(c=1 - p.c))]
        elif k == 1:
            found = [(g(p.c, every, p.ny, every, self.h1), self.ry, p.at(y=p.ny)),
                     (g(p.c, every, every, p.nx, self.h2), self.rx, p.at(x=p.nx))]
        elif k == 2:
            found = [(g(p.c, every, p.y, p.nx, self.h1), self.rx2, p.at(x=p.nx)),
                     (g(p.c, every, p.ny, p.x, self.h2), self.ry2, p.at(y=p.ny))]
        else:
            found = [(g(p.c, z, p.y, p.x, self.all), self.rz.at[d], p.at(z=z)) for d, z in enumerate(p.zs())]
        first = (0, 1, 3, 5)[k]
        return [remote(src, dst, self.send.at[first + i], self.recv.at[first + i], to) for i, (src, dst, to) in enumerate(found)]

    def step(self, k, last):
        p, g, every = self.p, self.piece, slice(None)
        if k > 0:
            for copy in self.make(k - 1):
                copy.wait_recv()
        if k == 0 and self.order >= SLOTS:
            pl.semaphore_wait(self.credit, 1)
        if k == 1:
            @pl.loop(0, p.nz)
            def _(z):
                add_into(g(p.c, z, every, every, self.all), self.rd.at[z])
            if self.order + SLOTS < last:
                pl.semaphore_signal(self.credit, inc=1, device_id=p.at(c=1 - p.c), device_id_type=MESH)
        elif k == 2:
            @pl.loop(0, p.nz)
            def _(z):
                add_into(g(p.c, z, p.y, every, self.h1), self.ry.at[z])
                add_into(g(p.c, z, every, p.x, self.h2), self.rx.at[z])
        elif k == 3:
            add_into(g(p.c, every, p.y, p.x, self.h1), self.rx2)
            add_into(g(p.c, every, p.y, p.x, self.h2), self.ry2)
        elif k == 4:
            total = g(p.c, p.z, p.y, p.x, self.all)[...].astype(F32)
            for d in range(p.nz - 1):
                total = total + self.rz[d].astype(F32)
            self.finish(total)
        if k < 4:
            for copy in self.make(k):
                copy.start()
        else:
            for j in range(4):
                for copy in self.make(j):
                    copy.wait_send()


def layer_kernel(
    comm,
    length_ref, idx_ref, x_ref, cot_ref, r_in, q_in, k_in, v_in, o_in, up_in, down_in,
    out_ref, gtok_ref, r_out, q_out, k_out, v_out, o_out, up_out, down_out,
    GR, GA, GO, GU, GD,
    q_ref, k_ref, v_ref, kf_ref, vf_ref, kprT_ref, kpsT_ref, qpsT_ref, pick_ref, pT_ref,
    ctx_ref, dcT_ref, n1_ref, inv1_ref, nb_ref, gd_ref, act_ref, gp_ref,
    grel_ref, cols_ref, rows_ref, bup_ref, small_ref, gbup_ref, mask_ref, flip_ref, select_ref,
    *rest,
):
    T, D = x_ref.shape
    FF = act_ref.shape[1]
    NB = pick_ref.shape[0]
    B = T // 2
    C = 256
    R = 128
    CH = FF // D
    scale = (3.0 * HEAD) ** -0.5
    length = length_ref[0]
    row = lambda k: rows_ref[k:k + 1, :]
    last = 1 + D // C + 1 + 2 * CH
    nA, nO, nU, nD = 1, 1 + D // C, 2 + D // C, 2 + D // C + CH
    whole = (slice(None),) * 4

    def part(ref, *lead, trail=()):
        return lambda c, z, y, x, cols: ref.at[(*lead, c, z, y, x, *trail, slice(None), cols)]

    pieces = ([(part(GR), NB + 128)] + [(part(GA, n), D) for n in range(D // C)] + [(part(GO), D)]
              + [(part(GU, k), D) for k in range(CH)] + [(part(GD, trail=(k,)), D) for k in range(CH)])
    gathers, scatters = [], []
    if comm:
        rd, ry, rx, rx2, ry2, rz, ag_send, ag_recv, rs_send, rs_recv, credit = rest
        place = Place()
        gathers = [Gather(place, piece, cols, ag_send.at[i], ag_recv.at[i]) for i, (piece, cols) in enumerate(pieces)]
        order = [nU + k for k in range(CH)] + [nD + k for k in range(CH)] + [nO] + [nA + n for n in range(D // C)] + [0]

        def finisher(i):
            def store(total):
                if i == 0:
                    r_out[...] = total
                elif i < nO:
                    cols = pl.ds((i - nA) * C, C)
                    q_out[:, cols], k_out[:, cols], v_out[:, cols] = total[:, :C], total[:, C:2 * C], total[:, 2 * C:]
                elif i == nO:
                    o_out[...] = total
                elif i < nD:
                    up_out[:, pl.ds((i - nU) * D, D)] = total
                else:
                    down_out[i - nD] = total
            return store

        for j, i in enumerate(order):
            piece, cols = pieces[i]
            scatters.append(Scatter(place, piece, cols, j, (rd, ry, rx, rx2, ry2, rz), rs_send.at[j], rs_recv.at[j], credit, finisher(i)))

    def gather_tick(t):
        if not comm:
            return
        for k in range(4):
            i = 2 + t - (k - 1)
            if (2 < i if k == 0 else 2 <= i) and i < last:
                gathers[i].step(k)

    starts = list(range(2 * CH + 1)) + [2 * CH + 1, 2 * CH + 3, 2 * CH + 6, 2 * CH + 7]

    def scatter_tick(t):
        if not comm:
            return
        for k in range(5):
            for j in range(last):
                if starts[j] + k == t:
                    scatters[j].step(k, last)

    if comm:
        place.barrier()
        me = (place.c, place.z, place.y, place.x)
        GR[me] = r_in[...]
        GA[(0, *me)] = jnp.concatenate([q_in[:, 0:C], k_in[:, 0:C], v_in[:, 0:C]], axis=1)
        gathers[0].step(0)
        gathers[1].step(0)
        for n in range(1, D // C):
            cols = pl.ds(n * C, C)
            GA[(n, *me)] = jnp.concatenate([q_in[:, cols], k_in[:, cols], v_in[:, cols]], axis=1)
        GO[me] = o_in[...]
        for k in range(CH):
            GU[(k, *me)] = up_in[:, pl.ds(k * D, D)]
            GD[(*me, k)] = down_in[k]
    else:
        GRh, GAh, GOh, GUh, GDh = rest[:5]
        sems = rest[10]
        loads = [pltpu.make_async_copy(src, dst, sems.at[i]) for i, (src, dst) in enumerate(zip((GRh, GAh, GOh, GUh, GDh), (GR, GA, GO, GU, GD)))]
        for copy in loads:
            copy.start()
        for copy in loads:
            copy.wait()
    pickA = act_ref.at[:, 0:2 * T]
    pickA[...] = jnp.where(iota((NB, 2 * T), 0) == idx_ref[0:1, :], 1.0, 0.0).astype(BF)
    pick_ref[...] = jnp.where(iota((NB, 2 * T), 0) == idx_ref[1:2, :], 1.0, 0.0).astype(BF)
    flip_ref[...] = jnp.where(iota((B, B), 0) + iota((B, B), 1) == B - 1, 1.0, 0.0).astype(BF)
    select_ref[...] = jnp.where(iota((C // CH, C), 0) == iota((C // CH, C), 1) // CH, 1.0, 0.0).astype(BF)
    mask_ref[...] = jnp.where(iota((8, T), 1) < length, 0.0, -1e30)
    small_ref[...] = jnp.zeros_like(small_ref)
    grel_ref[...] = jnp.zeros_like(grel_ref)
    if comm:
        gathers[0].step(1)
        gathers[2].step(0)
        gathers[1].step(1)
        gathers[0].step(2)
        gathers[1].step(2)
        gathers[0].step(3)
        gathers[1].step(3)
        gathers[0].step(4)
    cols_ref[...] = matrix(GR[(*whole, slice(None), pl.ds(NB, 128))].astype(F32))
    rows_ref[...] = cols_ref[...].T[0:16]

    @pl.loop(0, FF // C)
    def _(t):
        m = C // CH
        spread = tn(cols_ref[tile(t, m), :].astype(BF), select_ref[...])
        own = iota((128, C), 0) == 9 + iota((128, C), 1) % CH
        bup_ref[0:1, tile(t, C)] = column_sum(jnp.where(own, spread, 0.0))

    if comm:
        gathers[1].step(4)

    @pl.loop(0, D // C)
    def _(n):
        for m in range(1, D // C):
            if comm:
                @pl.when(n == m)
                def _():
                    gathers[nA + m].step(4)
        cols = tile(n, C)
        weight = lambda i: matrix(GA[(n, *whole, slice(None), pl.ds(i * C, C))])
        relT = matrix(GR[(*whole, slice(None), pl.ds(0, NB))])
        wq, wk, wv = weight(0), weight(1), weight(2)
        q_ref[:, cols] = (nn(x_ref[...], wq) + rows_ref[0:1, cols]).astype(BF)
        k = (nn(x_ref[...], wk) + rows_ref[1:2, cols]).astype(BF)
        v = (nn(x_ref[...], wv) + rows_ref[2:3, cols]).astype(BF)
        k_ref[:, cols] = k
        v_ref[:, cols] = v
        for src, dst in ((k, kf_ref), (v, vf_ref)):
            dst[0:B, cols] = nn(flip_ref[...], src[B:T]).astype(BF)
            dst[B:T, cols] = nn(flip_ref[...], src[0:B]).astype(BF)
        rk = (tn(wk, relT) + cols_ref[cols, 1:2]).astype(BF)
        rq = (tn(wq, relT) + cols_ref[cols, 0:1]).astype(BF)
        kprT_ref[cols, :] = nn(rk, act_ref[:, 0:2 * T]).astype(BF)
        kpsT_ref[cols, :] = nn(rk, pick_ref[...]).astype(BF)
        qpsT_ref[cols, :] = nn(rq, pick_ref[...]).astype(BF)
        for m in range(D // C):
            if comm:
                @pl.when(n == m)
                def _():
                    gather_tick(3 * m)

        @pl.loop(0, 2)
        def _(i):
            pair_forward(2 * n + i, q_ref, k_ref, v_ref, kprT_ref, qpsT_ref, mask_ref, flip_ref, ctx_ref, pT_ref, scale)
            for m in range(2 * D // C):
                if comm:
                    @pl.when(2 * n + i == m)
                    def _():
                        gather_tick(3 * (m // 2) + 1 + m % 2)

    if comm:
        gathers[nO].step(4)
    second_ref = gtok_ref

    @pl.loop(0, D // C)
    def _(n):
        cols = tile(n, C)
        w = matrix(GO[(*whole, slice(None), cols)])
        second_ref[:, cols] = x_ref[:, cols].astype(F32) + (nn(ctx_ref[...], w) + rows_ref[3:4, cols])

    gather_tick(9)

    @pl.loop(0, T // R)
    def _(r):
        rs = tile(r, R)
        n1, inv1 = norm_rows(second_ref[rs, :])
        n1_ref[rs, :] = n1
        inv1_ref[rs, :] = jnp.broadcast_to(inv1, (R, 128))
        nb_ref[rs, :] = (n1 * row(4) + row(5)).astype(BF)

    gather_tick(10)

    @pl.loop(0, CH)
    def _(k):
        for m in range(CH):
            if comm:
                @pl.when(k == m)
                def _():
                    gathers[nU + m].step(4)
                    if m > 0:
                        gather_tick(10 + m)

        @pl.loop(0, D // C)
        def _(j):
            w = matrix(GU[(k, *whole, slice(None), tile(j, C))])
            cols = tile(k * (D // C) + j, C)
            up = nn(nb_ref[...], w) + bup_ref[0:1, cols]
            phi, e = normal_cdf_pair(up)
            act_ref[:, cols] = (up * phi).astype(BF)
            gp_ref[:, cols] = (phi + up * e * 0.3989422804014327).astype(BF)

    if comm:
        gather_tick(14)
        for k in range(CH):
            gathers[nD + k].step(4)

    @pl.loop(0, D // C)
    def _(n):
        cols = tile(n, C)
        w = matrix(GD[(*whole, slice(None), slice(None), cols)])
        normed = n1_ref[:, cols] * rows_ref[4:5, cols] + rows_ref[5:6, cols]
        second_ref[:, cols] = normed + (nn(act_ref[...], w) + rows_ref[6:7, cols])

    @pl.loop(0, T // R)
    def _(r):
        rs = tile(r, R)
        live = jnp.where(iota((R, 1), 0) + r * R < length, 1.0, 0.0)
        n2, inv2 = norm_rows(second_ref[rs, :])
        out_ref[rs, :] = ((n2 * row(7) + row(8)) * live).astype(BF)
        start = cot_ref[rs, :].astype(F32) * live
        g = norm_back(start * row(7), n2, inv2)
        second_ref[rs, :] = g
        gd = g.astype(BF)
        gd_ref[rs, :] = gd
        small_ref[6:7, :] += column_sum(gd.astype(F32))
        small_ref[7:8, :] += column_sum(start * n2)
        small_ref[8:9, :] += column_sum(start)

    half = GRID[1] // 2

    @pl.loop(0, CH)
    def _(k):
        units = tile(k, D)
        c, z0 = lax.div(k, 2), half * lax.rem(k, 2)
        w = matrix(GD[c, pl.ds(z0, half)])
        gu = (nt(gd_ref[...], w) * gp_ref[:, units].astype(F32)).astype(BF)
        gp_ref[:, units] = gu
        gbup_ref[0:1, units] = column_sum(gu.astype(F32))

        @pl.loop(0, half)
        def _(i):
            at = pl.ds(pl.multiple_of(k * D + i * (D // 2), D // 2), D // 2)
            g = tn(act_ref[:, at], gd_ref[...])
            GD[c, z0 + i] = g.reshape(*GD.shape[2:]).astype(BF)

        second_ref[...] += nt(gu, matrix(GU[k]))

        @pl.loop(0, GRID[0])
        def _(i):
            g = tn(nb_ref[:, tile(i, D // 2)], gp_ref[:, units])
            GU[k, i] = g.reshape(*GU.shape[2:]).astype(BF)

        for m in range(CH):
            if comm:
                @pl.when(k == m)
                def _():
                    scatter_tick(m)

    scatter_tick(CH)

    @pl.loop(0, T // R)
    def _(r):
        rs = tile(r, R)
        g = second_ref[rs, :]
        n1 = n1_ref[rs, :]
        gm = norm_back(g * row(4), n1, inv1_ref[rs, 0:1])
        second_ref[rs, :] = gm
        ga = gm.astype(BF)
        gd_ref[rs, :] = ga
        small_ref[3:4, :] += column_sum(ga.astype(F32))
        small_ref[4:5, :] += column_sum(g * n1)
        small_ref[5:6, :] += column_sum(g)

    @pl.loop(0, GRID[0])
    def _(i):
        at = tile(i, D // 2)
        dcT_ref[at, :] = nt(matrix(GO[i]), gd_ref[...]).astype(BF)
        g = tn(ctx_ref[:, at], gd_ref[...])
        GO[i] = g.reshape(*GO.shape[1:]).astype(BF)

    scatter_tick(CH + 1)

    grkT, grqT = kprT_ref.at[:, 0:NB], kprT_ref.at[:, NB:2 * NB]

    @pl.loop(0, D // C)
    def _(n):
        cols = tile(n, C)

        @pl.loop(0, 2)
        def _(i):
            pair_backward(2 * n + i, q_ref, kf_ref, vf_ref, kpsT_ref, qpsT_ref, dcT_ref, pT_ref, scale)
            for m in range(2 * D // C):
                if comm:
                    @pl.when(2 * n + i == m)
                    def _():
                        scatter_tick(CH + 2 + 3 * (m // 2) + m % 2)

        dq = q_ref[:, cols]
        for src, dst in ((kf_ref, k_ref), (vf_ref, v_ref)):
            dst[0:B, cols] = nn(flip_ref[...], src[B:T, cols]).astype(BF)
            dst[B:T, cols] = nn(flip_ref[...], src[0:B, cols]).astype(BF)
        dk, dv = k_ref[:, cols], v_ref[:, cols]
        grk = nt(kpsT_ref[cols, :], pick_ref[...]).astype(BF)
        grq = nt(qpsT_ref[cols, :], pick_ref[...]).astype(BF)
        weight = lambda i: matrix(GA[(n, *whole, slice(None), pl.ds(i * C, C))])
        wq, wk = weight(0), weight(1)
        gtok_ref[...] += nt(dq, wq) + nt(dk, wk) + nt(dv, weight(2))
        grel_ref[...] += nn(wk, grk) + nn(wq, grq)
        ones_t, ones_b = jnp.ones((8, T), BF), jnp.ones((8, NB), BF)
        small_ref[0:1, cols] = (nn(ones_t, dq) + nt(ones_b, grq))[0:1]
        small_ref[1:2, cols] = (nn(ones_t, dk) + nt(ones_b, grk))[0:1]
        small_ref[2:3, cols] = nn(ones_t, dv)[0:1]

        @pl.loop(0, GRID[0])
        def _(i):
            at = tile(i, D // 2)
            xt = x_ref[:, at]
            relT = matrix(GR[(i, *whole[1:], slice(None), pl.ds(0, NB))])
            for s, g in enumerate((tn(xt, dq) + nt(relT, grq), tn(xt, dk) + nt(relT, grk), tn(xt, dv))):
                GA[(n, i, *whole[1:], slice(None), pl.ds(s * C, C))] = g.reshape(*GA.shape[2:6], C).astype(BF)

        for m in range(D // C):
            if comm:
                @pl.when(n == m)
                def _():
                    scatter_tick(CH + 2 + 3 * m + 2)

    small_ref[9:16, :] = jnp.zeros((7, D), F32)
    cols_ref[...] = jnp.concatenate([small_ref[...], jnp.zeros((112, D), F32)], axis=0).T

    @pl.loop(0, FF // C)
    def _(t):
        m = C // CH
        own = iota((128, C), 0) == 9 + iota((128, C), 1) % CH
        g = jnp.where(own, gbup_ref[0:1, tile(t, C)], 0.0).astype(BF)
        cols_ref[tile(t, m), :] += nt(select_ref[...], g)

    GR[(*whole, slice(None), pl.ds(0, NB))] = grel_ref[...].reshape(*GR.shape[:5], NB).astype(BF)
    GR[(*whole, slice(None), pl.ds(NB, 128))] = cols_ref[...].reshape(*GR.shape[:5], 128).astype(BF)
    if comm:
        for t in range(starts[-1], starts[-1] + 5):
            scatter_tick(t)
    else:
        GRh, GAh, GOh, GUh, GDh = rest[5:10]
        stores = [pltpu.make_async_copy(src, dst, sems.at[i]) for i, (dst, src) in enumerate(zip((GRh, GAh, GOh, GUh, GDh), (GR, GA, GO, GU, GD)))]
        for copy in stores:
            copy.start()
        for copy in stores:
            copy.wait()


def layer_scratch(T, D, FF, NB, heads):
    V = pltpu.VMEM
    n, ch = D // 256, FF // D
    rows = D // BLOCKS
    td = V((T, D), BF)
    return [
        V((*GRID, rows, NB + 128), BF), V((n, *GRID, rows, D), BF), V((*GRID, rows, D), BF), V((ch, *GRID, rows, D), BF), V((*GRID, ch, rows, D), BF),
        td, td, td, td, td, V((D, 2 * T), BF), V((D, 2 * T), BF), V((D, 2 * T), BF), V((NB, 2 * T), BF), V((heads, T, T), BF),
        td, V((D, T), BF), V((T, D), F32), V((T, 128), F32), td, td, V((T, FF), BF), V((T, FF), BF),
        V((D, NB), F32), V((D, 128), F32), V((16, D), F32), V((8, FF), F32), V((16, D), F32), V((8, FF), F32), V((8, T), F32),
        V((T // 2, T // 2), BF), V((256 // ch, 256), BF),
    ]


def call_layer(comm, length, idx, x, cot, parts):
    T, D = x.shape
    S = jax.ShapeDtypeStruct
    VM, HBM = pl.BlockSpec(memory_space=pltpu.VMEM), pl.BlockSpec(memory_space=pl.ANY)
    heads = D // HEAD
    if comm:
        rshard, wq, wk, wv, wo, wup, wdown = parts
        rows, FF = wup.shape
        NB = rshard.shape[1] - 128
        outs = [S((T, D), BF), S((T, D), F32), S(rshard.shape, F32)] + [S((rows, D), F32)] * 4 + [S(wup.shape, F32), S(wdown.shape, F32)]
        in_specs = [pl.BlockSpec(memory_space=pltpu.SMEM)] + [VM] * (3 + len(parts))
        out_specs = [VM] * len(outs)
        nz, last = GRID[1], 2 + D // 256 + 2 * (FF // D)
        V = pltpu.VMEM
        sems = [pltpu.SemaphoreType.DMA((last, 8))] * 4 + [pltpu.SemaphoreType.REGULAR]
        extra = [V((SLOTS, nz, 2, 2, rows, D), BF), V((last, nz, 2, rows, CUT), BF), V((last, nz, 2, rows, D - CUT), BF),
                 V((last, nz, rows, CUT), BF), V((last, nz, rows, D - CUT), BF), V((last, nz - 1, rows, D), BF)] + sems

        def kernel(*refs):
            layer_kernel(True, *refs)
    else:
        gr, ga, go, gu, gd = parts
        FF, NB = gu.shape[0] * D, gr.shape[-1] - 128
        outs = [S((T, D), BF), S((T, D), F32)] + [S(p.shape, p.dtype) for p in parts]
        in_specs = [pl.BlockSpec(memory_space=pltpu.SMEM)] + [VM] * 3 + [HBM] * 5
        out_specs = [VM] * 2 + [HBM] * 5
        extra = [pltpu.SemaphoreType.DMA((5,))]

        def kernel(*refs):
            ins, given, results, stored, scratch = refs[:4], refs[4:9], refs[9:11], refs[11:16], refs[16:]
            none = [None] * 7
            layer_kernel(False, *ins, *none, *results, *none, *scratch[:-1], *given, *stored, scratch[-1])

    return pl.pallas_call(
        kernel,
        out_shape=outs,
        in_specs=in_specs,
        out_specs=out_specs,
        scratch_shapes=layer_scratch(T, D, FF, NB, heads) + extra,
        compiler_params=pltpu.CompilerParams(
            vmem_limit_bytes=VMEM_LIMIT,
            **(dict(collective_id=0, has_side_effects=True) if comm else {}),
        ),
    )(length, idx, x, cot, *parts)


VMEM_LIMIT = 63 * 2**20


def body(comm, tokens, lengths, rel_index, w_query, b_query, w_key, b_key, w_value, b_value, w_out, b_out, rel_table,
         gain_one, shift_one, w_up, b_up, w_down, b_down, gain_two, shift_two, cotangent):
    rows, D = w_query.shape
    T = tokens.shape[0]
    NB = rel_table.shape[0]
    FF = w_up.shape[1]
    ch, n = FF // D, D // 256
    vectors = (b_query, b_key, b_value, b_out, gain_one, shift_one, b_down, gain_two, shift_two)
    pack = jnp.concatenate([rel_table.T, jnp.stack(vectors, axis=1), b_up.reshape(rows, ch), jnp.zeros((rows, 128 - 9 - ch), BF)], axis=1)
    shifted = jnp.concatenate([rel_index[1:], jnp.full((1,), -1, jnp.int32)])
    idx = jnp.concatenate([rel_index[None, ::-1], shifted[None, :], jnp.zeros((6, 2 * T), jnp.int32)])
    if comm:
        out, gtok, gr, gq, gk, gv, go, gup, gdown = call_layer(
            True, lengths, idx, tokens, cotangent, (pack, w_query, w_key, w_value, w_out, w_up, w_down.reshape(ch, rows, D)))
        gdown = gdown.reshape(w_down.shape)
    else:
        gather = lambda w: lax.all_gather(w, AXES, axis=0, tiled=True)
        r = D // BLOCKS
        attend = gather(jnp.concatenate([pack, w_out, w_query, w_key, w_value], axis=1))
        gr, go = attend[:, :NB + 128].reshape(*GRID, r, NB + 128), attend[:, NB + 128:NB + 128 + D].reshape(*GRID, r, D)
        qkv = attend[:, NB + 128 + D:].reshape(*GRID, r, 3, n, 256)
        ga = qkv.transpose(6, 0, 1, 2, 3, 4, 5, 7).reshape(n, *GRID, r, D)
        gu = gather(w_up).reshape(*GRID, r, ch, D).transpose(5, 0, 1, 2, 3, 4, 6)
        gd = gather(w_down).reshape(*GRID, ch, r, D)
        out, gtok, gr, ga, go, gu, gd = call_layer(False, lengths, idx, tokens, cotangent, (gr, ga, go, gu, gd))
        scatter = lambda g: lax.psum_scatter(g.astype(F32), AXES, scatter_dimension=0, tiled=True)
        ga = ga.reshape(n, *GRID, r, 3, 256).transpose(1, 2, 3, 4, 5, 6, 0, 7).reshape(D, 3 * D)
        gup = scatter(gu.transpose(1, 2, 3, 4, 5, 0, 6).reshape(D, FF))
        gdown = scatter(gd.reshape(FF, D))
        attend = scatter(jnp.concatenate([gr.reshape(D, NB + 128), go.reshape(D, D), ga], axis=1))
        gr = attend[:, :NB + 128]
        go, gq, gk, gv = (attend[:, NB + 128 + i * D:NB + 128 + (i + 1) * D] for i in range(4))
    grel = gr[:, :NB].T
    vec = lambda i: gr[:, NB + i]
    return (out, gtok, gq, vec(0), gk, vec(1), gv, vec(2), go, vec(3), grel, vec(4), vec(5),
            gup, gr[:, NB + 9:NB + 9 + ch].reshape(rows * ch), gdown, vec(6), vec(7), vec(8))


def solution(mesh):
    rows, vec = P(AXES, None), P(AXES)
    comm = mesh.shape["dp"] == GRID[0] and mesh.shape["fsdp"] == GRID[1] * GRID[2] * GRID[3]

    def step(*args):
        return body(comm, *args)

    return jax.shard_map(
        step,
        mesh=mesh,
        in_specs=(rows, vec, P(), rows, vec, rows, vec, rows, vec, rows, vec, P(None, AXES), vec, vec, rows, vec, rows, vec, vec, vec, rows),
        out_specs=(rows, rows, rows, vec, rows, vec, rows, vec, rows, vec, P(None, AXES), vec, vec, rows, vec, rows, vec, vec, vec),
        check_vma=False,
    )
```

```python
import jax
import jax.numpy as jnp
from jax import lax
from jax.experimental import pallas as pl
from jax.experimental.pallas import tpu as pltpu
from jax.sharding import PartitionSpec as P

BF = jnp.bfloat16
F32 = jnp.float32
EPS = 1e-6
HEAD = 64
AXES = ("dp", "fsdp")
MESH = pl.DeviceIdType.MESH
LOG2E = 1.4426950408889634
GRID = (2, 4, 2, 2)
BLOCKS = 32
SLOTS = 3


def dot(left, right, dims):
    return lax.dot_general(left, right, ((dims[:1], dims[1:]), ((), ())), preferred_element_type=F32)


def nn(left, right):
    return dot(left, right, (1, 0))


def nt(left, right):
    return dot(left, right, (1, 1))


def tn(left, right):
    return dot(left, right, (0, 0))


def iota(shape, axis):
    return lax.broadcasted_iota(jnp.int32, shape, axis)


def column_sum(x):
    return jnp.sum(x, axis=0, keepdims=True)


def row_mean(x):
    return jnp.sum(x, axis=1, keepdims=True) * (1.0 / x.shape[1])


def norm_rows(x):
    centred = x - row_mean(x)
    inv = lax.rsqrt(row_mean(centred * centred) + EPS)
    return centred * inv, inv


def norm_back(g, n, inv):
    return (g - row_mean(g) - n * row_mean(g * n)) * inv


def normal_cdf_pair(x):
    a = jnp.abs(x)
    e = jnp.exp2(x * x * (-0.5 * LOG2E))
    t = 1.0 / (1.0 + (0.3275911 * 0.7071067811865476) * a)
    poly = ((((1.061405429 * t - 1.453152027) * t + 1.421413741) * t - 0.284496736) * t + 0.254829592) * t
    tail = 0.5 * poly * e
    return jnp.where(x < 0, tail, 1.0 - tail), e


def tile(n, size):
    return pl.ds(pl.multiple_of(n * size, size), size)


def matrix(value):
    rows = 1
    for size in value.shape[:-1]:
        rows *= size
    return value.reshape(rows, value.shape[-1])


def pair_forward(pair, q_ref, k_ref, v_ref, kprT_ref, qpsT_ref, mask_ref, flip_ref, ctx_ref, pT_ref, scale):
    T = q_ref.shape[0]
    B = T // 2
    lanes = tile(pair, 128)
    outs = []
    for hh in range(2):
        keep = iota((1, 128), 1) // HEAD == hh
        qh = jnp.where(keep, q_ref[:, lanes], 0)
        kh = jnp.where(keep, k_ref[:, lanes], 0)
        content = nt(qh, k_ref[:, lanes])
        to, frm = [], []
        for b in range(2):
            u0 = B * (1 - b)
            t = nn(qh[b * B:(b + 1) * B], kprT_ref[lanes, u0:u0 + 3 * B])
            to.append(pltpu.roll(t, 2 * B + 1, 1, stride=1, stride_axis=0)[:, :T])
            f = nn(kh[b * B:(b + 1) * B], qpsT_ref[lanes, u0:u0 + 3 * B])
            frm.append(pltpu.roll(f, 2 * B + 1, 1, stride=1, stride_axis=0)[:, :T].T)
        s = content + jnp.concatenate(to, axis=0) + jnp.concatenate(frm, axis=1) + mask_ref[0:1, :]
        top = jnp.max(s, axis=1, keepdims=True)
        e = jnp.exp2((s - top) * (scale * LOG2E))
        p = (e * (1.0 / jnp.sum(e, axis=1, keepdims=True))).astype(BF)
        outs.append(nn(p, v_ref[:, lanes]))
        pT_ref[2 * pair + hh, 0:B, :] = nt(flip_ref[...], p[:, B:T]).astype(BF)
        pT_ref[2 * pair + hh, B:T, :] = nt(flip_ref[...], p[:, 0:B]).astype(BF)
    ctx_ref[:, lanes] = jnp.where(iota((1, 128), 1) < HEAD, outs[0], outs[1]).astype(BF)


def pair_backward(pair, q_ref, kf_ref, vf_ref, kpsT_ref, qpsT_ref, dcT_ref, pT_ref, scale):
    T = q_ref.shape[0]
    B = T // 2
    lanes = tile(pair, 128)
    low = iota((1, 128), 1) < HEAD
    q, kf, dcT = q_ref[:, lanes], kf_ref[:, lanes], dcT_ref[lanes, :]
    dqs, dks, dvs, gks, gqs = [], [], [], [], []
    for hh in range(2):
        vh = jnp.where(iota((1, 128), 1) // HEAD == hh, vf_ref[:, lanes], 0)
        pT = pT_ref[2 * pair + hh]
        dpT = nn(vh, dcT)
        wide = pT.astype(F32)
        prod = wide * dpT
        inner = column_sum(prod) / column_sum(wide)
        dsT = (prod - wide * inner).astype(BF)
        ds = dsT.T
        zero = jnp.zeros((B, B), BF)
        dk, dq, gq, gk = [], [], [], []
        for b in range(2):
            rows, span = slice(b * B, (b + 1) * B), slice(b * B, b * B + 3 * B)
            gf = pltpu.roll(jnp.concatenate([dsT[rows], zero], axis=1), 0, 1, stride=1, stride_axis=0)
            dk.append(nn(dsT[rows], q) + nt(gf, qpsT_ref[lanes, span]))
            gq.append(tn(kf[rows], gf)[hh * HEAD:(hh + 1) * HEAD])
            gt = pltpu.roll(jnp.concatenate([ds[rows], zero], axis=1), 0, 1, stride=1, stride_axis=0)
            dq.append(nn(ds[rows], kf) + nt(gt, kpsT_ref[lanes, span]))
            gk.append(tn(q[rows], gt)[hh * HEAD:(hh + 1) * HEAD])
        dks.append(jnp.concatenate(dk, axis=0))
        dqs.append(jnp.concatenate(dq, axis=0))
        dvs.append(nt(pT, dcT))
        gqs.append(gq)
        gks.append(gk)
    for ref, pieces in ((qpsT_ref, gqs), (kpsT_ref, gks)):
        for hh in range(2):
            g = pieces[hh]
            rows = pl.ds(pl.multiple_of(pair * 128 + HEAD * hh, HEAD), HEAD)
            ref[rows, 0:B] = (scale * g[0][:, 0:B]).astype(BF)
            ref[rows, B:3 * B] = (scale * (g[0][:, B:] + g[1][:, 0:2 * B])).astype(BF)
            ref[rows, 3 * B:] = (scale * g[1][:, 2 * B:]).astype(BF)
    q_ref[:, lanes] = (scale * jnp.where(low, dqs[0], dqs[1])).astype(BF)
    kf_ref[:, lanes] = (scale * jnp.where(low, dks[0], dks[1])).astype(BF)
    vf_ref[:, lanes] = jnp.where(low, dvs[0], dvs[1]).astype(BF)


class Place:
    def __init__(self):
        self.nz = GRID[1]
        self.c = lax.axis_index("dp")
        f = lax.axis_index("fsdp")
        self.x = lax.rem(f, 2)
        self.y = lax.rem(lax.div(f, 2), 2)
        self.z = lax.div(f, 4)
        self.nx = 1 - self.x
        self.ny = 1 - self.y

    def at(self, c=None, z=None, y=None, x=None):
        c = self.c if c is None else c
        z = self.z if z is None else z
        y = self.y if y is None else y
        x = self.x if x is None else x
        return (c, (z * 2 + y) * 2 + x)

    def zs(self):
        return [lax.rem(self.z + d, self.nz) for d in range(1, self.nz)]

    def barrier(self):
        sem = pltpu.get_barrier_semaphore()
        peers = [self.at(z=z) for z in self.zs()] + [self.at(x=self.nx), self.at(y=self.ny), self.at(c=1 - self.c)]
        for peer in peers:
            pl.semaphore_signal(sem, inc=1, device_id=peer, device_id_type=MESH)
        pl.semaphore_wait(sem, len(peers))


def remote(src, dst, send, recv, to):
    return pltpu.make_async_remote_copy(src_ref=src, dst_ref=dst, send_sem=send, recv_sem=recv, device_id=to, device_id_type=MESH)


class Part:
    def __init__(self, place, piece, lo, cols):
        cut = cols // 256 * 128
        self.p, self.piece, self.lo, self.cols, self.cut = place, piece, lo, cols, cut
        self.all, self.h1, self.h2 = pl.ds(lo, cols), pl.ds(lo, cut), pl.ds(lo + cut, cols - cut)


class Gather(Part):
    def __init__(self, place, piece, lo, cols, early, send, recv):
        super().__init__(place, piece, lo, cols)
        self.early, self.send, self.recv = early, send, recv

    def copies(self, k):
        p, g, every = self.p, self.piece, slice(None)
        if k == 0 and self.early:
            return [(g(p.c, p.z, p.y, p.x, self.h1), p.at(x=p.nx)), (g(p.c, p.z, p.y, p.x, self.h2), p.at(y=p.ny))]
        if k == 1 and self.early:
            return ([(g(p.c, p.z, p.y, every, self.h1), p.at(z=z)) for z in p.zs()]
                    + [(g(p.c, p.z, every, p.x, self.h2), p.at(z=z)) for z in p.zs()])
        if k == 0:
            return [(g(p.c, p.z, p.y, p.x, self.all), p.at(z=z)) for z in p.zs()]
        if k == 1:
            return [(g(p.c, every, p.y, p.x, self.h1), p.at(x=p.nx)), (g(p.c, every, p.y, p.x, self.h2), p.at(y=p.ny))]
        if k == 2:
            return [(g(p.c, every, p.y, every, self.h1), p.at(y=p.ny)), (g(p.c, every, every, p.x, self.h2), p.at(x=p.nx))]
        return [(g(p.c, every, every, every, self.all), p.at(c=1 - p.c))]

    def settle(self, k):
        p, g, every = self.p, self.piece, slice(None)
        three = pl.ds(0, p.nz - 1)
        if k == 0:
            ref = g(p.c, p.z, p.y, p.x, self.all) if self.early else g(p.c, three, p.y, p.x, self.all)
        elif k == 1:
            ref = g(p.c, three, p.y, every, self.all) if self.early else g(p.c, every, p.y, p.x, self.all)
        elif k == 2:
            ref = g(p.c, every, p.y, every, self.all)
        else:
            ref = g(p.c, every, every, every, self.all)
        copy = remote(ref, ref, self.send.at[0], self.recv.at[k], p.at(c=1 - p.c))
        copy.wait_recv()
        copy.wait_send()

    def step(self, k):
        if k > 0:
            self.settle(k - 1)
        if k < 4:
            for ref, to in self.copies(k):
                remote(ref, ref, self.send.at[0], self.recv.at[k], to).start()


def add_into(ref, *others):
    total = ref[...].astype(F32)
    for other in others:
        total = total + other[...].astype(F32)
    ref[...] = total.astype(BF)


class Scatter(Part):
    def __init__(self, place, piece, lo, cols, late, order, last, slots, buffers, send, recv, credit, finish):
        super().__init__(place, piece, lo, cols)
        self.late, self.order, self.last, self.send, self.recv, self.credit, self.finish = late, order, last, send, recv, credit, finish
        self.rd = slots.at[order % SLOTS, :, :, :, :, pl.ds(0, cols)]
        self.ry, self.rx, self.third, self.fourth = buffers[0], buffers[1], buffers[2:4], buffers[4:]

    def make(self, k):
        p, g, every = self.p, self.piece, slice(None)
        if k == 0:
            found = [(g(1 - p.c, every, every, every, self.all), self.rd, p.at(c=1 - p.c))]
        elif k == 1:
            found = [(g(p.c, every, p.ny, every, self.h1), self.ry, p.at(y=p.ny)),
                     (g(p.c, every, every, p.nx, self.h2), self.rx, p.at(x=p.nx))]
        elif self.late and k == 2:
            found = []
            for d, z in enumerate(p.zs()):
                found += [(g(p.c, z, p.y, every, self.h1), self.third[0].at[d], p.at(z=z)),
                          (g(p.c, z, every, p.x, self.h2), self.third[1].at[d], p.at(z=z))]
        elif self.late:
            found = [(g(p.c, p.z, p.y, p.nx, self.h1), self.fourth[0], p.at(x=p.nx)),
                     (g(p.c, p.z, p.ny, p.x, self.h2), self.fourth[1], p.at(y=p.ny))]
        elif k == 2:
            found = [(g(p.c, every, p.y, p.nx, self.h1), self.third[0], p.at(x=p.nx)),
                     (g(p.c, every, p.ny, p.x, self.h2), self.third[1], p.at(y=p.ny))]
        else:
            found = [(g(p.c, z, p.y, p.x, self.all), self.fourth[0].at[d], p.at(z=z)) for d, z in enumerate(p.zs())]
        return [remote(src, dst, self.send.at[0], self.recv.at[k], to) for src, dst, to in found]

    def settle(self, k):
        p, g, every = self.p, self.piece, slice(None)
        if k == 0:
            ref = self.rd
        elif k == 1:
            ref = g(p.c, every, p.y, every, self.all)
        elif k == 2:
            ref = g(p.c, pl.ds(0, p.nz - 1), p.y, every, self.all) if self.late else g(p.c, every, p.y, p.x, self.all)
        else:
            ref = g(p.c, p.z, p.y, p.x, self.all) if self.late else self.fourth[0]
        copy = remote(ref, ref, self.send.at[0], self.recv.at[k], p.at(c=1 - p.c))
        copy.wait_recv()
        copy.wait_send()

    def step(self, k):
        p, g, every = self.p, self.piece, slice(None)
        if k > 0:
            self.settle(k - 1)
        if k == 0 and self.order >= SLOTS:
            pl.semaphore_wait(self.credit, 1)
        if k == 1:
            @pl.loop(0, p.nz)
            def _(z):
                add_into(g(p.c, z, every, every, self.all), self.rd.at[z])
            if self.order + SLOTS < self.last:
                pl.semaphore_signal(self.credit, inc=1, device_id=p.at(c=1 - p.c), device_id_type=MESH)
        elif k == 2:
            @pl.loop(0, p.nz)
            def _(z):
                add_into(g(p.c, z, p.y, every, self.h1), self.ry.at[z])
                add_into(g(p.c, z, every, p.x, self.h2), self.rx.at[z])
        elif k == 3 and self.late:
            add_into(g(p.c, p.z, p.y, every, self.h1), *[self.third[0].at[d] for d in range(p.nz - 1)])
            add_into(g(p.c, p.z, every, p.x, self.h2), *[self.third[1].at[d] for d in range(p.nz - 1)])
        elif k == 3:
            add_into(g(p.c, every, p.y, p.x, self.h1), self.third[0])
            add_into(g(p.c, every, p.y, p.x, self.h2), self.third[1])
        elif k == 4 and self.late:
            self.finish(self.lo, g(p.c, p.z, p.y, p.x, self.h1)[...].astype(F32) + self.fourth[0][...].astype(F32))
            self.finish(self.lo + self.cut, g(p.c, p.z, p.y, p.x, self.h2)[...].astype(F32) + self.fourth[1][...].astype(F32))
        elif k == 4:
            total = g(p.c, p.z, p.y, p.x, self.all)[...].astype(F32)
            for d in range(p.nz - 1):
                total = total + self.fourth[0][d].astype(F32)
            self.finish(self.lo, total)
        if k < 4:
            for copy in self.make(k):
                copy.start()


def scatter_buffers(rows, cols, late):
    nz = GRID[1]
    h1 = cols // 256 * 128
    h2 = cols - h1
    shapes = [(nz, 2, rows, h1), (nz, 2, rows, h2)]
    shapes += [(nz - 1, 2, rows, h1), (nz - 1, 2, rows, h2), (rows, h1), (rows, h2)] if late else [(nz, rows, h1), (nz, rows, h2), (nz - 1, rows, cols)]
    return [pltpu.VMEM(shape, BF) for shape in shapes]


GATHERS = (
    (0, 0, 256, 0),
    (0, 256, 384, 0),
    (1, 0, 256, 0),
    (1, 256, 256, 0),
    (1, 512, 256, 0),
    (2, 0, 768, 0),
    (3, 0, 768, 0),
    (4, 0, 768, 0),
    (5, 0, 768, 1),
    (6, 0, 768, 0),
    (7, 0, 768, 0),
    (8, 0, 768, 1),
    (9, 0, 768, 0),
    (10, 0, 768, 0),
    (11, 0, 768, 1),
    (12, 0, 768, 1),
)
SCATTERS = (
    (5, 0, 768, 0),
    (6, 0, 768, 1),
    (7, 0, 768, 0),
    (8, 0, 768, 0),
    (9, 0, 768, 1),
    (10, 0, 768, 1),
    (11, 0, 768, 0),
    (12, 0, 768, 0),
    (4, 0, 768, 0),
    (1, 0, 768, 0),
    (2, 0, 768, 0),
    (0, 0, 256, 0),
    (0, 256, 384, 1),
    (3, 512, 256, 0),
    (3, 256, 256, 0),
    (3, 0, 256, 0),
)
TICKS = {
    "pre": ((0, 0, 0), (0, 1, 0), (0, 2, 0), (0, 3, 0), (0, 4, 0), (0, 5, 0), (0, 6, 0),),
    "before P0": ((0, 0, 1), (0, 1, 1), (0, 2, 1), (0, 7, 0), (0, 0, 2), (0, 1, 2), (0, 3, 1), (0, 2, 2), (0, 4, 1), (0, 0, 3), (0, 0, 4), (0, 1, 3), (0, 3, 2), (0, 2, 3), (0, 1, 4), (0, 4, 2), (0, 5, 1), (0, 8, 0), (0, 2, 4), (0, 3, 3), (0, 4, 3), (0, 6, 1), (0, 9, 0), (0, 3, 4), (0, 4, 4),),
    "P0": ((0, 5, 2), (0, 6, 2), (0, 7, 1), (0, 8, 1), (0, 10, 0), (0, 11, 0),),
    "F0": ((0, 5, 3), (0, 9, 1), (0, 12, 0),),
    "F1": ((0, 6, 3), (0, 7, 2), (0, 8, 2), (0, 11, 1), (0, 13, 0),),
    "before P1": ((0, 5, 4),),
    "P1": ((0, 9, 2), (0, 10, 1), (0, 14, 0),),
    "F2": ((0, 7, 3), (0, 12, 1), (0, 8, 3), (0, 15, 0),),
    "F3": ((0, 9, 3), (0, 11, 2),),
    "before P2": ((0, 6, 4),),
    "P2": ((0, 10, 2), (0, 12, 2), (0, 13, 1), (0, 14, 1), (0, 15, 1),),
    "F4": ((0, 11, 3),),
    "F5": ((0, 10, 3), (0, 14, 2),),
    "before wo": ((0, 7, 4),),
    "wo": ((0, 12, 3),),
    "before U0": ((0, 8, 4),),
    "U0": ((0, 13, 2),),
    "before U1": ((0, 9, 4),),
    "U1": ((0, 14, 3), (0, 15, 2),),
    "before U2": ((0, 10, 4),),
    "before U3": ((0, 11, 4),),
    "U3": ((0, 13, 3),),
    "before down": ((0, 12, 4), (0, 14, 4), (0, 15, 3), (0, 13, 4), (0, 15, 4),),
    "b0": ((1, 0, 0),),
    "b1": ((1, 0, 1), (1, 1, 0),),
    "b2": ((1, 1, 1), (1, 0, 2), (1, 2, 0),),
    "b3": ((1, 1, 2), (1, 2, 1), (1, 3, 0), (1, 4, 0), (1, 5, 0),),
    "ln1b": ((1, 0, 3),),
    "wob": ((1, 3, 1), (1, 6, 0),),
    "B0": ((1, 2, 2), (1, 1, 3), (1, 3, 2), (1, 4, 1), (1, 5, 1), (1, 6, 1), (1, 7, 0), (1, 8, 0),),
    "B1": ((1, 0, 4), (1, 1, 4), (1, 2, 3), (1, 3, 3), (1, 7, 1), (1, 8, 1), (1, 4, 2),),
    "gw0": ((1, 2, 4), (1, 5, 2), (1, 9, 0),),
    "B2": ((1, 3, 4), (1, 6, 2), (1, 9, 1),),
    "B3": ((1, 7, 2), (1, 4, 3), (1, 8, 2),),
    "gw1": ((1, 6, 3), (1, 10, 0),),
    "B4": ((1, 4, 4), (1, 5, 3), (1, 7, 3), (1, 8, 3), (1, 9, 2), (1, 6, 4), (1, 5, 4), (1, 10, 1),),
    "B5": ((1, 7, 4), (1, 9, 3),),
    "rel2": ((1, 10, 2), (1, 11, 0), (1, 12, 0),),
    "gv2": ((1, 8, 4), (1, 13, 0),),
    "gk2": ((1, 11, 1), (1, 12, 1), (1, 10, 3), (1, 13, 1), (1, 14, 0),),
    "gq2": ((1, 9, 4), (1, 11, 2), (1, 14, 1), (1, 15, 0),),
    "end": ((1, 12, 2), (1, 15, 1), (1, 13, 2), (1, 10, 4), (1, 11, 3), (1, 14, 2), (1, 15, 2), (1, 13, 3), (1, 12, 3), (1, 14, 3), (1, 11, 4), (1, 15, 3), (1, 12, 4), (1, 13, 4), (1, 14, 4), (1, 15, 4),),
}


def layer_kernel(
    comm,
    length_ref, index_ref, x_ref, cot_ref, vec_in, rel_in, q_in, k_in, v_in, o_in, up_in, down_in,
    out_ref, gtok_ref, r_out, q_out, k_out, v_out, o_out, up_out, down_out,
    GR, GA, GO, GU, GD,
    q_ref, k_ref, v_ref, kf_ref, vf_ref, kprT_ref, kpsT_ref, qpsT_ref, pick_ref, pT_ref,
    ctx_ref, dcT_ref, n1_ref, inv1_ref, nb_ref, gd_ref, act_ref, gp_ref,
    grel_ref, cols_ref, rows_ref, bup_ref, small_ref, gbup_ref, mask_ref, flip_ref, select_ref,
    *rest,
):
    T, D = x_ref.shape
    FF = act_ref.shape[1]
    NB = pick_ref.shape[0]
    B = T // 2
    C = 256
    R = 128
    CH = FF // D
    scale = (3.0 * HEAD) ** -0.5
    length = length_ref[0]
    row = lambda k: rows_ref[k:k + 1, :]
    whole = (slice(None),) * 4
    per = D // BLOCKS

    def part(ref, *lead, trail=()):
        return lambda c, z, y, x, cols: ref.at[(*lead, c, z, y, x, *trail, slice(None), cols)]

    pieces = [part(GR)] + [part(GA, n) for n in range(D // C)] + [part(GO)]
    pieces += [part(GU, k) for k in range(CH)] + [part(GD, trail=(k,)) for k in range(CH)]
    if comm:
        slots, buffers, (ag_send, ag_recv, rs_send, rs_recv, credit) = rest[0], list(rest[1:-5]), rest[-5:]
        place = Place()
        gathers = [Gather(place, pieces[i], lo, cols, early, ag_send.at[j], ag_recv.at[j]) for j, (i, lo, cols, early) in enumerate(GATHERS)]
        nA, nO, nU, nD = 1, 1 + D // C, 2 + D // C, 2 + D // C + CH

        def finisher(i):
            def store(lo, total):
                cols = pl.ds(lo, total.shape[1])
                if i == 0:
                    r_out[:, cols] = total
                elif i < nO:
                    for b in range(0, total.shape[1], 128):
                        ref = (q_out, k_out, v_out)[(lo + b) // C]
                        ref[:, pl.ds((i - nA) * C + (lo + b) % C, 128)] = total[:, b:b + 128]
                elif i == nO:
                    o_out[:, cols] = total
                elif i < nD:
                    up_out[:, pl.ds((i - nU) * D + lo, total.shape[1])] = total
                else:
                    down_out[pl.ds((i - nD) * per, per), cols] = total
            return store

        scatters = []
        for j, (i, lo, cols, late) in enumerate(SCATTERS):
            number = 6 if late else 5
            scatters.append(Scatter(place, pieces[i], lo, cols, late, j, len(SCATTERS), slots, buffers[:number],
                                    rs_send.at[j], rs_recv.at[j], credit, finisher(i)))
            buffers = buffers[number:]

    def run(name):
        if comm:
            for kind, j, k in TICKS.get(name, ()):
                (scatters if kind else gathers)[j].step(k)

    def due(name, index, values):
        if comm:
            for m in values:
                label = f"{name}{m}"
                if label in TICKS:
                    @pl.when(index == m)
                    def _():
                        run(label)

    if comm:
        me = (place.c, place.z, place.y, place.x)
        rows_ref[...] = jnp.zeros_like(rows_ref)
        for k, ref in enumerate(vec_in[:-1]):
            rows_ref[k:k + 1, 0:per] = ref[...].astype(F32).reshape(1, per)
        last = vec_in[-1][...].astype(F32).reshape(1, CH * per)
        for k in range(CH):
            rows_ref[9 + k:10 + k, 0:per] = last[:, k * per:(k + 1) * per]
        own = jnp.concatenate([rows_ref[:, 0:128], jnp.zeros((112, 128), F32)], axis=0).T
        GR[(*me, slice(None), pl.ds(0, NB))] = rel_in[...]
        GR[(*me, slice(None), pl.ds(NB, 128))] = own[0:per].astype(BF)
        for n in range(D // C):
            cols = pl.ds(n * C, C)
            for i, ref in enumerate((q_in, k_in, v_in)):
                GA[(n, *me, slice(None), pl.ds(i * C, C))] = ref[:, cols]
        GO[me] = o_in[...]
        for k in range(CH):
            GU[(k, *me)] = up_in[:, pl.ds(k * D, D)]
            GD[(*me, k)] = down_in[k]
        place.barrier()
        run("pre")
    else:
        GRh, GAh, GOh, GUh, GDh = rest[:5]
        sems = rest[10]
        loads = [pltpu.make_async_copy(src, dst, sems.at[i]) for i, (src, dst) in enumerate(zip((GRh, GAh, GOh, GUh, GDh), (GR, GA, GO, GU, GD)))]
        for copy in loads:
            copy.start()
        for copy in loads:
            copy.wait()
    flip_ref[...] = jnp.where(iota((B, B), 0) + iota((B, B), 1) == B - 1, 1.0, 0.0).astype(BF)
    index = jnp.broadcast_to(index_ref[...].reshape(1, 2 * T), (8, 2 * T))
    high = lax.shift_right_logical(index, 4)
    parts = [v.astype(F32).astype(BF) for v in (high, index - 16 * high)]
    back = [jnp.concatenate([nn(v[:, b * B:(b + 1) * B], flip_ref[...]) for b in range(2 * T // B - 1, -1, -1)], axis=1) for v in parts]
    reverse = (back[0] * 16.0 + back[1]).astype(jnp.int32)
    shifted = jnp.where(iota((8, 2 * T), 1) == 2 * T - 1, -1, pltpu.roll(index, 2 * T - 1, 1))
    act_ref[:, 0:2 * T] = jnp.where(iota((NB, 2 * T), 0) == reverse[0:1], 1.0, 0.0).astype(BF)
    pick_ref[...] = jnp.where(iota((NB, 2 * T), 0) == shifted[0:1], 1.0, 0.0).astype(BF)
    W = 4 * per
    block = sum(jnp.where(iota((W, CH * W), 0) >= per * i, 1, 0) for i in range(1, 4))
    ublock = sum(jnp.where(iota((1, CH * W), 1) >= per * CH * i, 1, 0) for i in range(1, 4))
    uslice = sum(jnp.where(iota((1, CH * W), 1) >= per * i, 1, 0) for i in range(1, 4 * CH))
    place_in = iota((1, CH * W), 1) - per * uslice
    select_ref[...] = jnp.where((block == ublock) & (iota((W, CH * W), 0) - per * block == place_in), 1.0, 0.0).astype(BF)
    own_column = iota((128, CH * W), 0) == 9 + uslice - CH * ublock
    mask_ref[...] = jnp.where(iota((8, T), 1) < length, 0.0, -1e30)
    small_ref[...] = jnp.zeros_like(small_ref)
    grel_ref[...] = jnp.zeros_like(grel_ref)
    run("before P0")
    cols_ref[...] = matrix(GR[(*whole, slice(None), pl.ds(NB, 128))].astype(F32))
    rows_ref[...] = cols_ref[...].T[0:16]

    @pl.loop(0, D // W)
    def _(t):
        spread = tn(cols_ref[tile(t, W), :].astype(BF), select_ref[...])
        bup_ref[0:1, tile(t, CH * W)] = column_sum(jnp.where(own_column, spread, 0.0))

    @pl.loop(0, D // C)
    def _(n):
        due("before P", n, range(1, D // C))
        cols = tile(n, C)
        weight = lambda i: matrix(GA[(n, *whole, slice(None), pl.ds(i * C, C))])
        relT = matrix(GR[(*whole, slice(None), pl.ds(0, NB))])
        wq, wk, wv = weight(0), weight(1), weight(2)
        q_ref[:, cols] = (nn(x_ref[...], wq) + rows_ref[0:1, cols]).astype(BF)
        k = (nn(x_ref[...], wk) + rows_ref[1:2, cols]).astype(BF)
        v = (nn(x_ref[...], wv) + rows_ref[2:3, cols]).astype(BF)
        k_ref[:, cols] = k
        v_ref[:, cols] = v
        for src, dst in ((k, kf_ref), (v, vf_ref)):
            dst[0:B, cols] = nn(flip_ref[...], src[B:T]).astype(BF)
            dst[B:T, cols] = nn(flip_ref[...], src[0:B]).astype(BF)
        rk = (tn(wk, relT) + cols_ref[cols, 1:2]).astype(BF)
        rq = (tn(wq, relT) + cols_ref[cols, 0:1]).astype(BF)
        kprT_ref[cols, :] = nn(rk, act_ref[:, 0:2 * T]).astype(BF)
        kpsT_ref[cols, :] = nn(rk, pick_ref[...]).astype(BF)
        qpsT_ref[cols, :] = nn(rq, pick_ref[...]).astype(BF)
        due("P", n, range(D // C))

        @pl.loop(0, 2)
        def _(i):
            pair_forward(2 * n + i, q_ref, k_ref, v_ref, kprT_ref, qpsT_ref, mask_ref, flip_ref, ctx_ref, pT_ref, scale)
            due("F", 2 * n + i, range(2 * D // C))

    run("before wo")
    second_ref = gtok_ref

    @pl.loop(0, D // C)
    def _(n):
        cols = tile(n, C)
        w = matrix(GO[(*whole, slice(None), cols)])
        second_ref[:, cols] = x_ref[:, cols].astype(F32) + (nn(ctx_ref[...], w) + rows_ref[3:4, cols])

    run("wo")

    @pl.loop(0, T // R)
    def _(r):
        rs = tile(r, R)
        n1, inv1 = norm_rows(second_ref[rs, :])
        n1_ref[rs, :] = n1
        inv1_ref[rs, :] = jnp.broadcast_to(inv1, (R, 128))
        nb_ref[rs, :] = (n1 * row(4) + row(5)).astype(BF)

    run("ln1")

    @pl.loop(0, CH)
    def _(k):
        due("before U", k, range(CH))

        @pl.loop(0, D // C)
        def _(j):
            w = matrix(GU[(k, *whole, slice(None), tile(j, C))])
            cols = tile(k * (D // C) + j, C)
            up = nn(nb_ref[...], w) + bup_ref[0:1, cols]
            phi, e = normal_cdf_pair(up)
            act_ref[:, cols] = (up * phi).astype(BF)
            gp_ref[:, cols] = (phi + up * e * 0.3989422804014327).astype(BF)

        due("U", k, range(CH))

    run("before down")

    @pl.loop(0, D // C)
    def _(n):
        cols = tile(n, C)
        w = matrix(GD[(*whole, slice(None), slice(None), cols)])
        normed = n1_ref[:, cols] * rows_ref[4:5, cols] + rows_ref[5:6, cols]
        second_ref[:, cols] = normed + (nn(act_ref[...], w) + rows_ref[6:7, cols])

    run("down")

    @pl.loop(0, T // R)
    def _(r):
        rs = tile(r, R)
        live = jnp.where(iota((R, 1), 0) + r * R < length, 1.0, 0.0)
        n2, inv2 = norm_rows(second_ref[rs, :])
        out_ref[rs, :] = ((n2 * row(7) + row(8)) * live).astype(BF)
        start = cot_ref[rs, :].astype(F32) * live
        g = norm_back(start * row(7), n2, inv2)
        second_ref[rs, :] = g
        gd = g.astype(BF)
        gd_ref[rs, :] = gd
        small_ref[6:7, :] += column_sum(gd.astype(F32))
        small_ref[7:8, :] += column_sum(start * n2)
        small_ref[8:9, :] += column_sum(start)

    run("ln2")
    half = GRID[1] // 2

    @pl.loop(0, CH)
    def _(k):
        units = tile(k, D)
        c, z0 = lax.div(k, 2), half * lax.rem(k, 2)
        w = matrix(GD[c, pl.ds(z0, half)])
        gu = (nt(gd_ref[...], w) * gp_ref[:, units].astype(F32)).astype(BF)
        gp_ref[:, units] = gu
        gbup_ref[0:1, units] = column_sum(gu.astype(F32))

        @pl.loop(0, half)
        def _(i):
            at = pl.ds(pl.multiple_of(k * D + i * (D // 2), D // 2), D // 2)
            g = tn(act_ref[:, at], gd_ref[...])
            GD[c, z0 + i] = g.reshape(*GD.shape[2:]).astype(BF)

        second_ref[...] += nt(gu, matrix(GU[k]))

        @pl.loop(0, GRID[0])
        def _(i):
            g = tn(nb_ref[:, tile(i, D // 2)], gp_ref[:, units])
            GU[k, i] = g.reshape(*GU.shape[2:]).astype(BF)

        due("b", k, range(CH))

    @pl.loop(0, T // R)
    def _(r):
        rs = tile(r, R)
        g = second_ref[rs, :]
        n1 = n1_ref[rs, :]
        gm = norm_back(g * row(4), n1, inv1_ref[rs, 0:1])
        second_ref[rs, :] = gm
        ga = gm.astype(BF)
        gd_ref[rs, :] = ga
        small_ref[3:4, :] += column_sum(ga.astype(F32))
        small_ref[4:5, :] += column_sum(g * n1)
        small_ref[5:6, :] += column_sum(g)

    run("ln1b")

    @pl.loop(0, GRID[0])
    def _(i):
        at = tile(i, D // 2)
        dcT_ref[at, :] = nt(matrix(GO[i]), gd_ref[...]).astype(BF)
        g = tn(ctx_ref[:, at], gd_ref[...])
        GO[i] = g.reshape(*GO.shape[1:]).astype(BF)

    run("wob")

    kprT_ref[:, 0:NB] = matrix(GR[(*whole, slice(None), pl.ds(0, NB))])

    @pl.loop(0, D // C)
    def _(n):
        cols = tile(n, C)
        final = (D // C - 1,)

        @pl.loop(0, 2)
        def _(i):
            pair_backward(2 * n + i, q_ref, kf_ref, vf_ref, kpsT_ref, qpsT_ref, dcT_ref, pT_ref, scale)
            due("B", 2 * n + i, range(2 * D // C))

        dq = q_ref[:, cols]
        for src, dst in ((kf_ref, k_ref), (vf_ref, v_ref)):
            dst[0:B, cols] = nn(flip_ref[...], src[B:T, cols]).astype(BF)
            dst[B:T, cols] = nn(flip_ref[...], src[0:B, cols]).astype(BF)
        dk, dv = k_ref[:, cols], v_ref[:, cols]
        grk = nt(kpsT_ref[cols, :], pick_ref[...]).astype(BF)
        grq = nt(qpsT_ref[cols, :], pick_ref[...]).astype(BF)
        weight = lambda i: matrix(GA[(n, *whole, slice(None), pl.ds(i * C, C))])
        grel_ref[...] += nn(weight(1), grk) + nn(weight(0), grq)
        ones_t, ones_b = jnp.ones((8, T), BF), jnp.ones((8, NB), BF)
        small_ref[0:1, cols] = (nn(ones_t, dq) + nt(ones_b, grq))[0:1]
        small_ref[1:2, cols] = (nn(ones_t, dk) + nt(ones_b, grk))[0:1]
        small_ref[2:3, cols] = nn(ones_t, dv)[0:1]

        @pl.when(n == final[0])
        def _():
            small_ref[9:16, :] = jnp.zeros((7, D), F32)
            cols_ref[...] = jnp.concatenate([small_ref[...], jnp.zeros((112, D), F32)], axis=0).T

            @pl.loop(0, D // W)
            def _(t):
                g = jnp.where(own_column, gbup_ref[0:1, tile(t, CH * W)], 0.0).astype(BF)
                cols_ref[tile(t, W), :] += nt(select_ref[...], g)

            GR[(*whole, slice(None), pl.ds(0, NB))] = grel_ref[...].reshape(*GR.shape[:5], NB).astype(BF)
            GR[(*whole, slice(None), pl.ds(NB, 128))] = cols_ref[...].reshape(*GR.shape[:5], 128).astype(BF)

        due("rel", n, final)
        for i, name, d, gr in ((2, "gv", dv, None), (1, "gk", dk, grk), (0, "gq", dq, grq)):
            gtok_ref[...] += nt(d, weight(i))
            for half in range(GRID[0]):
                g = tn(x_ref[:, half * (D // 2):(half + 1) * (D // 2)], d)
                if gr is not None:
                    g = g + nt(kprT_ref[half * (D // 2):(half + 1) * (D // 2), 0:NB], gr)
                GA[(n, half, *whole[1:], slice(None), pl.ds(i * C, C))] = g.reshape(*GA.shape[2:6], C).astype(BF)
            due(name, n, final)
        due("gw", n, range(D // C))

    if comm:
        run("end")
    else:
        GRh, GAh, GOh, GUh, GDh = rest[5:10]
        stores = [pltpu.make_async_copy(src, dst, sems.at[i]) for i, (dst, src) in enumerate(zip((GRh, GAh, GOh, GUh, GDh), (GR, GA, GO, GU, GD)))]
        for copy in stores:
            copy.start()
        for copy in stores:
            copy.wait()


def finish_kernel(r_ref, *refs):
    n = (len(refs) - 11) // 2
    for i in range(n):
        refs[n + i][...] = refs[i][...]
    rel_out, vectors, wide = refs[2 * n], refs[2 * n + 1:2 * n + 10], refs[2 * n + 10]
    rows, NB = rel_out.shape
    rel_out[...] = r_ref[:, 0:NB]
    flat = jnp.concatenate([r_ref[:, NB:], jnp.zeros((128 - rows, 128), F32)], axis=0).T
    for k, ref in enumerate(vectors):
        ref[...] = flat[k:k + 1, 0:rows].reshape(rows)
    wide[...] = jnp.concatenate([flat[9 + k:10 + k, 0:rows] for k in range(wide.shape[0] // rows)], axis=1).reshape(wide.shape[0])


def layer_scratch(T, D, FF, NB, heads):
    V = pltpu.VMEM
    n, ch = D // 256, FF // D
    rows = D // BLOCKS
    td, r = V((T, D), BF), V((*GRID, rows, NB + 128), BF)
    return [
        r, V((n, *GRID, rows, D), BF), V((*GRID, rows, D), BF), V((ch, *GRID, rows, D), BF), V((*GRID, ch, rows, D), BF),
        td, td, td, td, td, V((D, 2 * T), BF), V((D, 2 * T), BF), V((D, 2 * T), BF), V((NB, 2 * T), BF), V((heads, T, T), BF),
        td, V((D, T), BF), V((T, D), F32), V((T, 128), F32), td, td, V((T, FF), BF), V((T, FF), BF),
        V((D, NB), F32), V((D, 128), F32), V((16, D), F32), V((8, FF), F32), V((16, D), F32), V((8, FF), F32), V((8, T), F32),
        V((T // 2, T // 2), BF), V((4 * rows, 4 * rows * ch), BF),
    ]


def call_layer(comm, length, index, x, cot, parts):
    T, D = x.shape
    S = jax.ShapeDtypeStruct
    VM, HBM, SM = (pl.BlockSpec(memory_space=space) for space in (pltpu.VMEM, pl.ANY, pltpu.SMEM))
    heads = D // HEAD
    if comm:
        vectors, rel, wq, wk, wv, wo, wup, wdown = parts
        operands = (*vectors, rel, wq, wk, wv, wo, wup, wdown)
        rows, FF = wup.shape
        NB = rel.shape[1]
        outs = [S((T, D), BF), S((T, D), F32), S((rows, NB + 128), F32)] + [S((rows, D), F32)] * 4 + [S(wup.shape, F32), S((FF // D * rows, D), F32)]
        out_specs = [VM] * len(outs)
        in_specs = [SM] + [VM] * (3 + len(operands))
        sems = [pltpu.SemaphoreType.DMA((len(parts), k)) for parts in (GATHERS, SCATTERS) for k in (1, 4)] + [pltpu.SemaphoreType.REGULAR]
        extra = [pltpu.VMEM((SLOTS, *GRID[1:], rows, D), BF)]
        for _, _, cols, late in SCATTERS:
            extra += scatter_buffers(rows, cols, late)
        extra += sems

        def kernel(*refs):
            given = 4 + len(vectors)
            layer_kernel(True, *refs[:4], refs[4:given], *refs[given:])
    else:
        gr, ga, go, gu, gd = operands = parts
        FF, NB = gu.shape[0] * D, gr.shape[-1] - 128
        outs = [S((T, D), BF), S((T, D), F32)] + [S(p.shape, p.dtype) for p in parts]
        in_specs = [SM] + [VM] * 3 + [HBM] * 5
        out_specs = [VM] * 2 + [HBM] * 5
        extra = [pltpu.SemaphoreType.DMA((5,))]

        def kernel(*refs):
            ins, given, results, stored, scratch = refs[:4], refs[4:9], refs[9:11], refs[11:16], refs[16:]
            layer_kernel(False, *ins, *[None] * 8, *results, *[None] * 7, *scratch[:-1], *given, *stored, scratch[-1])

    return pl.pallas_call(
        kernel,
        out_shape=outs,
        in_specs=in_specs,
        out_specs=out_specs,
        scratch_shapes=layer_scratch(T, D, FF, NB, heads) + extra,
        compiler_params=pltpu.CompilerParams(
            vmem_limit_bytes=VMEM_LIMIT,
            **(dict(collective_id=0, has_side_effects=True) if comm else {}),
        ),
    )(length, index, x, cot, *operands)


VMEM_LIMIT = 63 * 2**20


def body(comm, tokens, lengths, rel_index, w_query, b_query, w_key, b_key, w_value, b_value, w_out, b_out, rel_table,
         gain_one, shift_one, w_up, b_up, w_down, b_down, gain_two, shift_two, cotangent):
    rows, D = w_query.shape
    NB = rel_table.shape[0]
    FF = w_up.shape[1]
    ch, n = FF // D, D // 256
    vectors = (b_query, b_key, b_value, b_out, gain_one, shift_one, b_down, gain_two, shift_two)
    if comm:
        results = call_layer(True, lengths, rel_index, tokens, cotangent,
                             ((*vectors, b_up), rel_table.T, w_query, w_key, w_value, w_out, w_up, w_down.reshape(ch, rows, D)))
        out, gtok, gr, gq, gk, gv, go, gup, gdown = results
        S = jax.ShapeDtypeStruct
        VM = pl.BlockSpec(memory_space=pltpu.VMEM)
        moved = (out, gtok, gq, gk, gv, go, gup, gdown)
        *moved, rel, bq, bk, bv, bo, g1, s1, bd, g2, s2, bu = pl.pallas_call(
            finish_kernel,
            out_shape=[S(a.shape, a.dtype) for a in moved] + [S((rows, NB), F32)] + [S((rows,), F32)] * 9 + [S(b_up.shape, F32)],
            in_specs=[VM] * 9,
            out_specs=[VM] * 19,
            compiler_params=pltpu.CompilerParams(vmem_limit_bytes=VMEM_LIMIT),
        )(gr, *moved)
        out, gtok, gq, gk, gv, go, gup, gdown = moved
        return (out, gtok, gq, bq, gk, bk, gv, bv, go, bo, rel.T, g1, s1, gup, bu, gdown, bd, g2, s2)
    gather = lambda w: lax.all_gather(w, AXES, axis=0, tiled=True)
    scatter = lambda g: lax.psum_scatter(g.astype(F32), AXES, scatter_dimension=0, tiled=True)
    r = D // BLOCKS
    pad = jnp.zeros((rows, 128 - 9), BF)
    attend = gather(jnp.concatenate([w_out, w_query, w_key, w_value, rel_table.T, jnp.stack(vectors, axis=1), pad], axis=1))
    wide = gather(b_up).reshape(BLOCKS, ch, r).transpose(0, 2, 1).reshape(D, ch)
    gr = jnp.concatenate([attend[:, 4 * D:4 * D + NB + 9], wide, pad[0] * jnp.ones((D, 1), BF)], axis=1)[:, :NB + 128].reshape(*GRID, r, NB + 128)
    go = attend[:, :D].reshape(*GRID, r, D)
    ga = attend[:, D:4 * D].reshape(*GRID, r, 3, n, 256).transpose(6, 0, 1, 2, 3, 4, 5, 7).reshape(n, *GRID, r, D)
    gu = gather(w_up).reshape(*GRID, r, ch, D).transpose(5, 0, 1, 2, 3, 4, 6)
    gd = gather(w_down).reshape(*GRID, ch, r, D)
    out, gtok, gr, ga, go, gu, gd = call_layer(False, lengths, rel_index, tokens, cotangent, (gr, ga, go, gu, gd))
    gr = gr.reshape(D, NB + 128)
    ga = ga.reshape(n, *GRID, r, 3, 256).transpose(1, 2, 3, 4, 5, 6, 0, 7).reshape(D, 3 * D)
    wide = scatter(gr[:, NB + 9:NB + 9 + ch].reshape(BLOCKS, r, ch).transpose(0, 2, 1).reshape(FF))
    gup = scatter(gu.transpose(1, 2, 3, 4, 5, 0, 6).reshape(D, FF))
    gdown = scatter(gd.reshape(FF, D))
    attend = scatter(jnp.concatenate([go.reshape(D, D), ga, gr], axis=1))
    go, gq, gk, gv = (attend[:, i * D:(i + 1) * D] for i in range(4))
    vec = lambda i: attend[:, 4 * D + NB + i]
    return (out, gtok, gq, vec(0), gk, vec(1), gv, vec(2), go, vec(3), attend[:, 4 * D:4 * D + NB].T, vec(4), vec(5),
            gup, wide, gdown, vec(6), vec(7), vec(8))


def solution(mesh):
    rows, vec = P(AXES, None), P(AXES)
    comm = mesh.shape["dp"] == GRID[0] and mesh.shape["fsdp"] == GRID[1] * GRID[2] * GRID[3]

    def step(*args):
        return body(comm, *args)

    return jax.shard_map(
        step,
        mesh=mesh,
        in_specs=(rows, vec, P(), rows, vec, rows, vec, rows, vec, rows, vec, P(None, AXES), vec, vec, rows, vec, rows, vec, vec, vec, rows),
        out_specs=(rows, rows, rows, vec, rows, vec, rows, vec, rows, vec, P(None, AXES), vec, vec, rows, vec, rows, vec, vec, vec),
        check_vma=False,
    )
```

```python
import jax
import jax.numpy as jnp
from jax import lax
from jax.experimental import pallas as pl
from jax.experimental.pallas import tpu as pltpu
from jax.sharding import PartitionSpec as P

BF = jnp.bfloat16
F32 = jnp.float32
EPS = 1e-6
HEAD = 64
AXES = ("dp", "fsdp")
MESH = pl.DeviceIdType.MESH
LOG2E = 1.4426950408889634
GRID = (2, 2, 2, 2, 2)
BLOCKS = 32
SLOTS = 3


def dot(left, right, dims):
    return lax.dot_general(left, right, ((dims[:1], dims[1:]), ((), ())), preferred_element_type=F32)


def nn(left, right):
    return dot(left, right, (1, 0))


def nt(left, right):
    return dot(left, right, (1, 1))


def tn(left, right):
    return dot(left, right, (0, 0))


def iota(shape, axis):
    return lax.broadcasted_iota(jnp.int32, shape, axis)


def column_sum(x):
    return jnp.sum(x, axis=0, keepdims=True)


def row_mean(x):
    return jnp.sum(x, axis=1, keepdims=True) * (1.0 / x.shape[1])


def norm_rows(x):
    centred = x - row_mean(x)
    inv = lax.rsqrt(row_mean(centred * centred) + EPS)
    return centred * inv, inv


def norm_back(g, n, inv):
    return (g - row_mean(g) - n * row_mean(g * n)) * inv


def normal_cdf_pair(x):
    a = jnp.abs(x)
    e = jnp.exp2(x * x * (-0.5 * LOG2E))
    t = 1.0 / (1.0 + (0.3275911 * 0.7071067811865476) * a)
    poly = ((((1.061405429 * t - 1.453152027) * t + 1.421413741) * t - 0.284496736) * t + 0.254829592) * t
    tail = 0.5 * poly * e
    return jnp.where(x < 0, tail, 1.0 - tail), e


def tile(n, size):
    return pl.ds(pl.multiple_of(n * size, size), size)


def matrix(value):
    rows = 1
    for size in value.shape[:-1]:
        rows *= size
    return value.reshape(rows, value.shape[-1])


def pair_forward(pair, q_ref, k_ref, v_ref, kprT_ref, qpsT_ref, mask_ref, flip_ref, ctx_ref, pT_ref, scale):
    T = q_ref.shape[0]
    B = T // 2
    lanes = tile(pair, 128)
    outs = []
    for hh in range(2):
        keep = iota((1, 128), 1) // HEAD == hh
        qh = jnp.where(keep, q_ref[:, lanes], 0)
        kh = jnp.where(keep, k_ref[:, lanes], 0)
        content = nt(qh, k_ref[:, lanes])
        to, frm = [], []
        for b in range(2):
            u0 = B * (1 - b)
            t = nn(qh[b * B:(b + 1) * B], kprT_ref[lanes, u0:u0 + 3 * B])
            to.append(pltpu.roll(t, 2 * B + 1, 1, stride=1, stride_axis=0)[:, :T])
            f = nn(kh[b * B:(b + 1) * B], qpsT_ref[lanes, u0:u0 + 3 * B])
            frm.append(pltpu.roll(f, 2 * B + 1, 1, stride=1, stride_axis=0)[:, :T].T)
        s = content + jnp.concatenate(to, axis=0) + jnp.concatenate(frm, axis=1) + mask_ref[0:1, :]
        top = jnp.max(s, axis=1, keepdims=True)
        e = jnp.exp2((s - top) * (scale * LOG2E))
        p = (e * (1.0 / jnp.sum(e, axis=1, keepdims=True))).astype(BF)
        outs.append(nn(p, v_ref[:, lanes]))
        pT_ref[2 * pair + hh, 0:B, :] = nt(flip_ref[...], p[:, B:T]).astype(BF)
        pT_ref[2 * pair + hh, B:T, :] = nt(flip_ref[...], p[:, 0:B]).astype(BF)
    ctx_ref[:, lanes] = jnp.where(iota((1, 128), 1) < HEAD, outs[0], outs[1]).astype(BF)


def pair_backward(pair, q_ref, kf_ref, vf_ref, kpsT_ref, qpsT_ref, dcT_ref, pT_ref, scale):
    T = q_ref.shape[0]
    B = T // 2
    lanes = tile(pair, 128)
    low = iota((1, 128), 1) < HEAD
    q, kf, dcT = q_ref[:, lanes], kf_ref[:, lanes], dcT_ref[lanes, :]
    dqs, dks, dvs, gks, gqs = [], [], [], [], []
    for hh in range(2):
        vh = jnp.where(iota((1, 128), 1) // HEAD == hh, vf_ref[:, lanes], 0)
        pT = pT_ref[2 * pair + hh]
        dpT = nn(vh, dcT)
        wide = pT.astype(F32)
        prod = wide * dpT
        inner = column_sum(prod) / column_sum(wide)
        dsT = (prod - wide * inner).astype(BF)
        ds = dsT.T
        zero = jnp.zeros((B, B), BF)
        dk, dq, gq, gk = [], [], [], []
        for b in range(2):
            rows, span = slice(b * B, (b + 1) * B), slice(b * B, b * B + 3 * B)
            gf = pltpu.roll(jnp.concatenate([dsT[rows], zero], axis=1), 0, 1, stride=1, stride_axis=0)
            dk.append(nn(dsT[rows], q) + nt(gf, qpsT_ref[lanes, span]))
            gq.append(tn(kf[rows], gf)[hh * HEAD:(hh + 1) * HEAD])
            gt = pltpu.roll(jnp.concatenate([ds[rows], zero], axis=1), 0, 1, stride=1, stride_axis=0)
            dq.append(nn(ds[rows], kf) + nt(gt, kpsT_ref[lanes, span]))
            gk.append(tn(q[rows], gt)[hh * HEAD:(hh + 1) * HEAD])
        dks.append(jnp.concatenate(dk, axis=0))
        dqs.append(jnp.concatenate(dq, axis=0))
        dvs.append(nt(pT, dcT))
        gqs.append(gq)
        gks.append(gk)
    for ref, pieces in ((qpsT_ref, gqs), (kpsT_ref, gks)):
        for hh in range(2):
            g = pieces[hh]
            rows = pl.ds(pl.multiple_of(pair * 128 + HEAD * hh, HEAD), HEAD)
            ref[rows, 0:B] = (scale * g[0][:, 0:B]).astype(BF)
            ref[rows, B:3 * B] = (scale * (g[0][:, B:] + g[1][:, 0:2 * B])).astype(BF)
            ref[rows, 3 * B:] = (scale * g[1][:, 2 * B:]).astype(BF)
    q_ref[:, lanes] = (scale * jnp.where(low, dqs[0], dqs[1])).astype(BF)
    kf_ref[:, lanes] = (scale * jnp.where(low, dks[0], dks[1])).astype(BF)
    vf_ref[:, lanes] = jnp.where(low, dvs[0], dvs[1]).astype(BF)


class Place:
    def __init__(self):
        f = lax.axis_index("fsdp")
        self.here = dict(c=lax.axis_index("dp"), v=lax.div(f, 8), w=lax.rem(lax.div(f, 4), 2), y=lax.rem(lax.div(f, 2), 2), x=lax.rem(f, 2))

    def across(self, axis):
        to = {**self.here, axis: 1 - self.here[axis]}
        return (to["c"], ((to["v"] * 2 + to["w"]) * 2 + to["y"]) * 2 + to["x"])

    def index(self, whole="", other=""):
        return tuple(slice(None) if a in whole else 1 - i if a in other else i for a, i in self.here.items())

    def barrier(self):
        sem = pltpu.get_barrier_semaphore()
        for axis in self.here:
            pl.semaphore_signal(sem, inc=1, device_id=self.across(axis), device_id_type=MESH)
        pl.semaphore_wait(sem, len(self.here))


def remote(src, dst, send, recv, to):
    return pltpu.make_async_remote_copy(src_ref=src, dst_ref=dst, send_sem=send, recv_sem=recv, device_id=to, device_id_type=MESH)


GATHERS = (
    (0, 384, 256),
    (1, 0, 256),
    (1, 256, 256),
    (1, 512, 256),
    (0, 0, 384),
    (2, 0, 768),
    (3, 0, 768),
    (4, 0, 768),
    (5, 0, 768),
    (6, 0, 768),
    (7, 0, 768),
    (8, 0, 768),
    (9, 0, 768),
    (10, 0, 768),
    (11, 0, 768),
    (12, 0, 768),
)
SCATTERS = (
    (5, 0, 768),
    (6, 0, 768),
    (7, 0, 768),
    (8, 0, 768),
    (9, 0, 768),
    (10, 0, 768),
    (11, 0, 768),
    (12, 0, 768),
    (4, 0, 768),
    (1, 0, 768),
    (2, 0, 768),
    (0, 0, 384),
    (0, 384, 256),
    (3, 512, 256),
    (3, 256, 256),
    (3, 0, 256),
)
TICKS = {
    "pre": ((0, 0, 0), (0, 1, 0), (0, 2, 0), (0, 3, 0), (0, 4, 0), (0, 5, 0), (0, 6, 0),),
    "before Q0": ((0, 0, 1), (0, 1, 1), (0, 2, 1), (0, 7, 0), (0, 3, 1), (0, 4, 1), (0, 0, 2), (0, 1, 2), (0, 2, 2), (0, 5, 1), (0, 8, 0), (0, 3, 2), (0, 4, 2), (0, 6, 1), (0, 9, 0), (0, 0, 3), (0, 7, 1), (0, 5, 2), (0, 1, 3), (0, 10, 0), (0, 2, 3), (0, 6, 2), (0, 8, 1), (0, 11, 0), (0, 0, 4), (0, 3, 3), (0, 7, 2), (0, 1, 4), (0, 4, 3), (0, 9, 1), (0, 12, 0), (0, 2, 4), (0, 0, 5), (0, 8, 2), (0, 1, 5), (0, 3, 4), (0, 2, 5), (0, 5, 3), (0, 4, 4), (0, 10, 1), (0, 13, 0), (0, 9, 2), (0, 3, 5),),
    "before P0": ((0, 4, 5),),
    "P0": ((0, 6, 3),),
    "F0": ((0, 5, 4), (0, 7, 3), (0, 10, 2), (0, 11, 1), (0, 14, 0),),
    "F1": ((0, 6, 4), (0, 8, 3), (0, 12, 1), (0, 15, 0),),
    "before Q1": ((0, 5, 5),),
    "Q1": ((0, 13, 1), (0, 7, 4),),
    "P1": ((0, 11, 2),),
    "F2": ((0, 8, 4), (0, 9, 3), (0, 12, 2), (0, 10, 3),),
    "F3": ((0, 13, 2), (0, 14, 1), (0, 15, 1),),
    "before Q2": ((0, 6, 5),),
    "Q2": ((0, 11, 3),),
    "P2": ((0, 9, 4),),
    "F4": ((0, 10, 4), (0, 12, 3), (0, 14, 2), (0, 15, 2),),
    "F5": ((0, 11, 4), (0, 13, 3),),
    "before wo": ((0, 7, 5),),
    "before U0": ((0, 8, 5),),
    "U0": ((0, 12, 4), (0, 14, 3),),
    "before U1": ((0, 9, 5),),
    "U1": ((0, 15, 3),),
    "before U2": ((0, 10, 5),),
    "U2": ((0, 13, 4),),
    "before U3": ((0, 11, 5),),
    "before down": ((0, 12, 5), (0, 14, 4), (0, 13, 5), (0, 15, 4), (0, 14, 5), (0, 15, 5),),
    "b0": ((1, 0, 0),),
    "b1": ((1, 1, 0),),
    "b2": ((1, 0, 1), (1, 2, 0),),
    "b3": ((1, 1, 1), (1, 3, 0),),
    "d0": ((1, 2, 1),),
    "d2": ((1, 0, 2),),
    "d3": ((1, 3, 1), (1, 4, 0), (1, 5, 0), (1, 6, 0),),
    "wob": ((1, 1, 2),),
    "B0": ((1, 0, 3), (1, 2, 2), (1, 4, 1), (1, 5, 1), (1, 6, 1), (1, 7, 0), (1, 8, 0),),
    "B1": ((1, 0, 4), (1, 1, 3), (1, 3, 2), (1, 7, 1),),
    "gw0": ((1, 2, 3), (1, 4, 2), (1, 8, 1), (1, 9, 0),),
    "B2": ((1, 0, 5), (1, 3, 3), (1, 5, 2), (1, 9, 1),),
    "B3": ((1, 1, 4), (1, 4, 3), (1, 6, 2),),
    "gw1": ((1, 2, 4), (1, 5, 3), (1, 7, 2), (1, 10, 0),),
    "B4": ((1, 1, 5), (1, 3, 4), (1, 2, 5), (1, 6, 3), (1, 8, 2), (1, 10, 1),),
    "B5": ((1, 3, 5), (1, 4, 4), (1, 5, 4), (1, 6, 4), (1, 7, 3), (1, 9, 2),),
    "rel2": ((1, 11, 0), (1, 12, 0),),
    "gv2": ((1, 13, 0),),
    "gk2": ((1, 8, 3),),
    "gq2": ((1, 10, 2), (1, 4, 5), (1, 7, 4), (1, 11, 1), (1, 14, 0), (1, 12, 1), (1, 15, 0), (1, 13, 1),),
    "end": ((1, 5, 5), (1, 8, 4), (1, 6, 5), (1, 14, 1), (1, 15, 1), (1, 9, 3), (1, 11, 2), (1, 12, 2), (1, 13, 2), (1, 10, 3), (1, 14, 2), (1, 7, 5), (1, 15, 2), (1, 8, 5), (1, 9, 4), (1, 11, 3), (1, 10, 4), (1, 12, 3), (1, 13, 3), (1, 11, 4), (1, 14, 3), (1, 12, 4), (1, 15, 3), (1, 13, 4), (1, 9, 5), (1, 10, 5), (1, 14, 4), (1, 11, 5), (1, 12, 5), (1, 15, 4), (1, 13, 5), (1, 14, 5), (1, 15, 5),),
}
STEPS = ((("v", ""),), (("x", "v"), ("y", "v")), (("w", "vx"), ("w", "vy")), (("y", "vxw"), ("x", "vyw")))


class Part:
    def __init__(self, place, piece, lo, cols):
        cut = cols // 256 * 128
        self.p, self.piece, self.lo, self.cols = place, piece, lo, cols
        self.all = pl.ds(lo, cols)
        self.halves = (pl.ds(lo, cut), pl.ds(lo + cut, cols - cut))

    def spans(self, k):
        return (self.all,) if len(STEPS[k]) == 1 else self.halves

    def settle(self, ref, send, recv):
        copy = remote(ref, ref, send, recv, self.p.across("c"))
        copy.wait_recv()
        copy.wait_send()


class Gather(Part):
    def __init__(self, place, piece, lo, cols, send, recv):
        super().__init__(place, piece, lo, cols)
        self.send, self.recv = send, recv

    def step(self, k):
        n = len(STEPS)
        if k > 0:
            done = "vwyx" if k - 1 == n else STEPS[k - 1][0][1]
            self.settle(self.piece(self.p.index(done), self.all), self.send.at[0], self.recv.at[k - 1])
        if k < n:
            for (axis, done), span in zip(STEPS[k], self.spans(k)):
                ref = self.piece(self.p.index(done), span)
                remote(ref, ref, self.send.at[0], self.recv.at[k], self.p.across(axis)).start()
        elif k == n:
            ref = self.piece(self.p.index("vwyx"), self.all)
            remote(ref, ref, self.send.at[0], self.recv.at[k], self.p.across("c")).start()


def add_into(ref, other):
    ref[...] = (ref[...].astype(F32) + other[...].astype(F32)).astype(BF)


class Scatter(Part):
    def __init__(self, place, piece, lo, cols, order, last, slots, buffers, send, recv, credit, finish):
        super().__init__(place, piece, lo, cols)
        self.order, self.last, self.send, self.recv, self.credit, self.finish = order, last, send, recv, credit, finish
        self.slot = slots.at[order % SLOTS, :, :, :, :, :, pl.ds(0, cols)]
        self.buffers = buffers

    def step(self, k):
        p, g, n = self.p, self.piece, len(STEPS)
        if k == 1:
            self.settle(self.slot, self.send.at[0], self.recv.at[0])

            @pl.loop(0, 2)
            def _(v):
                at = p.index("vwyx")
                add_into(g((at[0], v, *at[2:]), self.all), self.slot.at[v])

            if self.order + SLOTS < self.last:
                pl.semaphore_signal(self.credit, inc=1, device_id=p.across("c"), device_id_type=MESH)
        elif k > 1:
            j = n + 1 - k
            self.settle(g(p.index(STEPS[j][0][1]), self.all), self.send.at[0], self.recv.at[k - 1])
            if k <= n:
                for (_, done), span, buffer in zip(STEPS[j], self.spans(j), self.buffers[j]):
                    add_into(g(p.index(done), span), buffer)
            else:
                self.finish(self.lo, g(p.index(), self.all)[...].astype(F32) + self.buffers[0][0][...].astype(F32))
        if k == 0:
            if self.order >= SLOTS:
                pl.semaphore_wait(self.credit, 1)
            ref = g(p.index("vwyx", "c"), self.all)
            remote(ref, self.slot, self.send.at[0], self.recv.at[0], p.across("c")).start()
        elif k <= n:
            j = n - k
            for (axis, done), span, buffer in zip(STEPS[j], self.spans(j), self.buffers[j]):
                ref = g(p.index(done, axis), span)
                remote(ref, buffer, self.send.at[0], self.recv.at[k], p.across(axis)).start()


def scatter_buffers(rows, cols):
    cut = cols // 256 * 128
    found = []
    for step in STEPS:
        widths = (cols,) if len(step) == 1 else (cut, cols - cut)
        found.append([pltpu.VMEM((*(2,) * len(done), rows, width), BF) for (_, done), width in zip(step, widths)])
    return found


def layer_kernel(
    comm,
    length_ref, index_ref, x_ref, cot_ref, vec_in, rel_in, q_in, k_in, v_in, o_in, up_in, down_in,
    out_ref, gtok_ref, r_out, q_out, k_out, v_out, o_out, up_out, down_out,
    GR, GA, GO, GU, GD,
    q_ref, k_ref, v_ref, kf_ref, vf_ref, kprT_ref, kpsT_ref, qpsT_ref, pick_ref, pT_ref,
    ctx_ref, dcT_ref, n1_ref, inv1_ref, nb_ref, gd_ref, act_ref, gp_ref,
    grel_ref, cols_ref, rows_ref, bup_ref, small_ref, gbup_ref, mask_ref, flip_ref, select_ref,
    *rest,
):
    T, D = x_ref.shape
    FF = act_ref.shape[1]
    NB = pick_ref.shape[0]
    B = T // 2
    C = 256
    R = 128
    CH = FF // D
    scale = (3.0 * HEAD) ** -0.5
    length = length_ref[0]
    row = lambda k: rows_ref[k:k + 1, :]
    whole = (slice(None),) * len(GRID)
    per = D // BLOCKS

    def part(ref, *lead, trail=()):
        return lambda blocks, cols: ref.at[(*lead, *blocks, *trail, slice(None), cols)]

    pieces = [part(GR)] + [part(GA, n) for n in range(D // C)] + [part(GO)]
    pieces += [part(GU, k) for k in range(CH)] + [part(GD, trail=(k,)) for k in range(CH)]
    if comm:
        slots, buffers, (ag_send, ag_recv, rs_send, rs_recv, credit) = rest[0], rest[1:-5], rest[-5:]
        place = Place()
        gathers = [Gather(place, pieces[i], lo, cols, ag_send.at[j], ag_recv.at[j]) for j, (i, lo, cols) in enumerate(GATHERS)]
        nA, nO, nU, nD = 1, 1 + D // C, 2 + D // C, 2 + D // C + CH

        def finisher(i):
            def store(lo, total):
                cols = pl.ds(lo, total.shape[1])
                if i == 0:
                    r_out[:, cols] = total
                elif i < nO:
                    for b in range(0, total.shape[1], 128):
                        ref = (q_out, k_out, v_out)[(lo + b) // C]
                        ref[:, pl.ds((i - nA) * C + (lo + b) % C, 128)] = total[:, b:b + 128]
                elif i == nO:
                    o_out[:, cols] = total
                elif i < nD:
                    up_out[:, pl.ds((i - nU) * D + lo, total.shape[1])] = total
                else:
                    down_out[pl.ds((i - nD) * per, per), cols] = total
            return store

        scatters = []
        for j, (i, lo, cols) in enumerate(SCATTERS):
            scatters.append(Scatter(place, pieces[i], lo, cols, j, len(SCATTERS), slots, buffers[j], rs_send.at[j], rs_recv.at[j], credit, finisher(i)))

    def run(name):
        if comm:
            for kind, j, k in TICKS.get(name, ()):
                (scatters if kind else gathers)[j].step(k)

    def due(name, index, values):
        if comm:
            for m in values:
                label = f"{name}{m}"
                if label in TICKS:
                    @pl.when(index == m)
                    def _():
                        run(label)

    if comm:
        me = place.index()
        rows_ref[...] = jnp.zeros_like(rows_ref)
        for k, ref in enumerate(vec_in[:-1]):
            rows_ref[k:k + 1, 0:per] = ref[...].astype(F32).reshape(1, per)
        last = vec_in[-1][...].astype(F32).reshape(1, CH * per)
        for k in range(CH):
            rows_ref[9 + k:10 + k, 0:per] = last[:, k * per:(k + 1) * per]
        own = jnp.concatenate([rows_ref[:, 0:128], jnp.zeros((112, 128), F32)], axis=0).T
        GR[(*me, slice(None), pl.ds(0, NB))] = rel_in[...]
        GR[(*me, slice(None), pl.ds(NB, 128))] = own[0:per].astype(BF)
        for n in range(D // C):
            cols = pl.ds(n * C, C)
            for i, ref in enumerate((q_in, k_in, v_in)):
                GA[(n, *me, slice(None), pl.ds(i * C, C))] = ref[:, cols]
        GO[me] = o_in[...]
        for k in range(CH):
            GU[(k, *me)] = up_in[:, pl.ds(k * D, D)]
            GD[(*me, k)] = down_in[k]
        place.barrier()
        run("pre")
    else:
        GRh, GAh, GOh, GUh, GDh = rest[:5]
        sems = rest[10]
        loads = [pltpu.make_async_copy(src, dst, sems.at[i]) for i, (src, dst) in enumerate(zip((GRh, GAh, GOh, GUh, GDh), (GR, GA, GO, GU, GD)))]
        for copy in loads:
            copy.start()
        for copy in loads:
            copy.wait()
    flip_ref[...] = jnp.where(iota((B, B), 0) + iota((B, B), 1) == B - 1, 1.0, 0.0).astype(BF)
    index = jnp.broadcast_to(index_ref[...].reshape(1, 2 * T), (8, 2 * T))
    high = lax.shift_right_logical(index, 4)
    parts = [v.astype(F32).astype(BF) for v in (high, index - 16 * high)]
    back = [jnp.concatenate([nn(v[:, b * B:(b + 1) * B], flip_ref[...]) for b in range(2 * T // B - 1, -1, -1)], axis=1) for v in parts]
    reverse = (back[0] * 16.0 + back[1]).astype(jnp.int32)
    shifted = jnp.where(iota((8, 2 * T), 1) == 2 * T - 1, -1, pltpu.roll(index, 2 * T - 1, 1))
    act_ref[:, 0:2 * T] = jnp.where(iota((NB, 2 * T), 0) == reverse[0:1], 1.0, 0.0).astype(BF)
    pick_ref[...] = jnp.where(iota((NB, 2 * T), 0) == shifted[0:1], 1.0, 0.0).astype(BF)
    W = 4 * per
    block = sum(jnp.where(iota((W, CH * W), 0) >= per * i, 1, 0) for i in range(1, 4))
    ublock = sum(jnp.where(iota((1, CH * W), 1) >= per * CH * i, 1, 0) for i in range(1, 4))
    uslice = sum(jnp.where(iota((1, CH * W), 1) >= per * i, 1, 0) for i in range(1, 4 * CH))
    place_in = iota((1, CH * W), 1) - per * uslice
    select_ref[...] = jnp.where((block == ublock) & (iota((W, CH * W), 0) - per * block == place_in), 1.0, 0.0).astype(BF)
    own_column = iota((128, CH * W), 0) == 9 + uslice - CH * ublock
    mask_ref[...] = jnp.where(iota((8, T), 1) < length, 0.0, -1e30)
    small_ref[...] = jnp.zeros_like(small_ref)
    grel_ref[...] = jnp.zeros_like(grel_ref)
    run("before Q0")
    cols_ref[...] = matrix(GR[(*whole, slice(None), pl.ds(NB, 128))].astype(F32))
    rows_ref[...] = cols_ref[...].T[0:16]

    @pl.loop(0, D // W)
    def _(t):
        spread = tn(cols_ref[tile(t, W), :].astype(BF), select_ref[...])
        bup_ref[0:1, tile(t, CH * W)] = column_sum(jnp.where(own_column, spread, 0.0))

    @pl.loop(0, D // C)
    def _(n):
        due("before Q", n, range(1, D // C))
        cols = tile(n, C)
        weight = lambda i: matrix(GA[(n, *whole, slice(None), pl.ds(i * C, C))])
        q_ref[:, cols] = (nn(x_ref[...], weight(0)) + rows_ref[0:1, cols]).astype(BF)
        k = (nn(x_ref[...], weight(1)) + rows_ref[1:2, cols]).astype(BF)
        v = (nn(x_ref[...], weight(2)) + rows_ref[2:3, cols]).astype(BF)
        k_ref[:, cols] = k
        v_ref[:, cols] = v
        for src, dst in ((k, kf_ref), (v, vf_ref)):
            dst[0:B, cols] = nn(flip_ref[...], src[B:T]).astype(BF)
            dst[B:T, cols] = nn(flip_ref[...], src[0:B]).astype(BF)
        due("Q", n, range(D // C))
        due("before P", n, (0,))
        relT = matrix(GR[(*whole, slice(None), pl.ds(0, NB))])
        rk = (tn(weight(1), relT) + cols_ref[cols, 1:2]).astype(BF)
        rq = (tn(weight(0), relT) + cols_ref[cols, 0:1]).astype(BF)
        kprT_ref[cols, :] = nn(rk, act_ref[:, 0:2 * T]).astype(BF)
        kpsT_ref[cols, :] = nn(rk, pick_ref[...]).astype(BF)
        qpsT_ref[cols, :] = nn(rq, pick_ref[...]).astype(BF)
        due("P", n, range(D // C))

        @pl.loop(0, 2)
        def _(i):
            pair_forward(2 * n + i, q_ref, k_ref, v_ref, kprT_ref, qpsT_ref, mask_ref, flip_ref, ctx_ref, pT_ref, scale)
            due("F", 2 * n + i, range(2 * D // C))

    run("before wo")
    second_ref = gtok_ref

    @pl.loop(0, D // C)
    def _(n):
        cols = tile(n, C)
        w = matrix(GO[(*whole, slice(None), cols)])
        second_ref[:, cols] = x_ref[:, cols].astype(F32) + (nn(ctx_ref[...], w) + rows_ref[3:4, cols])

    run("wo")

    @pl.loop(0, T // R)
    def _(r):
        rs = tile(r, R)
        n1, inv1 = norm_rows(second_ref[rs, :])
        n1_ref[rs, :] = n1
        inv1_ref[rs, :] = jnp.broadcast_to(inv1, (R, 128))
        nb_ref[rs, :] = (n1 * row(4) + row(5)).astype(BF)

    run("ln1")

    @pl.loop(0, CH)
    def _(k):
        due("before U", k, range(CH))

        @pl.loop(0, D // C)
        def _(j):
            w = matrix(GU[(k, *whole, slice(None), tile(j, C))])
            cols = tile(k * (D // C) + j, C)
            up = nn(nb_ref[...], w) + bup_ref[0:1, cols]
            phi, e = normal_cdf_pair(up)
            act_ref[:, cols] = (up * phi).astype(BF)
            gp_ref[:, cols] = (phi + up * e * 0.3989422804014327).astype(BF)

        due("U", k, range(CH))

    run("before down")

    @pl.loop(0, D // C)
    def _(n):
        cols = tile(n, C)
        w = matrix(GD[(*whole, slice(None), slice(None), cols)])
        normed = n1_ref[:, cols] * rows_ref[4:5, cols] + rows_ref[5:6, cols]
        second_ref[:, cols] = normed + (nn(act_ref[...], w) + rows_ref[6:7, cols])

    run("down")

    @pl.loop(0, T // R)
    def _(r):
        rs = tile(r, R)
        live = jnp.where(iota((R, 1), 0) + r * R < length, 1.0, 0.0)
        n2, inv2 = norm_rows(second_ref[rs, :])
        out_ref[rs, :] = ((n2 * row(7) + row(8)) * live).astype(BF)
        start = cot_ref[rs, :].astype(F32) * live
        g = norm_back(start * row(7), n2, inv2)
        second_ref[rs, :] = g
        gd = g.astype(BF)
        gd_ref[rs, :] = gd
        small_ref[6:7, :] += column_sum(gd.astype(F32))
        small_ref[7:8, :] += column_sum(start * n2)
        small_ref[8:9, :] += column_sum(start)

    run("ln2")

    @pl.loop(0, CH)
    def _(k):
        units = tile(k, D)
        w = matrix(GD[lax.div(k, 2), lax.rem(k, 2)])
        gu = (nt(gd_ref[...], w) * gp_ref[:, units].astype(F32)).astype(BF)
        gp_ref[:, units] = gu
        gbup_ref[0:1, units] = column_sum(gu.astype(F32))
        second_ref[...] += nt(gu, matrix(GU[k]))

        @pl.loop(0, 2)
        def _(i):
            g = tn(nb_ref[:, tile(i, D // 2)], gp_ref[:, units])
            GU[k, i] = g.reshape(*GU.shape[2:]).astype(BF)

        due("b", k, range(CH))

    @pl.loop(0, CH)
    def _(k):
        @pl.loop(0, 2)
        def _(i):
            at = pl.ds(pl.multiple_of(k * D + i * (D // 2), D // 2), D // 2)
            g = tn(act_ref[:, at], gd_ref[...])
            GD[lax.div(k, 2), lax.rem(k, 2), i] = g.reshape(*GD.shape[3:]).astype(BF)

        due("d", k, range(CH))

    @pl.loop(0, T // R)
    def _(r):
        rs = tile(r, R)
        g = second_ref[rs, :]
        n1 = n1_ref[rs, :]
        gm = norm_back(g * row(4), n1, inv1_ref[rs, 0:1])
        second_ref[rs, :] = gm
        ga = gm.astype(BF)
        gd_ref[rs, :] = ga
        small_ref[3:4, :] += column_sum(ga.astype(F32))
        small_ref[4:5, :] += column_sum(g * n1)
        small_ref[5:6, :] += column_sum(g)

    run("ln1b")

    @pl.loop(0, GRID[0])
    def _(i):
        at = tile(i, D // 2)
        dcT_ref[at, :] = nt(matrix(GO[i]), gd_ref[...]).astype(BF)
        g = tn(ctx_ref[:, at], gd_ref[...])
        GO[i] = g.reshape(*GO.shape[1:]).astype(BF)

    run("wob")

    kprT_ref[:, 0:NB] = matrix(GR[(*whole, slice(None), pl.ds(0, NB))])

    @pl.loop(0, D // C)
    def _(n):
        cols = tile(n, C)
        final = (D // C - 1,)

        @pl.loop(0, 2)
        def _(i):
            pair_backward(2 * n + i, q_ref, kf_ref, vf_ref, kpsT_ref, qpsT_ref, dcT_ref, pT_ref, scale)
            due("B", 2 * n + i, range(2 * D // C))

        dq = q_ref[:, cols]
        for src, dst in ((kf_ref, k_ref), (vf_ref, v_ref)):
            dst[0:B, cols] = nn(flip_ref[...], src[B:T, cols]).astype(BF)
            dst[B:T, cols] = nn(flip_ref[...], src[0:B, cols]).astype(BF)
        dk, dv = k_ref[:, cols], v_ref[:, cols]
        grk = nt(kpsT_ref[cols, :], pick_ref[...]).astype(BF)
        grq = nt(qpsT_ref[cols, :], pick_ref[...]).astype(BF)
        weight = lambda i: matrix(GA[(n, *whole, slice(None), pl.ds(i * C, C))])
        grel_ref[...] += nn(weight(1), grk) + nn(weight(0), grq)
        ones_t, ones_b = jnp.ones((8, T), BF), jnp.ones((8, NB), BF)
        small_ref[0:1, cols] = (nn(ones_t, dq) + nt(ones_b, grq))[0:1]
        small_ref[1:2, cols] = (nn(ones_t, dk) + nt(ones_b, grk))[0:1]
        small_ref[2:3, cols] = nn(ones_t, dv)[0:1]

        @pl.when(n == final[0])
        def _():
            small_ref[9:16, :] = jnp.zeros((7, D), F32)
            cols_ref[...] = jnp.concatenate([small_ref[...], jnp.zeros((112, D), F32)], axis=0).T

            @pl.loop(0, D // W)
            def _(t):
                g = jnp.where(own_column, gbup_ref[0:1, tile(t, CH * W)], 0.0).astype(BF)
                cols_ref[tile(t, W), :] += nt(select_ref[...], g)

            GR[(*whole, slice(None), pl.ds(0, NB))] = grel_ref[...].reshape(*GR.shape[:6], NB).astype(BF)
            GR[(*whole, slice(None), pl.ds(NB, 128))] = cols_ref[...].reshape(*GR.shape[:6], 128).astype(BF)

        due("rel", n, final)
        for i, name, d, gr in ((2, "gv", dv, None), (1, "gk", dk, grk), (0, "gq", dq, grq)):
            gtok_ref[...] += nt(d, weight(i))
            for half in range(GRID[0]):
                g = tn(x_ref[:, half * (D // 2):(half + 1) * (D // 2)], d)
                if gr is not None:
                    g = g + nt(kprT_ref[half * (D // 2):(half + 1) * (D // 2), 0:NB], gr)
                GA[(n, half, *whole[1:], slice(None), pl.ds(i * C, C))] = g.reshape(*GA.shape[2:7], C).astype(BF)
            due(name, n, final)
        due("gw", n, range(D // C))

    if comm:
        run("end")
    else:
        GRh, GAh, GOh, GUh, GDh = rest[5:10]
        stores = [pltpu.make_async_copy(src, dst, sems.at[i]) for i, (dst, src) in enumerate(zip((GRh, GAh, GOh, GUh, GDh), (GR, GA, GO, GU, GD)))]
        for copy in stores:
            copy.start()
        for copy in stores:
            copy.wait()


def finish_kernel(r_ref, *refs):
    n = (len(refs) - 11) // 2
    for i in range(n):
        refs[n + i][...] = refs[i][...]
    rel_out, vectors, wide = refs[2 * n], refs[2 * n + 1:2 * n + 10], refs[2 * n + 10]
    rows, NB = rel_out.shape
    rel_out[...] = r_ref[:, 0:NB]
    flat = jnp.concatenate([r_ref[:, NB:], jnp.zeros((128 - rows, 128), F32)], axis=0).T
    for k, ref in enumerate(vectors):
        ref[...] = flat[k:k + 1, 0:rows].reshape(rows)
    wide[...] = jnp.concatenate([flat[9 + k:10 + k, 0:rows] for k in range(wide.shape[0] // rows)], axis=1).reshape(wide.shape[0])


def layer_scratch(T, D, FF, NB, heads):
    V = pltpu.VMEM
    n, ch = D // 256, FF // D
    rows = D // BLOCKS
    td, r = V((T, D), BF), V((*GRID, rows, NB + 128), BF)
    return [
        r, V((n, *GRID, rows, D), BF), V((*GRID, rows, D), BF), V((ch, *GRID, rows, D), BF), V((*GRID, ch, rows, D), BF),
        td, td, td, td, td, V((D, 2 * T), BF), V((D, 2 * T), BF), V((D, 2 * T), BF), V((NB, 2 * T), BF), V((heads, T, T), BF),
        td, V((D, T), BF), V((T, D), F32), V((T, 128), F32), td, td, V((T, FF), BF), V((T, FF), BF),
        V((D, NB), F32), V((D, 128), F32), V((16, D), F32), V((8, FF), F32), V((16, D), F32), V((8, FF), F32), V((8, T), F32),
        V((T // 2, T // 2), BF), V((4 * rows, 4 * rows * ch), BF),
    ]


def call_layer(comm, length, index, x, cot, parts):
    T, D = x.shape
    S = jax.ShapeDtypeStruct
    VM, HBM, SM = (pl.BlockSpec(memory_space=space) for space in (pltpu.VMEM, pl.ANY, pltpu.SMEM))
    heads = D // HEAD
    if comm:
        vectors, rel, wq, wk, wv, wo, wup, wdown = parts
        operands = (*vectors, rel, wq, wk, wv, wo, wup, wdown)
        rows, FF = wup.shape
        NB = rel.shape[1]
        outs = [S((T, D), BF), S((T, D), F32), S((rows, NB + 128), F32)] + [S((rows, D), F32)] * 4 + [S(wup.shape, F32), S((FF // D * rows, D), F32)]
        out_specs = [VM] * len(outs)
        in_specs = [SM] + [VM] * (3 + len(operands))
        sems = [pltpu.SemaphoreType.DMA((len(parts), k)) for parts in (GATHERS, SCATTERS) for k in (1, 5)] + [pltpu.SemaphoreType.REGULAR]
        extra = [pltpu.VMEM((SLOTS, *GRID[1:], rows, D), BF)]
        extra += [scatter_buffers(rows, cols) for _, _, cols in SCATTERS] + sems

        def kernel(*refs):
            given = 4 + len(vectors)
            layer_kernel(True, *refs[:4], refs[4:given], *refs[given:])
    else:
        gr, ga, go, gu, gd = operands = parts
        FF, NB = gu.shape[0] * D, gr.shape[-1] - 128
        outs = [S((T, D), BF), S((T, D), F32)] + [S(p.shape, p.dtype) for p in parts]
        in_specs = [SM] + [VM] * 3 + [HBM] * 5
        out_specs = [VM] * 2 + [HBM] * 5
        extra = [pltpu.SemaphoreType.DMA((5,))]

        def kernel(*refs):
            ins, given, results, stored, scratch = refs[:4], refs[4:9], refs[9:11], refs[11:16], refs[16:]
            layer_kernel(False, *ins, *[None] * 8, *results, *[None] * 7, *scratch[:-1], *given, *stored, scratch[-1])

    return pl.pallas_call(
        kernel,
        out_shape=outs,
        in_specs=in_specs,
        out_specs=out_specs,
        scratch_shapes=layer_scratch(T, D, FF, NB, heads) + extra,
        compiler_params=pltpu.CompilerParams(
            vmem_limit_bytes=VMEM_LIMIT,
            **(dict(collective_id=0, has_side_effects=True) if comm else {}),
        ),
    )(length, index, x, cot, *operands)


VMEM_LIMIT = 63 * 2**20


def body(comm, tokens, lengths, rel_index, w_query, b_query, w_key, b_key, w_value, b_value, w_out, b_out, rel_table,
         gain_one, shift_one, w_up, b_up, w_down, b_down, gain_two, shift_two, cotangent):
    rows, D = w_query.shape
    NB = rel_table.shape[0]
    FF = w_up.shape[1]
    ch, n = FF // D, D // 256
    vectors = (b_query, b_key, b_value, b_out, gain_one, shift_one, b_down, gain_two, shift_two)
    if comm:
        results = call_layer(True, lengths, rel_index, tokens, cotangent,
                             ((*vectors, b_up), rel_table.T, w_query, w_key, w_value, w_out, w_up, w_down.reshape(ch, rows, D)))
        out, gtok, gr, gq, gk, gv, go, gup, gdown = results
        S = jax.ShapeDtypeStruct
        VM = pl.BlockSpec(memory_space=pltpu.VMEM)
        moved = (out, gtok, gq, gk, gv, go, gup, gdown)
        *moved, rel, bq, bk, bv, bo, g1, s1, bd, g2, s2, bu = pl.pallas_call(
            finish_kernel,
            out_shape=[S(a.shape, a.dtype) for a in moved] + [S((rows, NB), F32)] + [S((rows,), F32)] * 9 + [S(b_up.shape, F32)],
            in_specs=[VM] * 9,
            out_specs=[VM] * 19,
            compiler_params=pltpu.CompilerParams(vmem_limit_bytes=VMEM_LIMIT),
        )(gr, *moved)
        out, gtok, gq, gk, gv, go, gup, gdown = moved
        return (out, gtok, gq, bq, gk, bk, gv, bv, go, bo, rel.T, g1, s1, gup, bu, gdown, bd, g2, s2)
    gather = lambda w: lax.all_gather(w, AXES, axis=0, tiled=True)
    scatter = lambda g: lax.psum_scatter(g.astype(F32), AXES, scatter_dimension=0, tiled=True)
    r = D // BLOCKS
    pad = jnp.zeros((rows, 128 - 9), BF)
    attend = gather(jnp.concatenate([w_out, w_query, w_key, w_value, rel_table.T, jnp.stack(vectors, axis=1), pad], axis=1))
    wide = gather(b_up).reshape(BLOCKS, ch, r).transpose(0, 2, 1).reshape(D, ch)
    gr = jnp.concatenate([attend[:, 4 * D:4 * D + NB + 9], wide, pad[0] * jnp.ones((D, 1), BF)], axis=1)[:, :NB + 128].reshape(*GRID, r, NB + 128)
    go = attend[:, :D].reshape(*GRID, r, D)
    ga = attend[:, D:4 * D].reshape(*GRID, r, 3, n, 256).transpose(7, 0, 1, 2, 3, 4, 5, 6, 8).reshape(n, *GRID, r, D)
    gu = gather(w_up).reshape(*GRID, r, ch, D).transpose(6, 0, 1, 2, 3, 4, 5, 7)
    gd = gather(w_down).reshape(*GRID, ch, r, D)
    out, gtok, gr, ga, go, gu, gd = call_layer(False, lengths, rel_index, tokens, cotangent, (gr, ga, go, gu, gd))
    gr = gr.reshape(D, NB + 128)
    ga = ga.reshape(n, *GRID, r, 3, 256).transpose(1, 2, 3, 4, 5, 6, 7, 0, 8).reshape(D, 3 * D)
    wide = scatter(gr[:, NB + 9:NB + 9 + ch].reshape(BLOCKS, r, ch).transpose(0, 2, 1).reshape(FF))
    gup = scatter(gu.transpose(1, 2, 3, 4, 5, 6, 0, 7).reshape(D, FF))
    gdown = scatter(gd.reshape(FF, D))
    attend = scatter(jnp.concatenate([go.reshape(D, D), ga, gr], axis=1))
    go, gq, gk, gv = (attend[:, i * D:(i + 1) * D] for i in range(4))
    vec = lambda i: attend[:, 4 * D + NB + i]
    return (out, gtok, gq, vec(0), gk, vec(1), gv, vec(2), go, vec(3), attend[:, 4 * D:4 * D + NB].T, vec(4), vec(5),
            gup, wide, gdown, vec(6), vec(7), vec(8))


def solution(mesh):
    rows, vec = P(AXES, None), P(AXES)
    comm = mesh.shape["dp"] == GRID[0] and mesh.shape["fsdp"] == BLOCKS // GRID[0]

    def step(*args):
        return body(comm, *args)

    return jax.shard_map(
        step,
        mesh=mesh,
        in_specs=(rows, vec, P(), rows, vec, rows, vec, rows, vec, rows, vec, P(None, AXES), vec, vec, rows, vec, rows, vec, vec, vec, rows),
        out_specs=(rows, rows, rows, vec, rows, vec, rows, vec, rows, vec, P(None, AXES), vec, vec, rows, vec, rows, vec, vec, vec),
        check_vma=False,
    )
```

```python
import jax
import jax.numpy as jnp
from jax import lax
from jax.experimental import pallas as pl
from jax.experimental.pallas import tpu as pltpu
from jax.sharding import PartitionSpec as P

BF = jnp.bfloat16
F32 = jnp.float32
EPS = 1e-6
HEAD = 64
AXES = ("dp", "fsdp")
MESH = pl.DeviceIdType.MESH
LOG2E = 1.4426950408889634
GRID = (2, 2, 2, 2, 2)
BLOCKS = 32
SLOTS = 3


def dot(left, right, dims):
    return lax.dot_general(left, right, ((dims[:1], dims[1:]), ((), ())), preferred_element_type=F32)


def nn(left, right):
    return dot(left, right, (1, 0))


def nt(left, right):
    return dot(left, right, (1, 1))


def tn(left, right):
    return dot(left, right, (0, 0))


def iota(shape, axis):
    return lax.broadcasted_iota(jnp.int32, shape, axis)


def column_sum(x):
    return jnp.sum(x, axis=0, keepdims=True)


def row_mean(x):
    return jnp.sum(x, axis=1, keepdims=True) * (1.0 / x.shape[1])


def norm_rows(x):
    centred = x - row_mean(x)
    inv = lax.rsqrt(row_mean(centred * centred) + EPS)
    return centred * inv, inv


def norm_back(g, n, inv):
    return (g - row_mean(g) - n * row_mean(g * n)) * inv


def normal_cdf_pair(x):
    a = jnp.abs(x)
    e = jnp.exp2(x * x * (-0.5 * LOG2E))
    t = 1.0 / (1.0 + (0.3275911 * 0.7071067811865476) * a)
    poly = ((((1.061405429 * t - 1.453152027) * t + 1.421413741) * t - 0.284496736) * t + 0.254829592) * t
    tail = 0.5 * poly * e
    return jnp.where(x < 0, tail, 1.0 - tail), e


def tile(n, size):
    return pl.ds(pl.multiple_of(n * size, size), size)


def matrix(value):
    rows = 1
    for size in value.shape[:-1]:
        rows *= size
    return value.reshape(rows, value.shape[-1])


def pair_forward(pair, q_ref, k_ref, v_ref, kprT_ref, qpsT_ref, mask_ref, flip_ref, ctx_ref, pT_ref, scale):
    T = q_ref.shape[0]
    B = T // 2
    lanes = tile(pair, 128)
    outs = []
    for hh in range(2):
        keep = iota((1, 128), 1) // HEAD == hh
        qh = jnp.where(keep, q_ref[:, lanes], 0)
        kh = jnp.where(keep, k_ref[:, lanes], 0)
        content = nt(qh, k_ref[:, lanes])
        to, frm = [], []
        for b in range(2):
            u0 = B * (1 - b)
            t = nn(qh[b * B:(b + 1) * B], kprT_ref[lanes, u0:u0 + 3 * B])
            to.append(pltpu.roll(t, 2 * B + 1, 1, stride=1, stride_axis=0)[:, :T])
            f = nn(kh[b * B:(b + 1) * B], qpsT_ref[lanes, u0:u0 + 3 * B])
            frm.append(pltpu.roll(f, 2 * B + 1, 1, stride=1, stride_axis=0)[:, :T].T)
        s = content + jnp.concatenate(to, axis=0) + jnp.concatenate(frm, axis=1) + mask_ref[0:1, :]
        top = jnp.max(s, axis=1, keepdims=True)
        e = jnp.exp2((s - top) * (scale * LOG2E))
        p = (e * (1.0 / jnp.sum(e, axis=1, keepdims=True))).astype(BF)
        outs.append(nn(p, v_ref[:, lanes]))
        pT_ref[2 * pair + hh, 0:B, :] = nt(flip_ref[...], p[:, B:T]).astype(BF)
        pT_ref[2 * pair + hh, B:T, :] = nt(flip_ref[...], p[:, 0:B]).astype(BF)
    ctx_ref[:, lanes] = jnp.where(iota((1, 128), 1) < HEAD, outs[0], outs[1]).astype(BF)


def pair_backward(pair, q_ref, kf_ref, vf_ref, kpsT_ref, qpsT_ref, dcT_ref, pT_ref, scale):
    T = q_ref.shape[0]
    B = T // 2
    lanes = tile(pair, 128)
    low = iota((1, 128), 1) < HEAD
    q, kf, dcT = q_ref[:, lanes], kf_ref[:, lanes], dcT_ref[lanes, :]
    dqs, dks, dvs, gks, gqs = [], [], [], [], []
    for hh in range(2):
        vh = jnp.where(iota((1, 128), 1) // HEAD == hh, vf_ref[:, lanes], 0)
        pT = pT_ref[2 * pair + hh]
        dpT = nn(vh, dcT)
        wide = pT.astype(F32)
        prod = wide * dpT
        inner = column_sum(prod) / column_sum(wide)
        dsT = (prod - wide * inner).astype(BF)
        ds = dsT.T
        zero = jnp.zeros((B, B), BF)
        dk, dq, gq, gk = [], [], [], []
        for b in range(2):
            rows, span = slice(b * B, (b + 1) * B), slice(b * B, b * B + 3 * B)
            gf = pltpu.roll(jnp.concatenate([dsT[rows], zero], axis=1), 0, 1, stride=1, stride_axis=0)
            dk.append(nn(dsT[rows], q) + nt(gf, qpsT_ref[lanes, span]))
            gq.append(tn(kf[rows], gf)[hh * HEAD:(hh + 1) * HEAD])
            gt = pltpu.roll(jnp.concatenate([ds[rows], zero], axis=1), 0, 1, stride=1, stride_axis=0)
            dq.append(nn(ds[rows], kf) + nt(gt, kpsT_ref[lanes, span]))
            gk.append(tn(q[rows], gt)[hh * HEAD:(hh + 1) * HEAD])
        dks.append(jnp.concatenate(dk, axis=0))
        dqs.append(jnp.concatenate(dq, axis=0))
        dvs.append(nt(pT, dcT))
        gqs.append(gq)
        gks.append(gk)
    for ref, pieces in ((qpsT_ref, gqs), (kpsT_ref, gks)):
        for hh in range(2):
            g = pieces[hh]
            rows = pl.ds(pl.multiple_of(pair * 128 + HEAD * hh, HEAD), HEAD)
            ref[rows, 0:B] = (scale * g[0][:, 0:B]).astype(BF)
            ref[rows, B:3 * B] = (scale * (g[0][:, B:] + g[1][:, 0:2 * B])).astype(BF)
            ref[rows, 3 * B:] = (scale * g[1][:, 2 * B:]).astype(BF)
    q_ref[:, lanes] = (scale * jnp.where(low, dqs[0], dqs[1])).astype(BF)
    kf_ref[:, lanes] = (scale * jnp.where(low, dks[0], dks[1])).astype(BF)
    vf_ref[:, lanes] = jnp.where(low, dvs[0], dvs[1]).astype(BF)


class Place:
    def __init__(self):
        f = lax.axis_index("fsdp")
        self.here = dict(c=lax.axis_index("dp"), v=lax.div(f, 8), w=lax.rem(lax.div(f, 4), 2), y=lax.rem(lax.div(f, 2), 2), x=lax.rem(f, 2))

    def across(self, axis):
        to = {**self.here, axis: 1 - self.here[axis]}
        return (to["c"], ((to["v"] * 2 + to["w"]) * 2 + to["y"]) * 2 + to["x"])

    def index(self, whole="", other=""):
        return tuple(slice(None) if a in whole else 1 - i if a in other else i for a, i in self.here.items())

    def barrier(self):
        sem = pltpu.get_barrier_semaphore()
        for axis in self.here:
            pl.semaphore_signal(sem, inc=1, device_id=self.across(axis), device_id_type=MESH)
        pl.semaphore_wait(sem, len(self.here))


def remote(src, dst, send, recv, to):
    return pltpu.make_async_remote_copy(src_ref=src, dst_ref=dst, send_sem=send, recv_sem=recv, device_id=to, device_id_type=MESH)


GATHERS = (
    (0, 384, 256),
    (1, 0, 256),
    (1, 256, 256),
    (1, 512, 256),
    (0, 0, 384),
    (2, 0, 768),
    (3, 0, 768),
    (4, 0, 768),
    (5, 0, 768),
    (6, 0, 768),
    (7, 0, 768),
    (8, 0, 768),
    (9, 0, 768),
    (10, 0, 768),
    (11, 0, 768),
    (12, 0, 768),
)
SCATTERS = (
    (5, 0, 768),
    (6, 0, 768),
    (7, 0, 768),
    (8, 0, 768),
    (9, 0, 768),
    (10, 0, 768),
    (11, 0, 768),
    (12, 0, 768),
    (4, 0, 768),
    (1, 0, 768),
    (2, 0, 768),
    (0, 0, 384),
    (0, 384, 256),
    (3, 512, 256),
    (3, 256, 256),
    (3, 0, 256),
)
TICKS = {
    "pre": ((0, 0, 0), (0, 1, 0), (0, 2, 0), (0, 3, 0), (0, 4, 0), (0, 5, 0),),
    "before Q0": ((0, 0, 1), (0, 1, 1), (0, 2, 1), (0, 6, 0), (0, 3, 1), (0, 4, 1), (0, 7, 0), (0, 0, 2), (0, 1, 2), (0, 2, 2), (0, 3, 2), (0, 4, 2), (0, 5, 1), (0, 8, 0), (0, 0, 3), (0, 6, 1), (0, 9, 0), (0, 5, 2), (0, 1, 3), (0, 7, 1), (0, 10, 0), (0, 2, 3), (0, 0, 4), (0, 6, 2), (0, 3, 3), (0, 0, 5), (0, 1, 4), (0, 4, 3), (0, 7, 2), (0, 1, 5), (0, 8, 1), (0, 11, 0), (0, 2, 4), (0, 9, 1), (0, 12, 0), (0, 3, 4), (0, 2, 5), (0, 3, 5),),
    "Q0": ((0, 4, 4), (0, 5, 3), (0, 8, 2), (0, 9, 2), (0, 10, 1), (0, 13, 0),),
    "before P0": ((0, 4, 5),),
    "F0": ((0, 5, 4), (0, 6, 3), (0, 7, 3), (0, 10, 2), (0, 11, 1), (0, 14, 0),),
    "F1": ((0, 6, 4), (0, 8, 3), (0, 12, 1), (0, 15, 0),),
    "before Q1": ((0, 5, 5),),
    "P1": ((0, 7, 4), (0, 9, 3), (0, 13, 1), (0, 11, 2),),
    "F2": ((0, 8, 4), (0, 10, 3), (0, 12, 2), (0, 14, 1), (0, 15, 1),),
    "F3": ((0, 9, 4), (0, 11, 3), (0, 13, 2),),
    "before Q2": ((0, 6, 5),),
    "P2": ((0, 10, 4), (0, 12, 3), (0, 14, 2),),
    "F4": ((0, 11, 4), (0, 13, 3), (0, 15, 2),),
    "F5": ((0, 12, 4), (0, 14, 3), (0, 15, 3),),
    "before wo": ((0, 7, 5),),
    "ln1": ((0, 13, 4),),
    "before U0": ((0, 8, 5),),
    "before U1": ((0, 9, 5),),
    "U1": ((0, 14, 4),),
    "before U2": ((0, 10, 5),),
    "U2": ((0, 15, 4),),
    "before U3": ((0, 11, 5),),
    "before down": ((0, 12, 5), (0, 13, 5), (0, 14, 5), (0, 15, 5),),
    "b0": ((1, 0, 0),),
    "b1": ((1, 1, 0),),
    "b2": ((1, 0, 1), (1, 2, 0),),
    "b3": ((1, 1, 1), (1, 3, 0),),
    "d0": ((1, 2, 1),),
    "d2": ((1, 0, 2),),
    "d3": ((1, 3, 1), (1, 4, 0), (1, 5, 0), (1, 6, 0),),
    "wob": ((1, 1, 2),),
    "B0": ((1, 0, 3), (1, 2, 2), (1, 4, 1), (1, 5, 1), (1, 6, 1), (1, 7, 0), (1, 8, 0),),
    "B1": ((1, 0, 4), (1, 1, 3), (1, 3, 2), (1, 7, 1),),
    "gw0": ((1, 2, 3), (1, 4, 2), (1, 8, 1), (1, 9, 0),),
    "B2": ((1, 0, 5), (1, 3, 3), (1, 5, 2), (1, 9, 1),),
    "B3": ((1, 1, 4), (1, 4, 3), (1, 6, 2),),
    "gw1": ((1, 2, 4), (1, 5, 3), (1, 7, 2), (1, 10, 0),),
    "B4": ((1, 1, 5), (1, 3, 4), (1, 2, 5), (1, 6, 3), (1, 8, 2), (1, 10, 1),),
    "B5": ((1, 3, 5), (1, 4, 4), (1, 5, 4), (1, 6, 4), (1, 7, 3), (1, 9, 2),),
    "rel2": ((1, 11, 0), (1, 12, 0),),
    "gv2": ((1, 13, 0),),
    "gk2": ((1, 8, 3),),
    "gq2": ((1, 10, 2), (1, 4, 5), (1, 7, 4), (1, 11, 1), (1, 14, 0), (1, 12, 1), (1, 15, 0), (1, 13, 1),),
    "end": ((1, 5, 5), (1, 8, 4), (1, 6, 5), (1, 14, 1), (1, 15, 1), (1, 9, 3), (1, 11, 2), (1, 12, 2), (1, 13, 2), (1, 10, 3), (1, 14, 2), (1, 7, 5), (1, 15, 2), (1, 8, 5), (1, 9, 4), (1, 11, 3), (1, 10, 4), (1, 12, 3), (1, 13, 3), (1, 11, 4), (1, 14, 3), (1, 12, 4), (1, 15, 3), (1, 13, 4), (1, 9, 5), (1, 10, 5), (1, 14, 4), (1, 11, 5), (1, 12, 5), (1, 15, 4), (1, 13, 5), (1, 14, 5), (1, 15, 5),),
}
STEPS = ((("v", ""),), (("x", "v"), ("y", "v")), (("w", "vx"), ("w", "vy")), (("y", "vxw"), ("x", "vyw")))


class Part:
    def __init__(self, place, piece, lo, cols):
        cut = cols // 256 * 128
        self.p, self.piece, self.lo, self.cols = place, piece, lo, cols
        self.all = pl.ds(lo, cols)
        self.halves = (pl.ds(lo, cut), pl.ds(lo + cut, cols - cut))

    def spans(self, k):
        return (self.all,) if len(STEPS[k]) == 1 else self.halves

    def settle(self, ref, send, recv):
        copy = remote(ref, ref, send, recv, self.p.across("c"))
        copy.wait_recv()
        copy.wait_send()


class Gather(Part):
    def __init__(self, place, piece, lo, cols, send, recv):
        super().__init__(place, piece, lo, cols)
        self.send, self.recv = send, recv

    def step(self, k):
        n = len(STEPS)
        if k > 0:
            done = "vwyx" if k - 1 == n else STEPS[k - 1][0][1]
            self.settle(self.piece(self.p.index(done), self.all), self.send.at[0], self.recv.at[k - 1])
        if k < n:
            for (axis, done), span in zip(STEPS[k], self.spans(k)):
                ref = self.piece(self.p.index(done), span)
                remote(ref, ref, self.send.at[0], self.recv.at[k], self.p.across(axis)).start()
        elif k == n:
            ref = self.piece(self.p.index("vwyx"), self.all)
            remote(ref, ref, self.send.at[0], self.recv.at[k], self.p.across("c")).start()


def add_into(ref, other):
    ref[...] = (ref[...].astype(F32) + other[...].astype(F32)).astype(BF)


class Scatter(Part):
    def __init__(self, place, piece, lo, cols, order, last, slots, buffers, send, recv, credit, finish):
        super().__init__(place, piece, lo, cols)
        self.order, self.last, self.send, self.recv, self.credit, self.finish = order, last, send, recv, credit, finish
        self.slot = slots.at[order % SLOTS, :, :, :, :, :, pl.ds(0, cols)]
        self.buffers = buffers

    def step(self, k):
        p, g, n = self.p, self.piece, len(STEPS)
        if k == 1:
            self.settle(self.slot, self.send.at[0], self.recv.at[0])

            @pl.loop(0, 2)
            def _(v):
                at = p.index("vwyx")
                add_into(g((at[0], v, *at[2:]), self.all), self.slot.at[v])

            if self.order + SLOTS < self.last:
                pl.semaphore_signal(self.credit, inc=1, device_id=p.across("c"), device_id_type=MESH)
        elif k > 1:
            j = n + 1 - k
            self.settle(g(p.index(STEPS[j][0][1]), self.all), self.send.at[0], self.recv.at[k - 1])
            if k <= n:
                for (_, done), span, buffer in zip(STEPS[j], self.spans(j), self.buffers[j]):
                    add_into(g(p.index(done), span), buffer)
            else:
                self.finish(self.lo, g(p.index(), self.all)[...].astype(F32) + self.buffers[0][0][...].astype(F32))
        if k == 0:
            if self.order >= SLOTS:
                pl.semaphore_wait(self.credit, 1)
            ref = g(p.index("vwyx", "c"), self.all)
            remote(ref, self.slot, self.send.at[0], self.recv.at[0], p.across("c")).start()
        elif k <= n:
            j = n - k
            for (axis, done), span, buffer in zip(STEPS[j], self.spans(j), self.buffers[j]):
                ref = g(p.index(done, axis), span)
                remote(ref, buffer, self.send.at[0], self.recv.at[k], p.across(axis)).start()


def scatter_buffers(rows, cols):
    cut = cols // 256 * 128
    found = []
    for step in STEPS:
        widths = (cols,) if len(step) == 1 else (cut, cols - cut)
        found.append([pltpu.VMEM((*(2,) * len(done), rows, width), BF) for (_, done), width in zip(step, widths)])
    return found


def layer_kernel(
    comm,
    length_ref, index_ref, x_ref, cot_ref, vec_in, rel_in, q_in, k_in, v_in, o_in, up_in, down_in,
    out_ref, gtok_ref, r_out, q_out, k_out, v_out, o_out, up_out, down_out,
    GR, GA, GO, GU, GD,
    q_ref, k_ref, v_ref, kf_ref, vf_ref, kprT_ref, kpsT_ref, qpsT_ref, pick_ref, pT_ref,
    ctx_ref, dcT_ref, n1_ref, inv1_ref, nb_ref, gd_ref, act_ref, gp_ref,
    grel_ref, cols_ref, rows_ref, bup_ref, small_ref, gbup_ref, mask_ref, flip_ref, select_ref,
    *rest,
):
    T, D = x_ref.shape
    FF = act_ref.shape[1]
    NB = pick_ref.shape[0]
    B = T // 2
    C = 256
    R = 128
    CH = FF // D
    scale = (3.0 * HEAD) ** -0.5
    length = length_ref[0]
    row = lambda k: rows_ref[k:k + 1, :]
    whole = (slice(None),) * len(GRID)
    per = D // BLOCKS

    def part(ref, *lead, trail=()):
        return lambda blocks, cols: ref.at[(*lead, *blocks, *trail, slice(None), cols)]

    pieces = [part(GR)] + [part(GA, n) for n in range(D // C)] + [part(GO)]
    pieces += [part(GU, k) for k in range(CH)] + [part(GD, trail=(k,)) for k in range(CH)]
    if comm:
        slots, buffers, (ag_send, ag_recv, rs_send, rs_recv, credit) = rest[0], rest[1:-5], rest[-5:]
        place = Place()
        gathers = [Gather(place, pieces[i], lo, cols, ag_send.at[j], ag_recv.at[j]) for j, (i, lo, cols) in enumerate(GATHERS)]
        nA, nO, nU, nD = 1, 1 + D // C, 2 + D // C, 2 + D // C + CH

        def finisher(i):
            def store(lo, total):
                cols = pl.ds(lo, total.shape[1])
                if i == 0:
                    r_out[:, cols] = total
                elif i < nO:
                    for b in range(0, total.shape[1], 128):
                        ref = (q_out, k_out, v_out)[(lo + b) // C]
                        ref[:, pl.ds((i - nA) * C + (lo + b) % C, 128)] = total[:, b:b + 128]
                elif i == nO:
                    o_out[:, cols] = total
                elif i < nD:
                    up_out[:, pl.ds((i - nU) * D + lo, total.shape[1])] = total
                else:
                    down_out[pl.ds((i - nD) * per, per), cols] = total
            return store

        scatters = []
        for j, (i, lo, cols) in enumerate(SCATTERS):
            scatters.append(Scatter(place, pieces[i], lo, cols, j, len(SCATTERS), slots, buffers[j], rs_send.at[j], rs_recv.at[j], credit, finisher(i)))

    def run(name):
        if comm:
            for kind, j, k in TICKS.get(name, ()):
                (scatters if kind else gathers)[j].step(k)

    def due(name, index, values):
        if comm:
            for m in values:
                label = f"{name}{m}"
                if label in TICKS:
                    @pl.when(index == m)
                    def _():
                        run(label)

    if comm:
        me = place.index()
        rows_ref[...] = jnp.zeros_like(rows_ref)
        for k, ref in enumerate(vec_in[:-1]):
            rows_ref[k:k + 1, 0:per] = ref[...].astype(F32).reshape(1, per)
        last = vec_in[-1][...].astype(F32).reshape(1, CH * per)
        for k in range(CH):
            rows_ref[9 + k:10 + k, 0:per] = last[:, k * per:(k + 1) * per]
        own = jnp.concatenate([rows_ref[:, 0:128], jnp.zeros((112, 128), F32)], axis=0).T
        GR[(*me, slice(None), pl.ds(0, NB))] = rel_in[...]
        GR[(*me, slice(None), pl.ds(NB, 128))] = own[0:per].astype(BF)
        for n in range(D // C):
            cols = pl.ds(n * C, C)
            for i, ref in enumerate((q_in, k_in, v_in)):
                GA[(n, *me, slice(None), pl.ds(i * C, C))] = ref[:, cols]
        GO[me] = o_in[...]
        for k in range(CH):
            GU[(k, *me)] = up_in[:, pl.ds(k * D, D)]
            GD[(*me, k)] = down_in[k]
        place.barrier()
        run("pre")
    else:
        GRh, GAh, GOh, GUh, GDh = rest[:5]
        sems = rest[10]
        loads = [pltpu.make_async_copy(src, dst, sems.at[i]) for i, (src, dst) in enumerate(zip((GRh, GAh, GOh, GUh, GDh), (GR, GA, GO, GU, GD)))]
        for copy in loads:
            copy.start()
        for copy in loads:
            copy.wait()
    flip_ref[...] = jnp.where(iota((B, B), 0) + iota((B, B), 1) == B - 1, 1.0, 0.0).astype(BF)
    index = jnp.broadcast_to(index_ref[...].reshape(1, 2 * T), (8, 2 * T))
    high = lax.shift_right_logical(index, 4)
    parts = [v.astype(F32).astype(BF) for v in (high, index - 16 * high)]
    back = [jnp.concatenate([nn(v[:, b * B:(b + 1) * B], flip_ref[...]) for b in range(2 * T // B - 1, -1, -1)], axis=1) for v in parts]
    reverse = (back[0] * 16.0 + back[1]).astype(jnp.int32)
    shifted = jnp.where(iota((8, 2 * T), 1) == 2 * T - 1, -1, pltpu.roll(index, 2 * T - 1, 1))
    act_ref[:, 0:2 * T] = jnp.where(iota((NB, 2 * T), 0) == reverse[0:1], 1.0, 0.0).astype(BF)
    pick_ref[...] = jnp.where(iota((NB, 2 * T), 0) == shifted[0:1], 1.0, 0.0).astype(BF)
    W = 4 * per
    block = sum(jnp.where(iota((W, CH * W), 0) >= per * i, 1, 0) for i in range(1, 4))
    ublock = sum(jnp.where(iota((1, CH * W), 1) >= per * CH * i, 1, 0) for i in range(1, 4))
    uslice = sum(jnp.where(iota((1, CH * W), 1) >= per * i, 1, 0) for i in range(1, 4 * CH))
    place_in = iota((1, CH * W), 1) - per * uslice
    select_ref[...] = jnp.where((block == ublock) & (iota((W, CH * W), 0) - per * block == place_in), 1.0, 0.0).astype(BF)
    own_column = iota((128, CH * W), 0) == 9 + uslice - CH * ublock
    mask_ref[...] = jnp.where(iota((8, T), 1) < length, 0.0, -1e30)
    small_ref[...] = jnp.zeros_like(small_ref)
    grel_ref[...] = jnp.zeros_like(grel_ref)
    run("before Q0")
    cols_ref[...] = matrix(GR[(*whole, slice(None), pl.ds(NB, 128))].astype(F32))
    rows_ref[...] = cols_ref[...].T[0:16]

    @pl.loop(0, D // W)
    def _(t):
        spread = tn(cols_ref[tile(t, W), :].astype(BF), select_ref[...])
        bup_ref[0:1, tile(t, CH * W)] = column_sum(jnp.where(own_column, spread, 0.0))

    @pl.loop(0, D // C)
    def _(n):
        due("before Q", n, range(1, D // C))
        cols = tile(n, C)
        weight = lambda i: matrix(GA[(n, *whole, slice(None), pl.ds(i * C, C))])
        q_ref[:, cols] = (nn(x_ref[...], weight(0)) + rows_ref[0:1, cols]).astype(BF)
        k = (nn(x_ref[...], weight(1)) + rows_ref[1:2, cols]).astype(BF)
        v = (nn(x_ref[...], weight(2)) + rows_ref[2:3, cols]).astype(BF)
        k_ref[:, cols] = k
        v_ref[:, cols] = v
        for src, dst in ((k, kf_ref), (v, vf_ref)):
            dst[0:B, cols] = nn(flip_ref[...], src[B:T]).astype(BF)
            dst[B:T, cols] = nn(flip_ref[...], src[0:B]).astype(BF)
        due("Q", n, range(D // C))
        due("before P", n, (0,))
        relT = matrix(GR[(*whole, slice(None), pl.ds(0, NB))])
        rk = (tn(weight(1), relT) + cols_ref[cols, 1:2]).astype(BF)
        rq = (tn(weight(0), relT) + cols_ref[cols, 0:1]).astype(BF)
        kprT_ref[cols, :] = nn(rk, act_ref[:, 0:2 * T]).astype(BF)
        kpsT_ref[cols, :] = nn(rk, pick_ref[...]).astype(BF)
        qpsT_ref[cols, :] = nn(rq, pick_ref[...]).astype(BF)
        due("P", n, range(D // C))

        @pl.loop(0, 2)
        def _(i):
            pair_forward(2 * n + i, q_ref, k_ref, v_ref, kprT_ref, qpsT_ref, mask_ref, flip_ref, ctx_ref, pT_ref, scale)
            due("F", 2 * n + i, range(2 * D // C))

    run("before wo")
    second_ref = gtok_ref

    @pl.loop(0, D // C)
    def _(n):
        cols = tile(n, C)
        w = matrix(GO[(*whole, slice(None), cols)])
        second_ref[:, cols] = x_ref[:, cols].astype(F32) + (nn(ctx_ref[...], w) + rows_ref[3:4, cols])

    run("wo")

    @pl.loop(0, T // R)
    def _(r):
        rs = tile(r, R)
        n1, inv1 = norm_rows(second_ref[rs, :])
        n1_ref[rs, :] = n1
        inv1_ref[rs, :] = jnp.broadcast_to(inv1, (R, 128))
        nb_ref[rs, :] = (n1 * row(4) + row(5)).astype(BF)

    run("ln1")

    @pl.loop(0, CH)
    def _(k):
        due("before U", k, range(CH))

        @pl.loop(0, D // C)
        def _(j):
            w = matrix(GU[(k, *whole, slice(None), tile(j, C))])
            cols = tile(k * (D // C) + j, C)
            up = nn(nb_ref[...], w) + bup_ref[0:1, cols]
            phi, e = normal_cdf_pair(up)
            act_ref[:, cols] = (up * phi).astype(BF)
            gp_ref[:, cols] = (phi + up * e * 0.3989422804014327).astype(BF)

        due("U", k, range(CH))

    run("before down")

    @pl.loop(0, D // C)
    def _(n):
        cols = tile(n, C)
        w = matrix(GD[(*whole, slice(None), slice(None), cols)])
        normed = n1_ref[:, cols] * rows_ref[4:5, cols] + rows_ref[5:6, cols]
        second_ref[:, cols] = normed + (nn(act_ref[...], w) + rows_ref[6:7, cols])

    run("down")

    @pl.loop(0, T // R)
    def _(r):
        rs = tile(r, R)
        live = jnp.where(iota((R, 1), 0) + r * R < length, 1.0, 0.0)
        n2, inv2 = norm_rows(second_ref[rs, :])
        out_ref[rs, :] = ((n2 * row(7) + row(8)) * live).astype(BF)
        start = cot_ref[rs, :].astype(F32) * live
        g = norm_back(start * row(7), n2, inv2)
        second_ref[rs, :] = g
        gd = g.astype(BF)
        gd_ref[rs, :] = gd
        small_ref[6:7, :] += column_sum(gd.astype(F32))
        small_ref[7:8, :] += column_sum(start * n2)
        small_ref[8:9, :] += column_sum(start)

    run("ln2")

    @pl.loop(0, CH)
    def _(k):
        units = tile(k, D)
        w = matrix(GD[lax.div(k, 2), lax.rem(k, 2)])
        gu = (nt(gd_ref[...], w) * gp_ref[:, units].astype(F32)).astype(BF)
        gp_ref[:, units] = gu
        gbup_ref[0:1, units] = column_sum(gu.astype(F32))
        second_ref[...] += nt(gu, matrix(GU[k]))

        @pl.loop(0, 2)
        def _(i):
            g = tn(nb_ref[:, tile(i, D // 2)], gp_ref[:, units])
            GU[k, i] = g.reshape(*GU.shape[2:]).astype(BF)

        due("b", k, range(CH))

    @pl.loop(0, CH)
    def _(k):
        @pl.loop(0, 2)
        def _(i):
            at = pl.ds(pl.multiple_of(k * D + i * (D // 2), D // 2), D // 2)
            g = tn(act_ref[:, at], gd_ref[...])
            GD[lax.div(k, 2), lax.rem(k, 2), i] = g.reshape(*GD.shape[3:]).astype(BF)

        due("d", k, range(CH))

    @pl.loop(0, T // R)
    def _(r):
        rs = tile(r, R)
        g = second_ref[rs, :]
        n1 = n1_ref[rs, :]
        gm = norm_back(g * row(4), n1, inv1_ref[rs, 0:1])
        second_ref[rs, :] = gm
        ga = gm.astype(BF)
        gd_ref[rs, :] = ga
        small_ref[3:4, :] += column_sum(ga.astype(F32))
        small_ref[4:5, :] += column_sum(g * n1)
        small_ref[5:6, :] += column_sum(g)

    run("ln1b")

    @pl.loop(0, GRID[0])
    def _(i):
        at = tile(i, D // 2)
        dcT_ref[at, :] = nt(matrix(GO[i]), gd_ref[...]).astype(BF)
        g = tn(ctx_ref[:, at], gd_ref[...])
        GO[i] = g.reshape(*GO.shape[1:]).astype(BF)

    run("wob")

    kprT_ref[:, 0:NB] = matrix(GR[(*whole, slice(None), pl.ds(0, NB))])

    @pl.loop(0, D // C)
    def _(n):
        cols = tile(n, C)
        final = (D // C - 1,)

        @pl.loop(0, 2)
        def _(i):
            pair_backward(2 * n + i, q_ref, kf_ref, vf_ref, kpsT_ref, qpsT_ref, dcT_ref, pT_ref, scale)
            due("B", 2 * n + i, range(2 * D // C))

        dq = q_ref[:, cols]
        for src, dst in ((kf_ref, k_ref), (vf_ref, v_ref)):
            dst[0:B, cols] = nn(flip_ref[...], src[B:T, cols]).astype(BF)
            dst[B:T, cols] = nn(flip_ref[...], src[0:B, cols]).astype(BF)
        dk, dv = k_ref[:, cols], v_ref[:, cols]
        grk = nt(kpsT_ref[cols, :], pick_ref[...]).astype(BF)
        grq = nt(qpsT_ref[cols, :], pick_ref[...]).astype(BF)
        weight = lambda i: matrix(GA[(n, *whole, slice(None), pl.ds(i * C, C))])
        grel_ref[...] += nn(weight(1), grk) + nn(weight(0), grq)
        ones_t, ones_b = jnp.ones((8, T), BF), jnp.ones((8, NB), BF)
        small_ref[0:1, cols] = (nn(ones_t, dq) + nt(ones_b, grq))[0:1]
        small_ref[1:2, cols] = (nn(ones_t, dk) + nt(ones_b, grk))[0:1]
        small_ref[2:3, cols] = nn(ones_t, dv)[0:1]

        @pl.when(n == final[0])
        def _():
            small_ref[9:16, :] = jnp.zeros((7, D), F32)
            cols_ref[...] = jnp.concatenate([small_ref[...], jnp.zeros((112, D), F32)], axis=0).T

            @pl.loop(0, D // W)
            def _(t):
                g = jnp.where(own_column, gbup_ref[0:1, tile(t, CH * W)], 0.0).astype(BF)
                cols_ref[tile(t, W), :] += nt(select_ref[...], g)

            GR[(*whole, slice(None), pl.ds(0, NB))] = grel_ref[...].reshape(*GR.shape[:6], NB).astype(BF)
            GR[(*whole, slice(None), pl.ds(NB, 128))] = cols_ref[...].reshape(*GR.shape[:6], 128).astype(BF)

        due("rel", n, final)
        for i, name, d, gr in ((2, "gv", dv, None), (1, "gk", dk, grk), (0, "gq", dq, grq)):
            gtok_ref[...] += nt(d, weight(i))
            for half in range(GRID[0]):
                g = tn(x_ref[:, half * (D // 2):(half + 1) * (D // 2)], d)
                if gr is not None:
                    g = g + nt(kprT_ref[half * (D // 2):(half + 1) * (D // 2), 0:NB], gr)
                GA[(n, half, *whole[1:], slice(None), pl.ds(i * C, C))] = g.reshape(*GA.shape[2:7], C).astype(BF)
            due(name, n, final)
        due("gw", n, range(D // C))

    if comm:
        run("end")
    else:
        GRh, GAh, GOh, GUh, GDh = rest[5:10]
        stores = [pltpu.make_async_copy(src, dst, sems.at[i]) for i, (dst, src) in enumerate(zip((GRh, GAh, GOh, GUh, GDh), (GR, GA, GO, GU, GD)))]
        for copy in stores:
            copy.start()
        for copy in stores:
            copy.wait()


def finish_kernel(r_ref, *refs):
    n = (len(refs) - 11) // 2
    for i in range(n):
        refs[n + i][...] = refs[i][...]
    rel_out, vectors, wide = refs[2 * n], refs[2 * n + 1:2 * n + 10], refs[2 * n + 10]
    rows, NB = rel_out.shape
    rel_out[...] = r_ref[:, 0:NB]
    flat = jnp.concatenate([r_ref[:, NB:], jnp.zeros((128 - rows, 128), F32)], axis=0).T
    for k, ref in enumerate(vectors):
        ref[...] = flat[k:k + 1, 0:rows].reshape(rows)
    wide[...] = jnp.concatenate([flat[9 + k:10 + k, 0:rows] for k in range(wide.shape[0] // rows)], axis=1).reshape(wide.shape[0])


def layer_scratch(T, D, FF, NB, heads):
    V = pltpu.VMEM
    n, ch = D // 256, FF // D
    rows = D // BLOCKS
    td, r = V((T, D), BF), V((*GRID, rows, NB + 128), BF)
    return [
        r, V((n, *GRID, rows, D), BF), V((*GRID, rows, D), BF), V((ch, *GRID, rows, D), BF), V((*GRID, ch, rows, D), BF),
        td, td, td, td, td, V((D, 2 * T), BF), V((D, 2 * T), BF), V((D, 2 * T), BF), V((NB, 2 * T), BF), V((heads, T, T), BF),
        td, V((D, T), BF), V((T, D), F32), V((T, 128), F32), td, td, V((T, FF), BF), V((T, FF), BF),
        V((D, NB), F32), V((D, 128), F32), V((16, D), F32), V((8, FF), F32), V((16, D), F32), V((8, FF), F32), V((8, T), F32),
        V((T // 2, T // 2), BF), V((4 * rows, 4 * rows * ch), BF),
    ]


def call_layer(comm, length, index, x, cot, parts):
    T, D = x.shape
    S = jax.ShapeDtypeStruct
    VM, HBM, SM = (pl.BlockSpec(memory_space=space) for space in (pltpu.VMEM, pl.ANY, pltpu.SMEM))
    heads = D // HEAD
    if comm:
        vectors, rel, wq, wk, wv, wo, wup, wdown = parts
        operands = (*vectors, rel, wq, wk, wv, wo, wup, wdown)
        rows, FF = wup.shape
        NB = rel.shape[1]
        outs = [S((T, D), BF), S((T, D), F32), S((rows, NB + 128), F32)] + [S((rows, D), F32)] * 4 + [S(wup.shape, F32), S((FF // D * rows, D), F32)]
        out_specs = [VM] * len(outs)
        in_specs = [SM] + [VM] * (3 + len(operands))
        sems = [pltpu.SemaphoreType.DMA((len(parts), k)) for parts in (GATHERS, SCATTERS) for k in (1, 5)] + [pltpu.SemaphoreType.REGULAR]
        extra = [pltpu.VMEM((SLOTS, *GRID[1:], rows, D), BF)]
        extra += [scatter_buffers(rows, cols) for _, _, cols in SCATTERS] + sems

        def kernel(*refs):
            given = 4 + len(vectors)
            layer_kernel(True, *refs[:4], refs[4:given], *refs[given:])
    else:
        gr, ga, go, gu, gd = operands = parts
        FF, NB = gu.shape[0] * D, gr.shape[-1] - 128
        outs = [S((T, D), BF), S((T, D), F32)] + [S(p.shape, p.dtype) for p in parts]
        in_specs = [SM] + [VM] * 3 + [HBM] * 5
        out_specs = [VM] * 2 + [HBM] * 5
        extra = [pltpu.SemaphoreType.DMA((5,))]

        def kernel(*refs):
            ins, given, results, stored, scratch = refs[:4], refs[4:9], refs[9:11], refs[11:16], refs[16:]
            layer_kernel(False, *ins, *[None] * 8, *results, *[None] * 7, *scratch[:-1], *given, *stored, scratch[-1])

    return pl.pallas_call(
        kernel,
        out_shape=outs,
        in_specs=in_specs,
        out_specs=out_specs,
        scratch_shapes=layer_scratch(T, D, FF, NB, heads) + extra,
        compiler_params=pltpu.CompilerParams(
            vmem_limit_bytes=VMEM_LIMIT,
            **(dict(collective_id=0, has_side_effects=True) if comm else {}),
        ),
    )(length, index, x, cot, *operands)


VMEM_LIMIT = 63 * 2**20


def body(comm, tokens, lengths, rel_index, w_query, b_query, w_key, b_key, w_value, b_value, w_out, b_out, rel_table,
         gain_one, shift_one, w_up, b_up, w_down, b_down, gain_two, shift_two, cotangent):
    rows, D = w_query.shape
    NB = rel_table.shape[0]
    FF = w_up.shape[1]
    ch, n = FF // D, D // 256
    vectors = (b_query, b_key, b_value, b_out, gain_one, shift_one, b_down, gain_two, shift_two)
    if comm:
        results = call_layer(True, lengths, rel_index, tokens, cotangent,
                             ((*vectors, b_up), rel_table.T, w_query, w_key, w_value, w_out, w_up, w_down.reshape(ch, rows, D)))
        out, gtok, gr, gq, gk, gv, go, gup, gdown = results
        S = jax.ShapeDtypeStruct
        VM = pl.BlockSpec(memory_space=pltpu.VMEM)
        moved = (out, gtok, gq, gk, gv, go, gup, gdown)
        *moved, rel, bq, bk, bv, bo, g1, s1, bd, g2, s2, bu = pl.pallas_call(
            finish_kernel,
            out_shape=[S(a.shape, a.dtype) for a in moved] + [S((rows, NB), F32)] + [S((rows,), F32)] * 9 + [S(b_up.shape, F32)],
            in_specs=[VM] * 9,
            out_specs=[VM] * 19,
            compiler_params=pltpu.CompilerParams(vmem_limit_bytes=VMEM_LIMIT),
        )(gr, *moved)
        out, gtok, gq, gk, gv, go, gup, gdown = moved
        return (out, gtok, gq, bq, gk, bk, gv, bv, go, bo, rel.T, g1, s1, gup, bu, gdown, bd, g2, s2)
    gather = lambda w: lax.all_gather(w, AXES, axis=0, tiled=True)
    scatter = lambda g: lax.psum_scatter(g.astype(F32), AXES, scatter_dimension=0, tiled=True)
    r = D // BLOCKS
    pad = jnp.zeros((rows, 128 - 9), BF)
    attend = gather(jnp.concatenate([w_out, w_query, w_key, w_value, rel_table.T, jnp.stack(vectors, axis=1), pad], axis=1))
    wide = gather(b_up).reshape(BLOCKS, ch, r).transpose(0, 2, 1).reshape(D, ch)
    gr = jnp.concatenate([attend[:, 4 * D:4 * D + NB + 9], wide, pad[0] * jnp.ones((D, 1), BF)], axis=1)[:, :NB + 128].reshape(*GRID, r, NB + 128)
    go = attend[:, :D].reshape(*GRID, r, D)
    ga = attend[:, D:4 * D].reshape(*GRID, r, 3, n, 256).transpose(7, 0, 1, 2, 3, 4, 5, 6, 8).reshape(n, *GRID, r, D)
    gu = gather(w_up).reshape(*GRID, r, ch, D).transpose(6, 0, 1, 2, 3, 4, 5, 7)
    gd = gather(w_down).reshape(*GRID, ch, r, D)
    out, gtok, gr, ga, go, gu, gd = call_layer(False, lengths, rel_index, tokens, cotangent, (gr, ga, go, gu, gd))
    gr = gr.reshape(D, NB + 128)
    ga = ga.reshape(n, *GRID, r, 3, 256).transpose(1, 2, 3, 4, 5, 6, 7, 0, 8).reshape(D, 3 * D)
    wide = scatter(gr[:, NB + 9:NB + 9 + ch].reshape(BLOCKS, r, ch).transpose(0, 2, 1).reshape(FF))
    gup = scatter(gu.transpose(1, 2, 3, 4, 5, 6, 0, 7).reshape(D, FF))
    gdown = scatter(gd.reshape(FF, D))
    attend = scatter(jnp.concatenate([go.reshape(D, D), ga, gr], axis=1))
    go, gq, gk, gv = (attend[:, i * D:(i + 1) * D] for i in range(4))
    vec = lambda i: attend[:, 4 * D + NB + i]
    return (out, gtok, gq, vec(0), gk, vec(1), gv, vec(2), go, vec(3), attend[:, 4 * D:4 * D + NB].T, vec(4), vec(5),
            gup, wide, gdown, vec(6), vec(7), vec(8))


def solution(mesh):
    rows, vec = P(AXES, None), P(AXES)
    comm = mesh.shape["dp"] == GRID[0] and mesh.shape["fsdp"] == BLOCKS // GRID[0]

    def step(*args):
        return body(comm, *args)

    return jax.shard_map(
        step,
        mesh=mesh,
        in_specs=(rows, vec, P(), rows, vec, rows, vec, rows, vec, rows, vec, P(None, AXES), vec, vec, rows, vec, rows, vec, vec, vec, rows),
        out_specs=(rows, rows, rows, vec, rows, vec, rows, vec, rows, vec, P(None, AXES), vec, vec, rows, vec, rows, vec, vec, vec),
        check_vma=False,
    )
```

```python
import jax
import jax.numpy as jnp
from jax import lax
from jax.experimental import pallas as pl
from jax.experimental.pallas import tpu as pltpu
from jax.sharding import PartitionSpec as P

BF = jnp.bfloat16
F32 = jnp.float32
EPS = 1e-6
HEAD = 64
AXES = ("dp", "fsdp")
MESH = pl.DeviceIdType.MESH
LOG2E = 1.4426950408889634
GRID = (2, 2, 2, 2, 2)
BLOCKS = 32
SLOTS = 3


def dot(left, right, dims):
    return lax.dot_general(left, right, ((dims[:1], dims[1:]), ((), ())), preferred_element_type=F32)


def nn(left, right):
    return dot(left, right, (1, 0))


def nt(left, right):
    return dot(left, right, (1, 1))


def tn(left, right):
    return dot(left, right, (0, 0))


def iota(shape, axis):
    return lax.broadcasted_iota(jnp.int32, shape, axis)


def column_sum(x):
    return jnp.sum(x, axis=0, keepdims=True)


def row_mean(x):
    return jnp.sum(x, axis=1, keepdims=True) * (1.0 / x.shape[1])


def norm_rows(x):
    centred = x - row_mean(x)
    inv = lax.rsqrt(row_mean(centred * centred) + EPS)
    return centred * inv, inv


def norm_back(g, n, inv):
    return (g - row_mean(g) - n * row_mean(g * n)) * inv


def normal_cdf_pair(x):
    a = jnp.abs(x)
    e = jnp.exp2(x * x * (-0.5 * LOG2E))
    t = 1.0 / (1.0 + (0.3275911 * 0.7071067811865476) * a)
    poly = ((((1.061405429 * t - 1.453152027) * t + 1.421413741) * t - 0.284496736) * t + 0.254829592) * t
    tail = 0.5 * poly * e
    return jnp.where(x < 0, tail, 1.0 - tail), e


def tile(n, size):
    return pl.ds(pl.multiple_of(n * size, size), size)


def matrix(value):
    rows = 1
    for size in value.shape[:-1]:
        rows *= size
    return value.reshape(rows, value.shape[-1])


def pair_forward(pair, q_ref, k_ref, v_ref, kprT_ref, qpsT_ref, mask_ref, flip_ref, ctx_ref, pT_ref, scale):
    T = q_ref.shape[0]
    B = T // 2
    lanes = tile(pair, 128)
    outs = []
    for hh in range(2):
        keep = iota((1, 128), 1) // HEAD == hh
        qh = jnp.where(keep, q_ref[:, lanes], 0)
        kh = jnp.where(keep, k_ref[:, lanes], 0)
        content = nt(qh, k_ref[:, lanes])
        to, frm = [], []
        for b in range(2):
            u0 = B * (1 - b)
            t = nn(qh[b * B:(b + 1) * B], kprT_ref[lanes, u0:u0 + 3 * B])
            to.append(pltpu.roll(t, 2 * B + 1, 1, stride=1, stride_axis=0)[:, :T])
            f = nn(kh[b * B:(b + 1) * B], qpsT_ref[lanes, u0:u0 + 3 * B])
            frm.append(pltpu.roll(f, 2 * B + 1, 1, stride=1, stride_axis=0)[:, :T].T)
        s = content + jnp.concatenate(to, axis=0) + jnp.concatenate(frm, axis=1) + mask_ref[0:1, :]
        top = jnp.max(s, axis=1, keepdims=True)
        e = jnp.exp2((s - top) * (scale * LOG2E))
        p = (e * (1.0 / jnp.sum(e, axis=1, keepdims=True))).astype(BF)
        outs.append(nn(p, v_ref[:, lanes]))
        pT_ref[2 * pair + hh, 0:B, :] = nt(flip_ref[...], p[:, B:T]).astype(BF)
        pT_ref[2 * pair + hh, B:T, :] = nt(flip_ref[...], p[:, 0:B]).astype(BF)
    ctx_ref[:, lanes] = jnp.where(iota((1, 128), 1) < HEAD, outs[0], outs[1]).astype(BF)


def pair_backward(pair, q_ref, kf_ref, vf_ref, kpsT_ref, qpsT_ref, dcT_ref, pT_ref, scale):
    T = q_ref.shape[0]
    B = T // 2
    lanes = tile(pair, 128)
    low = iota((1, 128), 1) < HEAD
    q, kf, dcT = q_ref[:, lanes], kf_ref[:, lanes], dcT_ref[lanes, :]
    dqs, dks, dvs, gks, gqs = [], [], [], [], []
    for hh in range(2):
        vh = jnp.where(iota((1, 128), 1) // HEAD == hh, vf_ref[:, lanes], 0)
        pT = pT_ref[2 * pair + hh]
        dpT = nn(vh, dcT)
        wide = pT.astype(F32)
        prod = wide * dpT
        inner = column_sum(prod) / column_sum(wide)
        dsT = (prod - wide * inner).astype(BF)
        ds = dsT.T
        zero = jnp.zeros((B, B), BF)
        dk, dq, gq, gk = [], [], [], []
        for b in range(2):
            rows, span = slice(b * B, (b + 1) * B), slice(b * B, b * B + 3 * B)
            gf = pltpu.roll(jnp.concatenate([dsT[rows], zero], axis=1), 0, 1, stride=1, stride_axis=0)
            dk.append(nn(dsT[rows], q) + nt(gf, qpsT_ref[lanes, span]))
            gq.append(tn(kf[rows], gf)[hh * HEAD:(hh + 1) * HEAD])
            gt = pltpu.roll(jnp.concatenate([ds[rows], zero], axis=1), 0, 1, stride=1, stride_axis=0)
            dq.append(nn(ds[rows], kf) + nt(gt, kpsT_ref[lanes, span]))
            gk.append(tn(q[rows], gt)[hh * HEAD:(hh + 1) * HEAD])
        dks.append(jnp.concatenate(dk, axis=0))
        dqs.append(jnp.concatenate(dq, axis=0))
        dvs.append(nt(pT, dcT))
        gqs.append(gq)
        gks.append(gk)
    for ref, pieces in ((qpsT_ref, gqs), (kpsT_ref, gks)):
        for hh in range(2):
            g = pieces[hh]
            rows = pl.ds(pl.multiple_of(pair * 128 + HEAD * hh, HEAD), HEAD)
            ref[rows, 0:B] = (scale * g[0][:, 0:B]).astype(BF)
            ref[rows, B:3 * B] = (scale * (g[0][:, B:] + g[1][:, 0:2 * B])).astype(BF)
            ref[rows, 3 * B:] = (scale * g[1][:, 2 * B:]).astype(BF)
    q_ref[:, lanes] = (scale * jnp.where(low, dqs[0], dqs[1])).astype(BF)
    kf_ref[:, lanes] = (scale * jnp.where(low, dks[0], dks[1])).astype(BF)
    vf_ref[:, lanes] = jnp.where(low, dvs[0], dvs[1]).astype(BF)


class Place:
    def __init__(self):
        f = lax.axis_index("fsdp")
        self.here = dict(c=lax.axis_index("dp"), v=lax.div(f, 8), w=lax.rem(lax.div(f, 4), 2), y=lax.rem(lax.div(f, 2), 2), x=lax.rem(f, 2))

    def across(self, axis):
        to = {**self.here, axis: 1 - self.here[axis]}
        return (to["c"], ((to["v"] * 2 + to["w"]) * 2 + to["y"]) * 2 + to["x"])

    def index(self, whole="", other=""):
        return tuple(slice(None) if a in whole else 1 - i if a in other else i for a, i in self.here.items())

    def greet(self):
        sem = pltpu.get_barrier_semaphore()
        for axis in self.here:
            pl.semaphore_signal(sem, inc=1, device_id=self.across(axis), device_id_type=MESH)

    def meet(self):
        pl.semaphore_wait(pltpu.get_barrier_semaphore(), len(self.here))


def remote(src, dst, send, recv, to):
    return pltpu.make_async_remote_copy(src_ref=src, dst_ref=dst, send_sem=send, recv_sem=recv, device_id=to, device_id_type=MESH)


GATHERS = (
    (0, 384, 256),
    (1, 0, 256),
    (1, 256, 256),
    (1, 512, 256),
    (0, 0, 384),
    (2, 0, 768),
    (3, 0, 768),
    (4, 0, 768),
    (5, 0, 768),
    (6, 0, 768),
    (7, 0, 768),
    (8, 0, 768),
    (9, 0, 768),
    (10, 0, 768),
    (11, 0, 768),
    (12, 0, 768),
)
SCATTERS = (
    (5, 0, 768),
    (6, 0, 768),
    (7, 0, 768),
    (8, 0, 768),
    (9, 0, 768),
    (10, 0, 768),
    (11, 0, 768),
    (12, 0, 768),
    (4, 0, 768),
    (1, 0, 768),
    (2, 0, 768),
    (0, 0, 384),
    (0, 384, 256),
    (3, 512, 256),
    (3, 256, 256),
    (3, 0, 256),
)
TICKS = {
    "pre": ((0, 0, 0), (0, 1, 0), (0, 2, 0), (0, 3, 0), (0, 4, 0), (0, 5, 0),),
    "before Q0": ((0, 0, 1), (0, 1, 1), (0, 2, 1), (0, 6, 0), (0, 3, 1), (0, 4, 1), (0, 7, 0), (0, 0, 2), (0, 1, 2), (0, 2, 2), (0, 3, 2), (0, 4, 2), (0, 5, 1), (0, 8, 0), (0, 0, 3), (0, 6, 1), (0, 9, 0), (0, 5, 2), (0, 1, 3), (0, 7, 1), (0, 10, 0), (0, 2, 3), (0, 0, 4), (0, 6, 2), (0, 3, 3), (0, 0, 5), (0, 1, 4), (0, 4, 3), (0, 7, 2), (0, 1, 5), (0, 8, 1), (0, 11, 0), (0, 2, 4), (0, 9, 1), (0, 12, 0), (0, 3, 4), (0, 2, 5), (0, 3, 5),),
    "Q0": ((0, 4, 4), (0, 5, 3), (0, 8, 2), (0, 9, 2), (0, 10, 1), (0, 13, 0),),
    "before P0": ((0, 4, 5),),
    "F0": ((0, 5, 4), (0, 6, 3), (0, 7, 3), (0, 10, 2), (0, 11, 1), (0, 14, 0),),
    "F1": ((0, 6, 4), (0, 8, 3), (0, 12, 1), (0, 15, 0),),
    "before Q1": ((0, 5, 5),),
    "P1": ((0, 7, 4), (0, 9, 3), (0, 13, 1), (0, 11, 2),),
    "F2": ((0, 8, 4), (0, 10, 3), (0, 12, 2), (0, 14, 1), (0, 15, 1),),
    "F3": ((0, 9, 4), (0, 11, 3), (0, 13, 2),),
    "before Q2": ((0, 6, 5),),
    "P2": ((0, 10, 4), (0, 12, 3), (0, 14, 2),),
    "F4": ((0, 11, 4), (0, 13, 3), (0, 15, 2),),
    "F5": ((0, 12, 4), (0, 14, 3), (0, 15, 3),),
    "before wo": ((0, 7, 5),),
    "ln1": ((0, 13, 4),),
    "before U0": ((0, 8, 5),),
    "before U1": ((0, 9, 5),),
    "U1": ((0, 14, 4),),
    "before U2": ((0, 10, 5),),
    "U2": ((0, 15, 4),),
    "before U3": ((0, 11, 5),),
    "before down": ((0, 12, 5), (0, 13, 5), (0, 14, 5), (0, 15, 5),),
    "b0": ((1, 0, 0),),
    "b1": ((1, 1, 0),),
    "b2": ((1, 0, 1), (1, 2, 0),),
    "b3": ((1, 1, 1), (1, 3, 0),),
    "d0": ((1, 2, 1),),
    "d2": ((1, 0, 2),),
    "d3": ((1, 3, 1), (1, 4, 0), (1, 5, 0), (1, 6, 0),),
    "wob": ((1, 1, 2),),
    "B0": ((1, 0, 3), (1, 2, 2), (1, 4, 1), (1, 5, 1), (1, 6, 1), (1, 7, 0), (1, 8, 0),),
    "B1": ((1, 0, 4), (1, 1, 3), (1, 3, 2), (1, 7, 1),),
    "gw0": ((1, 2, 3), (1, 4, 2), (1, 8, 1), (1, 9, 0),),
    "B2": ((1, 0, 5), (1, 3, 3), (1, 5, 2), (1, 9, 1),),
    "B3": ((1, 1, 4), (1, 4, 3), (1, 6, 2),),
    "gw1": ((1, 2, 4), (1, 5, 3), (1, 7, 2), (1, 10, 0),),
    "B4": ((1, 1, 5), (1, 3, 4), (1, 2, 5), (1, 6, 3), (1, 8, 2), (1, 10, 1),),
    "B5": ((1, 3, 5), (1, 4, 4), (1, 5, 4), (1, 6, 4), (1, 7, 3), (1, 9, 2),),
    "rel2": ((1, 11, 0), (1, 12, 0),),
    "gv2": ((1, 13, 0),),
    "gk2": ((1, 8, 3),),
    "gq2": ((1, 10, 2), (1, 4, 5), (1, 7, 4), (1, 11, 1), (1, 14, 0), (1, 12, 1), (1, 15, 0), (1, 13, 1),),
    "end": ((1, 5, 5), (1, 8, 4), (1, 6, 5), (1, 14, 1), (1, 15, 1), (1, 9, 3), (1, 11, 2), (1, 12, 2), (1, 13, 2), (1, 10, 3), (1, 14, 2), (1, 7, 5), (1, 15, 2), (1, 8, 5), (1, 9, 4), (1, 11, 3), (1, 10, 4), (1, 12, 3), (1, 13, 3), (1, 11, 4), (1, 14, 3), (1, 12, 4), (1, 15, 3), (1, 13, 4), (1, 9, 5), (1, 10, 5), (1, 14, 4), (1, 11, 5), (1, 12, 5), (1, 15, 4), (1, 13, 5), (1, 14, 5), (1, 15, 5),),
}
STEPS = ((("v", ""),), (("x", "v"), ("y", "v")), (("w", "vx"), ("w", "vy")), (("y", "vxw"), ("x", "vyw")))


class Part:
    def __init__(self, place, piece, lo, cols):
        cut = cols // 256 * 128
        self.p, self.piece, self.lo, self.cols = place, piece, lo, cols
        self.all = pl.ds(lo, cols)
        self.halves = (pl.ds(lo, cut), pl.ds(lo + cut, cols - cut))

    def spans(self, k):
        return (self.all,) if len(STEPS[k]) == 1 else self.halves

    def settle(self, ref, send, recv):
        copy = remote(ref, ref, send, recv, self.p.across("c"))
        copy.wait_recv()
        copy.wait_send()


class Gather(Part):
    def __init__(self, place, piece, lo, cols, send, recv):
        super().__init__(place, piece, lo, cols)
        self.send, self.recv = send, recv

    def step(self, k):
        n = len(STEPS)
        if k > 0:
            done = "vwyx" if k - 1 == n else STEPS[k - 1][0][1]
            self.settle(self.piece(self.p.index(done), self.all), self.send.at[0], self.recv.at[k - 1])
        if k < n:
            for (axis, done), span in zip(STEPS[k], self.spans(k)):
                ref = self.piece(self.p.index(done), span)
                remote(ref, ref, self.send.at[0], self.recv.at[k], self.p.across(axis)).start()
        elif k == n:
            ref = self.piece(self.p.index("vwyx"), self.all)
            remote(ref, ref, self.send.at[0], self.recv.at[k], self.p.across("c")).start()


def add_into(ref, other):
    ref[...] = (ref[...].astype(F32) + other[...].astype(F32)).astype(BF)


class Scatter(Part):
    def __init__(self, place, piece, lo, cols, order, last, slots, buffers, send, recv, credit, finish):
        super().__init__(place, piece, lo, cols)
        self.order, self.last, self.send, self.recv, self.credit, self.finish = order, last, send, recv, credit, finish
        self.slot = slots.at[order % SLOTS, :, :, :, :, :, pl.ds(0, cols)]
        self.buffers = buffers

    def step(self, k):
        p, g, n = self.p, self.piece, len(STEPS)
        if k == 1:
            self.settle(self.slot, self.send.at[0], self.recv.at[0])

            @pl.loop(0, 2)
            def _(v):
                at = p.index("vwyx")
                add_into(g((at[0], v, *at[2:]), self.all), self.slot.at[v])

            if self.order + SLOTS < self.last:
                pl.semaphore_signal(self.credit, inc=1, device_id=p.across("c"), device_id_type=MESH)
        elif k > 1:
            j = n + 1 - k
            self.settle(g(p.index(STEPS[j][0][1]), self.all), self.send.at[0], self.recv.at[k - 1])
            if k <= n:
                for (_, done), span, buffer in zip(STEPS[j], self.spans(j), self.buffers[j]):
                    add_into(g(p.index(done), span), buffer)
            else:
                self.finish(self.lo, g(p.index(), self.all)[...].astype(F32) + self.buffers[0][0][...].astype(F32))
        if k == 0:
            if self.order >= SLOTS:
                pl.semaphore_wait(self.credit, 1)
            ref = g(p.index("vwyx", "c"), self.all)
            remote(ref, self.slot, self.send.at[0], self.recv.at[0], p.across("c")).start()
        elif k <= n:
            j = n - k
            for (axis, done), span, buffer in zip(STEPS[j], self.spans(j), self.buffers[j]):
                ref = g(p.index(done, axis), span)
                remote(ref, buffer, self.send.at[0], self.recv.at[k], p.across(axis)).start()


def scatter_buffers(rows, cols):
    cut = cols // 256 * 128
    found = []
    for step in STEPS:
        widths = (cols,) if len(step) == 1 else (cut, cols - cut)
        found.append([pltpu.VMEM((*(2,) * len(done), rows, width), BF) for (_, done), width in zip(step, widths)])
    return found


def layer_kernel(
    comm,
    length_ref, index_ref, x_ref, cot_ref, vec_in, rel_in, q_in, k_in, v_in, o_in, up_in, down_in,
    out_ref, gtok_ref, r_out, q_out, k_out, v_out, o_out, up_out, down_out,
    GR, GA, GO, GU, GD,
    q_ref, k_ref, v_ref, kf_ref, vf_ref, kprT_ref, kpsT_ref, qpsT_ref, pick_ref, pT_ref,
    ctx_ref, dcT_ref, n1_ref, inv1_ref, nb_ref, gd_ref, act_ref, gp_ref,
    grel_ref, cols_ref, rows_ref, bup_ref, small_ref, gbup_ref, mask_ref, flip_ref, select_ref,
    *rest,
):
    T, D = x_ref.shape
    FF = act_ref.shape[1]
    NB = pick_ref.shape[0]
    B = T // 2
    C = 256
    R = 128
    CH = FF // D
    scale = (3.0 * HEAD) ** -0.5
    length = length_ref[0]
    row = lambda k: rows_ref[k:k + 1, :]
    whole = (slice(None),) * len(GRID)
    per = D // BLOCKS

    def part(ref, *lead, trail=()):
        return lambda blocks, cols: ref.at[(*lead, *blocks, *trail, slice(None), cols)]

    pieces = [part(GR)] + [part(GA, n) for n in range(D // C)] + [part(GO)]
    pieces += [part(GU, k) for k in range(CH)] + [part(GD, trail=(k,)) for k in range(CH)]
    if comm:
        slots, buffers, (ag_send, ag_recv, rs_send, rs_recv, credit) = rest[0], rest[1:-5], rest[-5:]
        place = Place()
        gathers = [Gather(place, pieces[i], lo, cols, ag_send.at[j], ag_recv.at[j]) for j, (i, lo, cols) in enumerate(GATHERS)]
        nA, nO, nU, nD = 1, 1 + D // C, 2 + D // C, 2 + D // C + CH

        def finisher(i):
            def store(lo, total):
                cols = pl.ds(lo, total.shape[1])
                if i == 0:
                    r_out[:, cols] = total
                elif i < nO:
                    for b in range(0, total.shape[1], 128):
                        ref = (q_out, k_out, v_out)[(lo + b) // C]
                        ref[:, pl.ds((i - nA) * C + (lo + b) % C, 128)] = total[:, b:b + 128]
                elif i == nO:
                    o_out[:, cols] = total
                elif i < nD:
                    up_out[:, pl.ds((i - nU) * D + lo, total.shape[1])] = total
                else:
                    down_out[pl.ds((i - nD) * per, per), cols] = total
            return store

        scatters = []
        for j, (i, lo, cols) in enumerate(SCATTERS):
            scatters.append(Scatter(place, pieces[i], lo, cols, j, len(SCATTERS), slots, buffers[j], rs_send.at[j], rs_recv.at[j], credit, finisher(i)))

    def run(name):
        if comm:
            for kind, j, k in TICKS.get(name, ()):
                (scatters if kind else gathers)[j].step(k)

    def due(name, index, values):
        if comm:
            for m in values:
                label = f"{name}{m}"
                if label in TICKS:
                    @pl.when(index == m)
                    def _():
                        run(label)

    if comm:
        place.greet()
        me = place.index()
        rows_ref[...] = jnp.zeros_like(rows_ref)
        for k, ref in enumerate(vec_in[:-1]):
            rows_ref[k:k + 1, 0:per] = ref[...].astype(F32).reshape(1, per)
        last = vec_in[-1][...].astype(F32).reshape(1, CH * per)
        for k in range(CH):
            rows_ref[9 + k:10 + k, 0:per] = last[:, k * per:(k + 1) * per]
        own = jnp.concatenate([rows_ref[:, 0:128], jnp.zeros((112, 128), F32)], axis=0).T
        GR[(*me, slice(None), pl.ds(0, NB))] = rel_in[...]
        GR[(*me, slice(None), pl.ds(NB, 128))] = own[0:per].astype(BF)
        for n in range(D // C):
            cols = pl.ds(n * C, C)
            for i, ref in enumerate((q_in, k_in, v_in)):
                GA[(n, *me, slice(None), pl.ds(i * C, C))] = ref[:, cols]
        GO[me] = o_in[...]
        for k in range(CH):
            GU[(k, *me)] = up_in[:, pl.ds(k * D, D)]
            GD[(*me, k)] = down_in[k]
        place.meet()
        run("pre")
    else:
        GRh, GAh, GOh, GUh, GDh = rest[:5]
        sems = rest[10]
        loads = [pltpu.make_async_copy(src, dst, sems.at[i]) for i, (src, dst) in enumerate(zip((GRh, GAh, GOh, GUh, GDh), (GR, GA, GO, GU, GD)))]
        for copy in loads:
            copy.start()
        for copy in loads:
            copy.wait()
    flip_ref[...] = jnp.where(iota((B, B), 0) + iota((B, B), 1) == B - 1, 1.0, 0.0).astype(BF)
    index = jnp.broadcast_to(index_ref[...].reshape(1, 2 * T), (8, 2 * T))
    high = lax.shift_right_logical(index, 4)
    parts = [v.astype(F32).astype(BF) for v in (high, index - 16 * high)]
    back = [jnp.concatenate([nn(v[:, b * B:(b + 1) * B], flip_ref[...]) for b in range(2 * T // B - 1, -1, -1)], axis=1) for v in parts]
    reverse = (back[0] * 16.0 + back[1]).astype(jnp.int32)
    shifted = jnp.where(iota((8, 2 * T), 1) == 2 * T - 1, -1, pltpu.roll(index, 2 * T - 1, 1))
    act_ref[:, 0:2 * T] = jnp.where(iota((NB, 2 * T), 0) == reverse[0:1], 1.0, 0.0).astype(BF)
    pick_ref[...] = jnp.where(iota((NB, 2 * T), 0) == shifted[0:1], 1.0, 0.0).astype(BF)
    W = 4 * per
    block = sum(jnp.where(iota((W, CH * W), 0) >= per * i, 1, 0) for i in range(1, 4))
    ublock = sum(jnp.where(iota((1, CH * W), 1) >= per * CH * i, 1, 0) for i in range(1, 4))
    uslice = sum(jnp.where(iota((1, CH * W), 1) >= per * i, 1, 0) for i in range(1, 4 * CH))
    place_in = iota((1, CH * W), 1) - per * uslice
    select_ref[...] = jnp.where((block == ublock) & (iota((W, CH * W), 0) - per * block == place_in), 1.0, 0.0).astype(BF)
    own_column = iota((128, CH * W), 0) == 9 + uslice - CH * ublock
    mask_ref[...] = jnp.where(iota((8, T), 1) < length, 0.0, -1e30)
    small_ref[...] = jnp.zeros_like(small_ref)
    grel_ref[...] = jnp.zeros_like(grel_ref)
    run("before Q0")
    cols_ref[...] = matrix(GR[(*whole, slice(None), pl.ds(NB, 128))].astype(F32))
    rows_ref[...] = cols_ref[...].T[0:16]

    @pl.loop(0, D // W)
    def _(t):
        spread = tn(cols_ref[tile(t, W), :].astype(BF), select_ref[...])
        bup_ref[0:1, tile(t, CH * W)] = column_sum(jnp.where(own_column, spread, 0.0))

    @pl.loop(0, D // C)
    def _(n):
        due("before Q", n, range(1, D // C))
        cols = tile(n, C)
        weight = lambda i: matrix(GA[(n, *whole, slice(None), pl.ds(i * C, C))])
        q_ref[:, cols] = (nn(x_ref[...], weight(0)) + rows_ref[0:1, cols]).astype(BF)
        k = (nn(x_ref[...], weight(1)) + rows_ref[1:2, cols]).astype(BF)
        v = (nn(x_ref[...], weight(2)) + rows_ref[2:3, cols]).astype(BF)
        k_ref[:, cols] = k
        v_ref[:, cols] = v
        for src, dst in ((k, kf_ref), (v, vf_ref)):
            dst[0:B, cols] = nn(flip_ref[...], src[B:T]).astype(BF)
            dst[B:T, cols] = nn(flip_ref[...], src[0:B]).astype(BF)
        due("Q", n, range(D // C))
        due("before P", n, (0,))
        relT = matrix(GR[(*whole, slice(None), pl.ds(0, NB))])
        rk = (tn(weight(1), relT) + cols_ref[cols, 1:2]).astype(BF)
        rq = (tn(weight(0), relT) + cols_ref[cols, 0:1]).astype(BF)
        kprT_ref[cols, :] = nn(rk, act_ref[:, 0:2 * T]).astype(BF)
        kpsT_ref[cols, :] = nn(rk, pick_ref[...]).astype(BF)
        qpsT_ref[cols, :] = nn(rq, pick_ref[...]).astype(BF)
        due("P", n, range(D // C))

        @pl.loop(0, 2)
        def _(i):
            pair_forward(2 * n + i, q_ref, k_ref, v_ref, kprT_ref, qpsT_ref, mask_ref, flip_ref, ctx_ref, pT_ref, scale)
            due("F", 2 * n + i, range(2 * D // C))

    run("before wo")
    second_ref = gtok_ref

    @pl.loop(0, D // C)
    def _(n):
        cols = tile(n, C)
        w = matrix(GO[(*whole, slice(None), cols)])
        second_ref[:, cols] = x_ref[:, cols].astype(F32) + (nn(ctx_ref[...], w) + rows_ref[3:4, cols])

    run("wo")

    @pl.loop(0, T // R)
    def _(r):
        rs = tile(r, R)
        n1, inv1 = norm_rows(second_ref[rs, :])
        n1_ref[rs, :] = n1
        inv1_ref[rs, :] = jnp.broadcast_to(inv1, (R, 128))
        nb_ref[rs, :] = (n1 * row(4) + row(5)).astype(BF)

    run("ln1")

    @pl.loop(0, CH)
    def _(k):
        due("before U", k, range(CH))

        @pl.loop(0, D // C)
        def _(j):
            w = matrix(GU[(k, *whole, slice(None), tile(j, C))])
            cols = tile(k * (D // C) + j, C)
            up = nn(nb_ref[...], w) + bup_ref[0:1, cols]
            phi, e = normal_cdf_pair(up)
            act_ref[:, cols] = (up * phi).astype(BF)
            gp_ref[:, cols] = (phi + up * e * 0.3989422804014327).astype(BF)

        due("U", k, range(CH))

    run("before down")

    @pl.loop(0, D // C)
    def _(n):
        cols = tile(n, C)
        w = matrix(GD[(*whole, slice(None), slice(None), cols)])
        normed = n1_ref[:, cols] * rows_ref[4:5, cols] + rows_ref[5:6, cols]
        second_ref[:, cols] = normed + (nn(act_ref[...], w) + rows_ref[6:7, cols])

    run("down")

    @pl.loop(0, T // R)
    def _(r):
        rs = tile(r, R)
        live = jnp.where(iota((R, 1), 0) + r * R < length, 1.0, 0.0)
        n2, inv2 = norm_rows(second_ref[rs, :])
        out_ref[rs, :] = ((n2 * row(7) + row(8)) * live).astype(BF)
        start = cot_ref[rs, :].astype(F32) * live
        g = norm_back(start * row(7), n2, inv2)
        second_ref[rs, :] = g
        gd = g.astype(BF)
        gd_ref[rs, :] = gd
        small_ref[6:7, :] += column_sum(gd.astype(F32))
        small_ref[7:8, :] += column_sum(start * n2)
        small_ref[8:9, :] += column_sum(start)

    run("ln2")

    @pl.loop(0, CH)
    def _(k):
        units = tile(k, D)
        w = matrix(GD[lax.div(k, 2), lax.rem(k, 2)])
        gu = (nt(gd_ref[...], w) * gp_ref[:, units].astype(F32)).astype(BF)
        gp_ref[:, units] = gu
        gbup_ref[0:1, units] = column_sum(gu.astype(F32))
        second_ref[...] += nt(gu, matrix(GU[k]))

        @pl.loop(0, 2)
        def _(i):
            g = tn(nb_ref[:, tile(i, D // 2)], gp_ref[:, units])
            GU[k, i] = g.reshape(*GU.shape[2:]).astype(BF)

        due("b", k, range(CH))

    @pl.loop(0, CH)
    def _(k):
        @pl.loop(0, 2)
        def _(i):
            at = pl.ds(pl.multiple_of(k * D + i * (D // 2), D // 2), D // 2)
            g = tn(act_ref[:, at], gd_ref[...])
            GD[lax.div(k, 2), lax.rem(k, 2), i] = g.reshape(*GD.shape[3:]).astype(BF)

        due("d", k, range(CH))

    @pl.loop(0, T // R)
    def _(r):
        rs = tile(r, R)
        g = second_ref[rs, :]
        n1 = n1_ref[rs, :]
        gm = norm_back(g * row(4), n1, inv1_ref[rs, 0:1])
        second_ref[rs, :] = gm
        ga = gm.astype(BF)
        gd_ref[rs, :] = ga
        small_ref[3:4, :] += column_sum(ga.astype(F32))
        small_ref[4:5, :] += column_sum(g * n1)
        small_ref[5:6, :] += column_sum(g)

    run("ln1b")

    @pl.loop(0, GRID[0])
    def _(i):
        at = tile(i, D // 2)
        dcT_ref[at, :] = nt(matrix(GO[i]), gd_ref[...]).astype(BF)
        g = tn(ctx_ref[:, at], gd_ref[...])
        GO[i] = g.reshape(*GO.shape[1:]).astype(BF)

    run("wob")

    kprT_ref[:, 0:NB] = matrix(GR[(*whole, slice(None), pl.ds(0, NB))])

    @pl.loop(0, D // C)
    def _(n):
        cols = tile(n, C)
        final = (D // C - 1,)

        @pl.loop(0, 2)
        def _(i):
            pair_backward(2 * n + i, q_ref, kf_ref, vf_ref, kpsT_ref, qpsT_ref, dcT_ref, pT_ref, scale)
            due("B", 2 * n + i, range(2 * D // C))

        dq = q_ref[:, cols]
        for src, dst in ((kf_ref, k_ref), (vf_ref, v_ref)):
            dst[0:B, cols] = nn(flip_ref[...], src[B:T, cols]).astype(BF)
            dst[B:T, cols] = nn(flip_ref[...], src[0:B, cols]).astype(BF)
        dk, dv = k_ref[:, cols], v_ref[:, cols]
        grk = nt(kpsT_ref[cols, :], pick_ref[...]).astype(BF)
        grq = nt(qpsT_ref[cols, :], pick_ref[...]).astype(BF)
        weight = lambda i: matrix(GA[(n, *whole, slice(None), pl.ds(i * C, C))])
        grel_ref[...] += nn(weight(1), grk) + nn(weight(0), grq)
        ones_t, ones_b = jnp.ones((8, T), BF), jnp.ones((8, NB), BF)
        small_ref[0:1, cols] = (nn(ones_t, dq) + nt(ones_b, grq))[0:1]
        small_ref[1:2, cols] = (nn(ones_t, dk) + nt(ones_b, grk))[0:1]
        small_ref[2:3, cols] = nn(ones_t, dv)[0:1]

        @pl.when(n == final[0])
        def _():
            small_ref[9:16, :] = jnp.zeros((7, D), F32)
            cols_ref[...] = jnp.concatenate([small_ref[...], jnp.zeros((112, D), F32)], axis=0).T

            @pl.loop(0, D // W)
            def _(t):
                g = jnp.where(own_column, gbup_ref[0:1, tile(t, CH * W)], 0.0).astype(BF)
                cols_ref[tile(t, W), :] += nt(select_ref[...], g)

            GR[(*whole, slice(None), pl.ds(0, NB))] = grel_ref[...].reshape(*GR.shape[:6], NB).astype(BF)
            GR[(*whole, slice(None), pl.ds(NB, 128))] = cols_ref[...].reshape(*GR.shape[:6], 128).astype(BF)

        due("rel", n, final)
        for i, name, d, gr in ((2, "gv", dv, None), (1, "gk", dk, grk), (0, "gq", dq, grq)):
            gtok_ref[...] += nt(d, weight(i))
            for half in range(GRID[0]):
                g = tn(x_ref[:, half * (D // 2):(half + 1) * (D // 2)], d)
                if gr is not None:
                    g = g + nt(kprT_ref[half * (D // 2):(half + 1) * (D // 2), 0:NB], gr)
                GA[(n, half, *whole[1:], slice(None), pl.ds(i * C, C))] = g.reshape(*GA.shape[2:7], C).astype(BF)
            due(name, n, final)
        due("gw", n, range(D // C))

    if comm:
        run("end")
    else:
        GRh, GAh, GOh, GUh, GDh = rest[5:10]
        stores = [pltpu.make_async_copy(src, dst, sems.at[i]) for i, (dst, src) in enumerate(zip((GRh, GAh, GOh, GUh, GDh), (GR, GA, GO, GU, GD)))]
        for copy in stores:
            copy.start()
        for copy in stores:
            copy.wait()


def finish_kernel(r_ref, *refs):
    n = (len(refs) - 11) // 2
    for i in range(n):
        refs[n + i][...] = refs[i][...]
    rel_out, vectors, wide = refs[2 * n], refs[2 * n + 1:2 * n + 10], refs[2 * n + 10]
    rows, NB = rel_out.shape
    rel_out[...] = r_ref[:, 0:NB]
    flat = jnp.concatenate([r_ref[:, NB:], jnp.zeros((128 - rows, 128), F32)], axis=0).T
    for k, ref in enumerate(vectors):
        ref[...] = flat[k:k + 1, 0:rows].reshape(rows)
    wide[...] = jnp.concatenate([flat[9 + k:10 + k, 0:rows] for k in range(wide.shape[0] // rows)], axis=1).reshape(wide.shape[0])


def layer_scratch(T, D, FF, NB, heads):
    V = pltpu.VMEM
    n, ch = D // 256, FF // D
    rows = D // BLOCKS
    td, r = V((T, D), BF), V((*GRID, rows, NB + 128), BF)
    return [
        r, V((n, *GRID, rows, D), BF), V((*GRID, rows, D), BF), V((ch, *GRID, rows, D), BF), V((*GRID, ch, rows, D), BF),
        td, td, td, td, td, V((D, 2 * T), BF), V((D, 2 * T), BF), V((D, 2 * T), BF), V((NB, 2 * T), BF), V((heads, T, T), BF),
        td, V((D, T), BF), V((T, D), F32), V((T, 128), F32), td, td, V((T, FF), BF), V((T, FF), BF),
        V((D, NB), F32), V((D, 128), F32), V((16, D), F32), V((8, FF), F32), V((16, D), F32), V((8, FF), F32), V((8, T), F32),
        V((T // 2, T // 2), BF), V((4 * rows, 4 * rows * ch), BF),
    ]


def call_layer(comm, length, index, x, cot, parts):
    T, D = x.shape
    S = jax.ShapeDtypeStruct
    VM, HBM, SM = (pl.BlockSpec(memory_space=space) for space in (pltpu.VMEM, pl.ANY, pltpu.SMEM))
    heads = D // HEAD
    if comm:
        vectors, rel, wq, wk, wv, wo, wup, wdown = parts
        operands = (*vectors, rel, wq, wk, wv, wo, wup, wdown)
        rows, FF = wup.shape
        NB = rel.shape[1]
        outs = [S((T, D), BF), S((T, D), F32), S((rows, NB + 128), F32)] + [S((rows, D), F32)] * 4 + [S(wup.shape, F32), S((FF // D * rows, D), F32)]
        out_specs = [VM] * len(outs)
        in_specs = [SM] + [VM] * (3 + len(operands))
        sems = [pltpu.SemaphoreType.DMA((len(parts), k)) for parts in (GATHERS, SCATTERS) for k in (1, 5)] + [pltpu.SemaphoreType.REGULAR]
        extra = [pltpu.VMEM((SLOTS, *GRID[1:], rows, D), BF)]
        extra += [scatter_buffers(rows, cols) for _, _, cols in SCATTERS] + sems

        def kernel(*refs):
            given = 4 + len(vectors)
            layer_kernel(True, *refs[:4], refs[4:given], *refs[given:])
    else:
        gr, ga, go, gu, gd = operands = parts
        FF, NB = gu.shape[0] * D, gr.shape[-1] - 128
        outs = [S((T, D), BF), S((T, D), F32)] + [S(p.shape, p.dtype) for p in parts]
        in_specs = [SM] + [VM] * 3 + [HBM] * 5
        out_specs = [VM] * 2 + [HBM] * 5
        extra = [pltpu.SemaphoreType.DMA((5,))]

        def kernel(*refs):
            ins, given, results, stored, scratch = refs[:4], refs[4:9], refs[9:11], refs[11:16], refs[16:]
            layer_kernel(False, *ins, *[None] * 8, *results, *[None] * 7, *scratch[:-1], *given, *stored, scratch[-1])

    return pl.pallas_call(
        kernel,
        out_shape=outs,
        in_specs=in_specs,
        out_specs=out_specs,
        scratch_shapes=layer_scratch(T, D, FF, NB, heads) + extra,
        compiler_params=pltpu.CompilerParams(
            vmem_limit_bytes=VMEM_LIMIT,
            **(dict(collective_id=0, has_side_effects=True) if comm else {}),
        ),
    )(length, index, x, cot, *operands)


VMEM_LIMIT = 63 * 2**20


def body(comm, tokens, lengths, rel_index, w_query, b_query, w_key, b_key, w_value, b_value, w_out, b_out, rel_table,
         gain_one, shift_one, w_up, b_up, w_down, b_down, gain_two, shift_two, cotangent):
    rows, D = w_query.shape
    NB = rel_table.shape[0]
    FF = w_up.shape[1]
    ch, n = FF // D, D // 256
    vectors = (b_query, b_key, b_value, b_out, gain_one, shift_one, b_down, gain_two, shift_two)
    if comm:
        results = call_layer(True, lengths, rel_index, tokens, cotangent,
                             ((*vectors, b_up), rel_table.T, w_query, w_key, w_value, w_out, w_up, w_down.reshape(ch, rows, D)))
        out, gtok, gr, gq, gk, gv, go, gup, gdown = results
        S = jax.ShapeDtypeStruct
        VM = pl.BlockSpec(memory_space=pltpu.VMEM)
        moved = (out, gtok, gq, gk, gv, go, gup, gdown)
        *moved, rel, bq, bk, bv, bo, g1, s1, bd, g2, s2, bu = pl.pallas_call(
            finish_kernel,
            out_shape=[S(a.shape, a.dtype) for a in moved] + [S((rows, NB), F32)] + [S((rows,), F32)] * 9 + [S(b_up.shape, F32)],
            in_specs=[VM] * 9,
            out_specs=[VM] * 19,
            compiler_params=pltpu.CompilerParams(vmem_limit_bytes=VMEM_LIMIT),
        )(gr, *moved)
        out, gtok, gq, gk, gv, go, gup, gdown = moved
        return (out, gtok, gq, bq, gk, bk, gv, bv, go, bo, rel.T, g1, s1, gup, bu, gdown, bd, g2, s2)
    gather = lambda w: lax.all_gather(w, AXES, axis=0, tiled=True)
    scatter = lambda g: lax.psum_scatter(g.astype(F32), AXES, scatter_dimension=0, tiled=True)
    r = D // BLOCKS
    pad = jnp.zeros((rows, 128 - 9), BF)
    attend = gather(jnp.concatenate([w_out, w_query, w_key, w_value, rel_table.T, jnp.stack(vectors, axis=1), pad], axis=1))
    wide = gather(b_up).reshape(BLOCKS, ch, r).transpose(0, 2, 1).reshape(D, ch)
    gr = jnp.concatenate([attend[:, 4 * D:4 * D + NB + 9], wide, pad[0] * jnp.ones((D, 1), BF)], axis=1)[:, :NB + 128].reshape(*GRID, r, NB + 128)
    go = attend[:, :D].reshape(*GRID, r, D)
    ga = attend[:, D:4 * D].reshape(*GRID, r, 3, n, 256).transpose(7, 0, 1, 2, 3, 4, 5, 6, 8).reshape(n, *GRID, r, D)
    gu = gather(w_up).reshape(*GRID, r, ch, D).transpose(6, 0, 1, 2, 3, 4, 5, 7)
    gd = gather(w_down).reshape(*GRID, ch, r, D)
    out, gtok, gr, ga, go, gu, gd = call_layer(False, lengths, rel_index, tokens, cotangent, (gr, ga, go, gu, gd))
    gr = gr.reshape(D, NB + 128)
    ga = ga.reshape(n, *GRID, r, 3, 256).transpose(1, 2, 3, 4, 5, 6, 7, 0, 8).reshape(D, 3 * D)
    wide = scatter(gr[:, NB + 9:NB + 9 + ch].reshape(BLOCKS, r, ch).transpose(0, 2, 1).reshape(FF))
    gup = scatter(gu.transpose(1, 2, 3, 4, 5, 6, 0, 7).reshape(D, FF))
    gdown = scatter(gd.reshape(FF, D))
    attend = scatter(jnp.concatenate([go.reshape(D, D), ga, gr], axis=1))
    go, gq, gk, gv = (attend[:, i * D:(i + 1) * D] for i in range(4))
    vec = lambda i: attend[:, 4 * D + NB + i]
    return (out, gtok, gq, vec(0), gk, vec(1), gv, vec(2), go, vec(3), attend[:, 4 * D:4 * D + NB].T, vec(4), vec(5),
            gup, wide, gdown, vec(6), vec(7), vec(8))


def solution(mesh):
    rows, vec = P(AXES, None), P(AXES)
    comm = mesh.shape["dp"] == GRID[0] and mesh.shape["fsdp"] == BLOCKS // GRID[0]

    def step(*args):
        return body(comm, *args)

    return jax.shard_map(
        step,
        mesh=mesh,
        in_specs=(rows, vec, P(), rows, vec, rows, vec, rows, vec, rows, vec, P(None, AXES), vec, vec, rows, vec, rows, vec, vec, vec, rows),
        out_specs=(rows, rows, rows, vec, rows, vec, rows, vec, rows, vec, P(None, AXES), vec, vec, rows, vec, rows, vec, vec, vec),
        check_vma=False,
    )
```
